32 devices in a mesh: context: 8 (over y, x, core), tensor: 4 (over z).
Axes of the slice: x: 2, y: 2, z: 4, core: 2. Of those that a mesh axis runs over, the one named last changes fastest.
Arguments:
- inputs: float32 [32, 32768], P('tensor', 'context'), may hold values from -0.078125 to 0.078125
- grads: float32 [32, 32768], P('tensor', 'context'), may hold values from -6 to 6
- response: float32 [32, 32768], P('tensor', 'context'), may hold values from -0.078125 to 0.078125
Outputs:
- input_grad: float32 [32, 32768], P('tensor', 'context')
- filter_grad: float32 [32, 32768], P('tensor', 'context')
The draws below stay inside these ranges and needn't reach their ends.
All inputs are finite; a program needn't handle non-finite values.
Results may differ from the reference program's by a relative error of at most 0.00014.
Values sent between devices are 32-bit elements; how exact they have to be, the bound alone decides.
No kernel may reach another device: no remote copies, remote signals or barrier semaphores. Data moves between devices by JAX's collectives and lax.ppermute only.
A program may use at most 64 MiB of HBM per device.

```python
import jax
import jax.numpy as jnp
from jax import lax

CH_DEV = 8
CH = 32
LEN = 32768
N_TENSOR = 4


def level_of(rng, dims, shards, least, largest):
    level = 1.0
    for dim, shards_of in shards:
        draws = jax.random.uniform(jax.random.fold_in(jax.random.fold_in(rng, 6), dim), (shards_of,), jnp.float32, least / len(shards), largest / len(shards))
        level = level * jnp.repeat(jnp.exp(draws), dims[dim] // shards_of).reshape((-1,) + (1,) * (len(dims) - 1 - dim))
    return level


def scatter_about(key, dims, scale, reach, cuts=(), kind=jnp.bfloat16):
    drawn = scale * jax.random.normal(key, dims, jnp.float32)
    if cuts:
        drawn = drawn * level_of(key, dims, cuts, -0.22, 0.18)
    return jnp.clip(drawn, -reach, reach).astype(kind)


def setup_inputs(seed: int = 0) -> dict:
    splits = jax.random.split(jax.random.key(seed), 4)
    inputs = scatter_about(splits[0], (CH, LEN), (LEN ** -0.5), 0.078125, ((0, 4), (1, 8)), jnp.float32)
    grads = scatter_about(splits[1], (CH, LEN), 1.0, 6.0, ((0, 4), (1, 8)), jnp.float32)
    response = scatter_about(splits[2], (CH, LEN), (LEN ** -0.5), 0.078125, ((0, 4), (1, 8)), jnp.float32)
    return {"inputs": inputs, "grads": grads, "response": response}


def channel_group(packed):
    signal_in, signal_grad, signal_filter = packed
    padded_len = 2 * LEN
    input_spec = jnp.fft.fft(signal_in, n=padded_len)
    grad_spec = jnp.fft.fft(signal_grad, n=padded_len)
    filter_spec = jnp.fft.fft(signal_filter, n=padded_len)
    input_grad = jnp.real(jnp.fft.ifft(jnp.conj(filter_spec) * grad_spec))[:, :LEN]
    filter_grad = jnp.real(jnp.fft.ifft(jnp.conj(input_spec) * grad_spec))[:, :LEN]
    return input_grad, filter_grad


def reference(inputs, grads, response):
    shaped_in = inputs.reshape(N_TENSOR, CH_DEV, LEN)
    shaped_grad = grads.reshape(N_TENSOR, CH_DEV, LEN)
    shaped_filter = response.reshape(N_TENSOR, CH_DEV, LEN)
    input_grad, filter_grad = lax.map(channel_group, (shaped_in, shaped_grad, shaped_filter))
    return input_grad.reshape(CH_DEV * N_TENSOR, LEN), filter_grad.reshape(CH_DEV * N_TENSOR, LEN)
```

```python
import functools
import math

import jax
import jax.numpy as jnp
import numpy as np
from jax import lax
from jax.experimental import pallas as pl
from jax.experimental.pallas import tpu as pltpu
from jax.sharding import PartitionSpec as P

LANES = 128
MODE = "a2a"
BF = jnp.bfloat16


def halves(table):
    high = table.astype(BF)
    low = (table - high.astype(np.float32)).astype(BF)
    return high, low


def tables(length):
    rows = length // LANES
    k = np.arange(rows)[:, None] + 0.25
    r = np.arange(rows)[None, :]
    ang = 2 * np.pi * (k * r / rows)
    cos1, sin1 = np.cos(ang), np.sin(ang)
    fwd = np.concatenate([cos1, -sin1], axis=0).astype(np.float32)
    inv = (np.concatenate([cos1.T, -sin1.T], axis=1) / length).astype(np.float32)
    lane = np.arange(LANES)
    tw = 2 * np.pi * (k * lane[None, :] / length)
    twc, tws = np.cos(tw).astype(np.float32), np.sin(tw).astype(np.float32)
    a2 = 2 * np.pi * (lane[:, None] * lane[None, :] % LANES) / LANES
    c2, s2 = np.cos(a2), np.sin(a2)
    w_f = np.block([[c2, -s2], [s2, c2]]).astype(np.float32)
    w_i = np.block([[c2, s2], [-s2, c2]]).astype(np.float32)
    fh, fl = halves(fwd)
    ih, il = halves(inv)
    wfh, wfl = halves(w_f)
    wih, wil = halves(w_i)
    return fh, fl, ih, il, wfh, wfl, wih, wil, twc, tws


def split(x):
    high = x.astype(BF)
    low = (x - high.astype(jnp.float32)).astype(BF)
    return high, low


def dot(a, b):
    return jnp.dot(a, b, preferred_element_type=jnp.float32)


def dot_left(th, tl, x):
    xh, xl = split(x)
    return dot(th, xh) + (dot(th, xl) + dot(tl, xh))


def dot_right(x, th, tl):
    xh, xl = split(x)
    return dot(xh, th) + (dot(xl, th) + dot(xh, tl))


def spread(a, b, c, out):
    channels, block = a.shape
    chunks = block // LANES
    for i, ref in enumerate((a, b, c)):
        for j in range(chunks):
            out[pl.ds(i * chunks + j, channels, stride=3 * chunks), :] = ref[:, pl.ds(j * LANES, LANES)]


def gather(x, a, b):
    channels, block = a.shape
    chunks = block // LANES
    for i, ref in enumerate((a, b)):
        for j in range(chunks):
            ref[:, pl.ds(j * LANES, LANES)] = x[pl.ds(i * chunks + j, channels, stride=2 * chunks), :]


def transform(x, fh, fl, ih, il, wfh, wfl, wih, wil, twc, tws, out):
    nblk, _, chunks, lanes = x.shape
    rows = nblk * chunks
    sig = jnp.concatenate([x[:, i].reshape(rows, lanes) for i in range(3)], axis=1)
    spec = dot_left(fh[...], fl[...], sig)
    c, s = twc[...], tws[...]
    parts = []
    for i in range(3):
        re = spec[:rows, i * lanes:(i + 1) * lanes]
        im = spec[rows:, i * lanes:(i + 1) * lanes]
        v = jnp.concatenate([re * c + im * s, im * c - re * s], axis=1)
        b = dot_right(v, wfh[...], wfl[...])
        parts.append((b[:, :lanes], b[:, lanes:]))
    (xr, xi), (gr, gi), (hr, hi) = parts
    back = []
    for (ur, ui) in ((hr, hi), (xr, xi)):
        p = jnp.concatenate([ur * gr + ui * gi, ur * gi - ui * gr], axis=1)
        d = dot_right(p, wih[...], wil[...])
        dr, di = d[:, :lanes], d[:, lanes:]
        back.append(jnp.concatenate([dr * c - di * s, di * c + dr * s], axis=0))
    y = dot_left(ih[...], il[...], jnp.concatenate(back, axis=1))
    for i in range(2):
        out[:, i] = y[:, i * lanes:(i + 1) * lanes].reshape(nblk, chunks, lanes)


def vm(n):
    return [pl.BlockSpec(memory_space=pltpu.VMEM)] * n


def per_device(inputs, grads, response):
    n = lax.axis_size("context")
    channels, block = inputs.shape
    length = block * n
    chunks = block // LANES
    sent = pl.pallas_call(
        spread,
        out_shape=jax.ShapeDtypeStruct((channels * 3 * chunks, LANES), jnp.float32),
        in_specs=vm(3),
        out_specs=vm(1)[0],
    )(inputs, grads, response)
    got = lax.all_to_all(sent.reshape(n, 3, chunks, LANES), "context", split_axis=0, concat_axis=0, tiled=True)
    y = pl.pallas_call(
        transform,
        out_shape=jax.ShapeDtypeStruct((n, 2, chunks, LANES), jnp.float32),
        in_specs=vm(11),
        out_specs=vm(1)[0],
    )(got, *[jnp.asarray(t) for t in tables(length)])
    back = lax.all_to_all(y, "context", split_axis=0, concat_axis=0, tiled=True)
    return pl.pallas_call(
        gather,
        out_shape=[jax.ShapeDtypeStruct((channels, block), jnp.float32)] * 2,
        in_specs=vm(1),
        out_specs=vm(2),
    )(back.reshape(channels * 2 * chunks, LANES))


RADIX = 128


HIGHEST = lax.Precision.HIGHEST


def phase_pair(row_index, col_index, period, sign_flip):
    product = row_index[:, None] * col_index[None, :] % period
    angles = 2.0 * math.pi / period * product.astype(jnp.float32)
    return (jnp.cos(angles), sign_flip * jnp.sin(angles))


def complex_apply(pattern, tables, values):
    real_real = jnp.einsum(pattern, tables[0], values[0], precision=HIGHEST)
    imag_imag = jnp.einsum(pattern, tables[1], values[1], precision=HIGHEST)
    real_imag = jnp.einsum(pattern, tables[0], values[1], precision=HIGHEST)
    imag_real = jnp.einsum(pattern, tables[1], values[0], precision=HIGHEST)
    return (real_real - imag_imag, real_imag + imag_real)


def complex_times(left_pair, right_pair):
    return (
        left_pair[0] * right_pair[0] - left_pair[1] * right_pair[1],
        left_pair[0] * right_pair[1] + left_pair[1] * right_pair[0],
    )


def by_columns(inputs, grads, response):
    context_size = lax.axis_size("context")
    device_index = lax.axis_index("context")
    channels, block_len = inputs.shape
    column_len = block_len // context_size
    full_length = block_len * context_size
    padded_len = 2 * full_length
    split_len = block_len // RADIX
    freq_rows = jnp.arange(2 * context_size, dtype=jnp.int32)
    part_rows = jnp.arange(context_size, dtype=jnp.int32)
    outer_fwd = phase_pair(freq_rows, part_rows, 2 * context_size, -1.0)
    outer_inv = phase_pair(part_rows, freq_rows, 2 * context_size, 1.0)
    split_rows = jnp.arange(split_len, dtype=jnp.int32)
    radix_rows = jnp.arange(RADIX, dtype=jnp.int32)
    first_fwd = phase_pair(split_rows, split_rows, split_len, -1.0)
    first_inv = (first_fwd[0], -first_fwd[1])
    inner_fwd = phase_pair(split_rows, radix_rows, block_len, -1.0)
    inner_inv = (inner_fwd[0], -inner_fwd[1])
    last_fwd = phase_pair(radix_rows, radix_rows, RADIX, -1.0)
    last_inv = (last_fwd[0], -last_fwd[1])
    pair_rows = 2 * device_index + jnp.arange(2, dtype=jnp.int32)
    column_rows = jnp.arange(block_len, dtype=jnp.int32)
    global_fwd = phase_pair(pair_rows, column_rows, padded_len, -1.0)
    global_inv = (global_fwd[0], -global_fwd[1])
    signals = jnp.stack([inputs, grads, response])
    columns = lax.all_to_all(
        signals.reshape(3, channels, context_size, column_len),
        "context",
        split_axis=2,
        concat_axis=2,
        tiled=True,
    )
    real_part = jnp.einsum("kn,smnj->smkj", outer_fwd[0], columns, precision=HIGHEST)
    imag_part = jnp.einsum("kn,smnj->smkj", outer_fwd[1], columns, precision=HIGHEST)
    columns = jnp.stack([real_part, imag_part], axis=1)
    arrived = lax.all_to_all(columns, "context", split_axis=3, concat_axis=4, tiled=True)
    values = complex_times((arrived[:, 0], arrived[:, 1]), global_fwd)
    shaped = tuple((v.reshape(v.shape[:3] + (split_len, RADIX)) for v in values))
    sectioned = complex_apply("xa,smrab->smrxb", first_fwd, shaped)
    turned = complex_times(sectioned, inner_fwd)
    spec_real, spec_imag = complex_apply("bd,smrxb->smrxd", last_fwd, turned)
    back_input = (
        spec_real[2] * spec_real[1] + spec_imag[2] * spec_imag[1],
        spec_real[2] * spec_imag[1] - spec_imag[2] * spec_real[1],
    )
    back_filter = (
        spec_real[0] * spec_real[1] + spec_imag[0] * spec_imag[1],
        spec_real[0] * spec_imag[1] - spec_imag[0] * spec_real[1],
    )
    inverse_in = ((back_input[0] - back_filter[1])[None], (back_input[1] + back_filter[0])[None])
    sectioned = complex_apply("bd,smrxd->smrxb", last_inv, inverse_in)
    turned = complex_times(sectioned, inner_inv)
    rebuilt = complex_apply("ax,smrxb->smrab", first_inv, turned)
    flat = tuple((v.reshape(v.shape[:3] + (block_len,)) for v in rebuilt))
    untwisted = complex_times(flat, global_inv)
    rows_back = jnp.stack([untwisted[0], untwisted[1]], axis=1)
    arrived = lax.all_to_all(rows_back, "context", split_axis=4, concat_axis=3, tiled=True)
    cos_real = jnp.einsum("nk,smkj->smnj", outer_inv[0], arrived[:, 0], precision=HIGHEST)
    sin_imag = jnp.einsum("nk,smkj->smnj", outer_inv[1], arrived[:, 1], precision=HIGHEST)
    cos_imag = jnp.einsum("nk,smkj->smnj", outer_inv[0], arrived[:, 1], precision=HIGHEST)
    sin_real = jnp.einsum("nk,smkj->smnj", outer_inv[1], arrived[:, 0], precision=HIGHEST)
    folded = jnp.concatenate([cos_real - sin_imag, cos_imag + sin_real], axis=0) / padded_len
    restored = lax.all_to_all(folded, "context", split_axis=2, concat_axis=3, tiled=True).reshape(
        2, channels, block_len
    )
    return (restored[0], restored[1])


def by_shape(inputs, grads, response):
    if inputs.shape[0] == lax.axis_size("context"):
        return per_device(inputs, grads, response)
    return by_columns(inputs, grads, response)


def solution(mesh):
    spec = P("tensor", "context")
    return jax.shard_map(by_shape, mesh=mesh, in_specs=(spec,) * 3, out_specs=(spec,) * 2, check_vma=False)
```

```python
import functools
import math

import jax
import jax.numpy as jnp
import numpy as np
from jax import lax
from jax.experimental import pallas as pl
from jax.experimental.pallas import tpu as pltpu
from jax.sharding import PartitionSpec as P

LANES = 128
BF = jnp.bfloat16


def halves(table):
    table = table.astype(np.float32)
    high = table.astype(BF)
    low = (table - high.astype(np.float32)).astype(BF)
    return high, low


def tables(length):
    rows = length // LANES
    k = np.arange(rows)[:, None] + 0.25
    r = np.arange(rows)[None, :]
    outer = 2 * np.pi * k * r / rows
    cos1, sin1 = np.cos(outer), np.sin(outer)
    first = halves(np.concatenate([cos1, -sin1], axis=0))
    last = halves(np.concatenate([cos1.T, -sin1.T], axis=1) / length)
    lane = np.arange(LANES)
    turn = 2 * np.pi * k * lane[None, :] / length
    twiddle = halves(np.concatenate([np.cos(turn), np.sin(turn)], axis=1))
    inner = 2 * np.pi * (lane[:, None] * lane[None, :] % LANES) / LANES
    c2, s2 = np.cos(inner), np.sin(inner)
    into = halves(np.block([[c2, -s2], [s2, c2]]))
    wide = [t.reshape(-1, 2 * LANES) for t in (*into, *twiddle)]
    return np.concatenate(first, axis=0), np.concatenate(last, axis=0), np.concatenate(wide, axis=0)


def split(x):
    high = x.astype(BF)
    low = (x - high.astype(jnp.float32)).astype(BF)
    return high, low


def dot(a, b):
    return jnp.dot(a, b, preferred_element_type=jnp.float32)


def dot_left(th, tl, x):
    xh, xl = split(x)
    return dot(th, xh) + (dot(th, xl) + dot(tl, xh))


def dot_right(x, th, tl):
    xh, xl = split(x)
    return dot(xh, th) + (dot(xl, th) + dot(xh, tl))


def place():
    me = lax.axis_index("context")
    chip, core = me // 2, me % 2
    return core, chip, chip ^ 3, chip ^ (1 + core), chip ^ (2 - core)


def part(index, step):
    return pl.ds(pl.multiple_of(index * step, step), step)


def pack(pieces, own, far, aside, beside):
    core, chip, opposite, one, two = place()
    step = own.shape[0]
    here, other = core, 1 - core
    for out, at, to_chip, to_core in (
        (own, 0, chip, here), (far, 0, opposite, here), (far, 1, opposite, other),
        (aside, 0, chip, other), (aside, 1, two, other), (aside, 2, one, other),
        (beside, 0, one, here), (beside, 1, two, here),
    ):
        out[at * step:(at + 1) * step, :] = pieces[part(to_chip * 2 + to_core, step), :]


def merge(beside, aside, first, second):
    step = beside.shape[0] // 2
    for i, out in enumerate((first, second)):
        out[:step, :] = beside[i * step:(i + 1) * step, :]
        out[step:, :] = aside[(i + 1) * step:(i + 2) * step, :]


def second_half(x, out):
    out[...] = x[out.shape[0]:, :]


def unpack(got, held):
    core, chip, opposite, one, two = place()
    own, aside, far, far_other, first, second = got
    step = own.shape[0]
    here, other = core, 1 - core
    for ref, at, from_chip, from_core in (
        (own, 0, chip, here), (aside, 0, chip, other), (far, 0, opposite, here), (far_other, 0, opposite, other),
        (first, 0, one, here), (first, 1, one, other), (second, 0, two, here), (second, 1, two, other),
    ):
        held[part(from_chip * 2 + from_core, step), :] = ref[at * step:(at + 1) * step, :]


def fetch(*refs):
    count = (len(refs) - 2) // 2
    copies = [pltpu.make_async_copy(refs[i], refs[count + 1 + i], refs[-1].at[i]) for i in range(count)]
    for copy in copies:
        copy.start()
    for copy in copies:
        copy.wait()


def spread(a, b, c, *rest):
    *outs, held = rest
    channels, block = a.shape
    chunks = block // LANES
    for i, ref in enumerate((a, b, c)):
        for j in range(chunks):
            held[pl.ds(i * chunks + j, channels, stride=3 * chunks), :] = ref[:, pl.ds(j * LANES, LANES)]
    pack(held, *outs)


def gather(*refs):
    *got, a, b, held = refs
    unpack(got, held)
    channels, block = a.shape
    chunks = block // LANES
    for i, ref in enumerate((a, b)):
        for j in range(chunks):
            ref[:, pl.ds(j * LANES, LANES)] = held[pl.ds(i * chunks + j, channels, stride=2 * chunks), :]


def transform(*refs):
    got, (first, last, wide), outs, (held, y) = refs[:6], refs[6:9], refs[9:13], refs[13:]
    unpack(got, held)
    n = held.shape[0] // got[0].shape[0]
    chunks = got[0].shape[0] // 3
    rows = n * chunks
    pieces = held[...].reshape(n, 3, chunks, LANES)
    sig = jnp.concatenate([pieces[:, i].reshape(rows, LANES) for i in range(3)], axis=1)
    spec = dot_left(first[:2 * rows], first[2 * rows:], sig)
    two = 2 * LANES
    into_h, into_l = wide[:two], wide[two:2 * two]
    twiddle = wide[2 * two:2 * two + rows].astype(jnp.float32) + wide[2 * two + rows:].astype(jnp.float32)
    c, s = twiddle[:, :LANES], twiddle[:, LANES:]
    parts = []
    for i in range(3):
        re = spec[:rows, i * LANES:(i + 1) * LANES]
        im = spec[rows:, i * LANES:(i + 1) * LANES]
        v = jnp.concatenate([re * c + im * s, im * c - re * s], axis=1)
        f = dot_right(v, into_h, into_l)
        parts.append((f[:, :LANES], f[:, LANES:]))
    (xr, xi), (gr, gi), (hr, hi) = parts
    turned = []
    for ur, ui in ((hr, hi), (xr, xi)):
        p = jnp.concatenate([ur * gr + ui * gi, ui * gr - ur * gi], axis=1)
        d = dot_right(p, into_h, into_l)
        dr, di = d[:, :LANES], d[:, LANES:]
        turned.append(jnp.concatenate([dr * c + di * s, dr * s - di * c], axis=0))
    out = dot_left(last[:rows], last[rows:], jnp.concatenate(turned, axis=1))
    for d in range(n):
        for i in range(2):
            y[(d * 2 + i) * chunks:(d * 2 + i + 1) * chunks, :] = out[d * chunks:(d + 1) * chunks, i * LANES:(i + 1) * LANES]
    pack(y, *outs)


def call(body, ins, outs, scratch=(), near_in=True, near_out=True):
    where = pl.BlockSpec(memory_space=pltpu.VMEM)
    if near_in:
        ins = [pltpu.with_memory_space_constraint(x, pltpu.VMEM) for x in ins]
    kind = pltpu.VMEM if near_out else jax.ShapeDtypeStruct
    return pl.pallas_call(
        body,
        out_shape=[kind(shape, jnp.float32) for shape in outs],
        in_specs=[where] * len(ins),
        out_specs=[where] * len(outs),
        scratch_shapes=[pltpu.VMEM(shape, jnp.float32) for shape in scratch],
        name=body.__name__,
    )(*ins)


def per_device(inputs, grads, response):
    n = lax.axis_size("context")
    channels, block = inputs.shape
    length = block * n
    chunks = block // LANES
    rows = length // LANES
    signals = (inputs, grads, response)

    def swap(x, even, odd):
        return lax.ppermute(x, "context", [(i, i ^ (odd if i % 2 else even)) for i in range(n)])

    def sizes(arrays):
        return [(u * arrays * chunks, LANES) for u in (1, 2, 3, 2)]

    def exchange(own, far, aside, beside):
        step = own.shape[0]
        aside = swap(aside, 1, 1)
        far = swap(far, 6, 6)
        first, second = call(merge, [beside, aside], [(2 * step, LANES)] * 2)
        first, second = swap(first, 2, 4), swap(second, 4, 2)
        (half,) = call(second_half, [far], [(step, LANES)])
        return own, aside, far, swap(half, 1, 1), first, second

    sent = call(spread, signals, sizes(3), [(channels * 3 * chunks, LANES)], near_in=False)
    got = exchange(*sent)
    held = [jnp.asarray(t) for t in tables(length)]
    held = pl.pallas_call(
        fetch,
        out_shape=[pltpu.VMEM(t.shape, t.dtype) for t in held],
        in_specs=[pl.BlockSpec(memory_space=pl.ANY)] * len(held) + [pl.BlockSpec(memory_space=pltpu.VMEM)],
        out_specs=[pl.BlockSpec(memory_space=pltpu.VMEM)] * len(held),
        scratch_shapes=[pltpu.SemaphoreType.DMA((len(held),))],
        name="fetch",
    )(*held, pltpu.with_memory_space_constraint(got[1], pltpu.VMEM))
    sent = call(transform, [*got, *held], sizes(2), [(rows * 3, LANES), (rows * 2, LANES)])
    got = exchange(*sent)
    return call(gather, got, [(channels, block)] * 2, [(rows * 2, LANES)], near_out=False)


RADIX = 128


HIGHEST = lax.Precision.HIGHEST


def phase_pair(row_index, col_index, period, sign_flip):
    product = row_index[:, None] * col_index[None, :] % period
    angles = 2.0 * math.pi / period * product.astype(jnp.float32)
    return (jnp.cos(angles), sign_flip * jnp.sin(angles))


def complex_apply(pattern, tables, values):
    real_real = jnp.einsum(pattern, tables[0], values[0], precision=HIGHEST)
    imag_imag = jnp.einsum(pattern, tables[1], values[1], precision=HIGHEST)
    real_imag = jnp.einsum(pattern, tables[0], values[1], precision=HIGHEST)
    imag_real = jnp.einsum(pattern, tables[1], values[0], precision=HIGHEST)
    return (real_real - imag_imag, real_imag + imag_real)


def complex_times(left_pair, right_pair):
    return (
        left_pair[0] * right_pair[0] - left_pair[1] * right_pair[1],
        left_pair[0] * right_pair[1] + left_pair[1] * right_pair[0],
    )


def by_columns(inputs, grads, response):
    context_size = lax.axis_size("context")
    device_index = lax.axis_index("context")
    channels, block_len = inputs.shape
    column_len = block_len // context_size
    full_length = block_len * context_size
    padded_len = 2 * full_length
    split_len = block_len // RADIX
    freq_rows = jnp.arange(2 * context_size, dtype=jnp.int32)
    part_rows = jnp.arange(context_size, dtype=jnp.int32)
    outer_fwd = phase_pair(freq_rows, part_rows, 2 * context_size, -1.0)
    outer_inv = phase_pair(part_rows, freq_rows, 2 * context_size, 1.0)
    split_rows = jnp.arange(split_len, dtype=jnp.int32)
    radix_rows = jnp.arange(RADIX, dtype=jnp.int32)
    first_fwd = phase_pair(split_rows, split_rows, split_len, -1.0)
    first_inv = (first_fwd[0], -first_fwd[1])
    inner_fwd = phase_pair(split_rows, radix_rows, block_len, -1.0)
    inner_inv = (inner_fwd[0], -inner_fwd[1])
    last_fwd = phase_pair(radix_rows, radix_rows, RADIX, -1.0)
    last_inv = (last_fwd[0], -last_fwd[1])
    pair_rows = 2 * device_index + jnp.arange(2, dtype=jnp.int32)
    column_rows = jnp.arange(block_len, dtype=jnp.int32)
    global_fwd = phase_pair(pair_rows, column_rows, padded_len, -1.0)
    global_inv = (global_fwd[0], -global_fwd[1])
    signals = jnp.stack([inputs, grads, response])
    columns = lax.all_to_all(
        signals.reshape(3, channels, context_size, column_len),
        "context",
        split_axis=2,
        concat_axis=2,
        tiled=True,
    )
    real_part = jnp.einsum("kn,smnj->smkj", outer_fwd[0], columns, precision=HIGHEST)
    imag_part = jnp.einsum("kn,smnj->smkj", outer_fwd[1], columns, precision=HIGHEST)
    columns = jnp.stack([real_part, imag_part], axis=1)
    arrived = lax.all_to_all(columns, "context", split_axis=3, concat_axis=4, tiled=True)
    values = complex_times((arrived[:, 0], arrived[:, 1]), global_fwd)
    shaped = tuple((v.reshape(v.shape[:3] + (split_len, RADIX)) for v in values))
    sectioned = complex_apply("xa,smrab->smrxb", first_fwd, shaped)
    turned = complex_times(sectioned, inner_fwd)
    spec_real, spec_imag = complex_apply("bd,smrxb->smrxd", last_fwd, turned)
    back_input = (
        spec_real[2] * spec_real[1] + spec_imag[2] * spec_imag[1],
        spec_real[2] * spec_imag[1] - spec_imag[2] * spec_real[1],
    )
    back_filter = (
        spec_real[0] * spec_real[1] + spec_imag[0] * spec_imag[1],
        spec_real[0] * spec_imag[1] - spec_imag[0] * spec_real[1],
    )
    inverse_in = ((back_input[0] - back_filter[1])[None], (back_input[1] + back_filter[0])[None])
    sectioned = complex_apply("bd,smrxd->smrxb", last_inv, inverse_in)
    turned = complex_times(sectioned, inner_inv)
    rebuilt = complex_apply("ax,smrxb->smrab", first_inv, turned)
    flat = tuple((v.reshape(v.shape[:3] + (block_len,)) for v in rebuilt))
    untwisted = complex_times(flat, global_inv)
    rows_back = jnp.stack([untwisted[0], untwisted[1]], axis=1)
    arrived = lax.all_to_all(rows_back, "context", split_axis=4, concat_axis=3, tiled=True)
    cos_real = jnp.einsum("nk,smkj->smnj", outer_inv[0], arrived[:, 0], precision=HIGHEST)
    sin_imag = jnp.einsum("nk,smkj->smnj", outer_inv[1], arrived[:, 1], precision=HIGHEST)
    cos_imag = jnp.einsum("nk,smkj->smnj", outer_inv[0], arrived[:, 1], precision=HIGHEST)
    sin_real = jnp.einsum("nk,smkj->smnj", outer_inv[1], arrived[:, 0], precision=HIGHEST)
    folded = jnp.concatenate([cos_real - sin_imag, cos_imag + sin_real], axis=0) / padded_len
    restored = lax.all_to_all(folded, "context", split_axis=2, concat_axis=3, tiled=True).reshape(
        2, channels, block_len
    )
    return (restored[0], restored[1])


def by_shape(inputs, grads, response):
    if inputs.shape[0] == lax.axis_size("context") == 2 * 2 * 2:
        return per_device(inputs, grads, response)
    return by_columns(inputs, grads, response)


def solution(mesh):
    spec = P("tensor", "context")
    return jax.shard_map(by_shape, mesh=mesh, in_specs=(spec,) * 3, out_specs=(spec,) * 2, check_vma=False)
```

```python
import functools
import math

import jax
import jax.numpy as jnp
import numpy as np
from jax import lax
from jax.experimental import pallas as pl
from jax.experimental.pallas import tpu as pltpu
from jax.sharding import PartitionSpec as P

LANES = 128
BF = jnp.bfloat16
PARTS, JOINED, LOADS = 4, 2, 4


def halves(table):
    table = table.astype(np.float32)
    high = table.astype(BF)
    low = (table - high.astype(np.float32)).astype(BF)
    return high, low


def tables(length, parts, joined):
    rows = length // LANES
    k = np.arange(rows)[:, None] + 0.25
    r = np.arange(rows)[None, :]
    outer = 2 * np.pi * k * r / rows
    stacked = np.stack([np.cos(outer), -np.sin(outer)])
    first = stacked.reshape(2, parts, rows // parts, rows).swapaxes(0, 1).reshape(2 * rows, rows)
    last = (stacked / length).reshape(2, joined, rows // joined, rows).transpose(1, 3, 0, 2)
    last = last.reshape(joined, rows, 2 * rows // joined)
    lane = np.arange(LANES)
    turn = 2 * np.pi * k * lane[None, :] / length
    twiddle = np.concatenate([np.cos(turn), np.sin(turn)], axis=1).astype(np.float32)
    inner = 2 * np.pi * (lane[:, None] * lane[None, :] % LANES) / LANES
    cos2, sin2 = np.cos(inner), np.sin(inner)
    into = np.block([[cos2, -sin2], [sin2, cos2]])
    return np.stack(halves(first)), np.stack(halves(last)), np.stack(halves(into)), twiddle


def split(x):
    high = x.astype(BF)
    low = (x - high.astype(jnp.float32)).astype(BF)
    return high, low


def dot(a, b):
    return jnp.dot(a, b, preferred_element_type=jnp.float32)


def dot_right(x, table):
    high, low = split(x)
    return dot(high, table[0]) + (dot(low, table[0]) + dot(high, table[1]))


def dot_left(table_high, table_low, x):
    high, low = x
    return dot(table_high, high) + (dot(table_high, low) + dot(table_low, high))


def lanes_of(x, i, m):
    return x[i * m:(i + 1) * m, :LANES], x[i * m:(i + 1) * m, LANES:]


def place():
    me = lax.axis_index("context")
    chip, core = me // 2, me % 2
    return core, chip, chip ^ 3, chip ^ (1 + core), chip ^ (2 - core)


def part(index, step):
    return pl.ds(pl.multiple_of(index * step, step), step)


def pack(pieces, own, far, aside, beside):
    core, chip, opposite, one, two = place()
    step = own.shape[0]
    here, other = core, 1 - core
    for out, at, to_chip, to_core in (
        (own, 0, chip, here), (far, 0, opposite, here), (far, 1, opposite, other),
        (aside, 0, chip, other), (aside, 1, two, other), (aside, 2, one, other),
        (beside, 0, one, here), (beside, 1, two, here),
    ):
        out[at * step:(at + 1) * step, :] = pieces[part(to_chip * 2 + to_core, step), :]


def merge(beside, aside, first, second):
    step = beside.shape[0] // 2
    for i, out in enumerate((first, second)):
        out[:step, :] = beside[i * step:(i + 1) * step, :]
        out[step:, :] = aside[(i + 1) * step:(i + 2) * step, :]


def second_half(x, *rest):
    out = rest[-1]
    out[...] = x[out.shape[0]:, :]


def unpack(got, held):
    core, chip, opposite, one, two = place()
    own, aside, far, far_other, first, second = got
    step = own.shape[0]
    here, other = core, 1 - core
    for ref, at, from_chip, from_core in (
        (own, 0, chip, here), (aside, 0, chip, other), (far, 0, opposite, here), (far_other, 0, opposite, other),
        (first, 0, one, here), (first, 1, one, other), (second, 0, two, here), (second, 1, two, other),
    ):
        held[part(from_chip * 2 + from_core, step), :] = ref[at * step:(at + 1) * step, :]


def fetch(*refs):
    count = (len(refs) - 2) // 2
    copies = [pltpu.make_async_copy(refs[i], refs[count + 1 + i], refs[-1].at[i]) for i in range(count)]
    for copy in copies:
        copy.start()
    for copy in copies:
        copy.wait()


def spread(*refs):
    signals, outs, near, (held, arrived) = refs[:3], refs[3:7], refs[7:10], refs[10:]
    channels, block = signals[0].shape
    chunks = block // LANES
    width = block // LOADS
    copies = []
    for load in range(LOADS):
        at = pl.ds(load * width, width)
        for i in range(3):
            copies.append(pltpu.make_async_copy(signals[i].at[:, at], near[i].at[:, at], arrived.at[load * 3 + i]))
            copies[-1].start()
    for load in range(LOADS):
        for i in range(3):
            copies[load * 3 + i].wait()
            for j in range(load * chunks // LOADS, (load + 1) * chunks // LOADS):
                held[pl.ds(i * chunks + j, channels, stride=3 * chunks), :] = near[i][:, pl.ds(j * LANES, LANES)]
    pack(held, *outs)


def transform(*refs):
    got, (first, last, into, twiddle), outs, (held, y) = refs[:6], refs[6:10], refs[10:14], refs[14:]
    unpack(got, held)
    n = held.shape[0] // got[0].shape[0]
    chunks = got[0].shape[0] // 3
    rows = n * chunks
    m = rows // PARTS
    pieces = held[...].reshape(n, 3, chunks, LANES)
    signals = split(jnp.concatenate([pieces[:, i].reshape(rows, LANES) for i in range(3)], axis=1))
    turns = [lanes_of(twiddle, q, m) for q in range(PARTS)]
    outer = [dot_left(first[0, 2 * m * q:2 * m * (q + 1)], first[1, 2 * m * q:2 * m * (q + 1)], signals) for q in range(PARTS)]
    spectra = []
    for z, (c, s) in zip(outer, turns):
        turned = []
        for i in range(3):
            re, im = z[:m, i * LANES:(i + 1) * LANES], z[m:, i * LANES:(i + 1) * LANES]
            turned.append(jnp.concatenate([re * c + im * s, im * c - re * s], axis=1))
        spectra.append(dot_right(jnp.concatenate(turned, axis=0), into))
    backs = []
    for z in spectra:
        (xr, xi), (gr, gi), (hr, hi) = (lanes_of(z, i, m) for i in range(3))
        p = [jnp.concatenate([ur * gr + ui * gi, ui * gr - ur * gi], axis=1) for ur, ui in ((hr, hi), (xr, xi))]
        backs.append(dot_right(jnp.concatenate(p, axis=0), into))
    out = 0.0
    for joined in range(JOINED):
        real, imag = [], []
        for q in range(joined * PARTS // JOINED, (joined + 1) * PARTS // JOINED):
            c, s = turns[q]
            pairs = [lanes_of(backs[q], i, m) for i in range(2)]
            real.append(jnp.concatenate([dr * c + di * s for dr, di in pairs], axis=1))
            imag.append(jnp.concatenate([dr * s - di * c for dr, di in pairs], axis=1))
        out += dot_left(last[0, joined], last[1, joined], split(jnp.concatenate(real + imag, axis=0)))
    for d in range(n):
        for i in range(2):
            y[(d * 2 + i) * chunks:(d * 2 + i + 1) * chunks, :] = out[d * chunks:(d + 1) * chunks, i * LANES:(i + 1) * LANES]
    pack(y, *outs)


def gather(*refs):
    *got, a, b, held = refs
    unpack(got, held)
    channels, block = a.shape
    chunks = block // LANES
    for i, ref in enumerate((a, b)):
        for j in range(chunks):
            ref[:, pl.ds(j * LANES, LANES)] = held[pl.ds(i * chunks + j, channels, stride=2 * chunks), :]


def call(body, ins, outs, scratch=(), far_in=0, near_out=True):
    near = pl.BlockSpec(memory_space=pltpu.VMEM)
    kind = pltpu.VMEM if near_out else jax.ShapeDtypeStruct
    return pl.pallas_call(
        body,
        out_shape=[kind(shape, dtype) for shape, dtype in outs],
        in_specs=[pl.BlockSpec(memory_space=pl.ANY)] * far_in + [near] * (len(ins) - far_in),
        out_specs=[near] * len(outs),
        scratch_shapes=scratch,
        name=body.__name__,
    )(*ins[:far_in], *(pltpu.with_memory_space_constraint(x, pltpu.VMEM) for x in ins[far_in:]))


def per_device(inputs, grads, response):
    n = lax.axis_size("context")
    channels, block = inputs.shape
    chunks = block // LANES
    kind = jnp.float32

    def swap(x, even, odd):
        return lax.ppermute(x, "context", [(i, i ^ (odd if i % 2 else even)) for i in range(n)])

    def sizes(arrays):
        return [((u * arrays * chunks, LANES), kind) for u in (1, 2, 3, 2)]

    def exchange(own, far, aside, beside, meanwhile=lambda x: []):
        step = own.shape[0]
        aside = swap(aside, 1, 1)
        far = swap(far, 6, 6)
        first, second = call(merge, [beside, aside], [((2 * step, LANES), kind)] * 2)
        made = meanwhile(second)
        first, second = swap(first, 2, 4), swap(second, 4, 2)
        (half,) = call(second_half, [far, *made[:1]], [((step, LANES), kind)])
        return [own, aside, far, swap(half, 1, 1), first, second, *made]

    held = [jnp.asarray(t) for t in tables(n * block, PARTS, JOINED)]

    def bring(after):
        return call(fetch, [*held, after], [(t.shape, t.dtype) for t in held], [pltpu.SemaphoreType.DMA((len(held),))], len(held))

    near = [pltpu.VMEM((channels, block), kind)] * 3
    near += [pltpu.VMEM((channels * 3 * chunks, LANES), kind), pltpu.SemaphoreType.DMA((3 * LOADS,))]
    sent = call(spread, [inputs, grads, response], sizes(3), near, 3)
    got = exchange(*sent, meanwhile=bring)
    near = [pltpu.VMEM((n * arrays * chunks, LANES), kind) for arrays in (3, 2)]
    got = exchange(*call(transform, got, sizes(2), near))
    return call(gather, got, [((channels, block), kind)] * 2, near[1:], near_out=False)


RADIX = 128


HIGHEST = lax.Precision.HIGHEST


def phase_pair(row_index, col_index, period, sign_flip):
    product = row_index[:, None] * col_index[None, :] % period
    angles = 2.0 * math.pi / period * product.astype(jnp.float32)
    return (jnp.cos(angles), sign_flip * jnp.sin(angles))


def complex_apply(pattern, tables, values):
    real_real = jnp.einsum(pattern, tables[0], values[0], precision=HIGHEST)
    imag_imag = jnp.einsum(pattern, tables[1], values[1], precision=HIGHEST)
    real_imag = jnp.einsum(pattern, tables[0], values[1], precision=HIGHEST)
    imag_real = jnp.einsum(pattern, tables[1], values[0], precision=HIGHEST)
    return (real_real - imag_imag, real_imag + imag_real)


def complex_times(left_pair, right_pair):
    return (
        left_pair[0] * right_pair[0] - left_pair[1] * right_pair[1],
        left_pair[0] * right_pair[1] + left_pair[1] * right_pair[0],
    )


def by_columns(inputs, grads, response):
    context_size = lax.axis_size("context")
    device_index = lax.axis_index("context")
    channels, block_len = inputs.shape
    column_len = block_len // context_size
    full_length = block_len * context_size
    padded_len = 2 * full_length
    split_len = block_len // RADIX
    freq_rows = jnp.arange(2 * context_size, dtype=jnp.int32)
    part_rows = jnp.arange(context_size, dtype=jnp.int32)
    outer_fwd = phase_pair(freq_rows, part_rows, 2 * context_size, -1.0)
    outer_inv = phase_pair(part_rows, freq_rows, 2 * context_size, 1.0)
    split_rows = jnp.arange(split_len, dtype=jnp.int32)
    radix_rows = jnp.arange(RADIX, dtype=jnp.int32)
    first_fwd = phase_pair(split_rows, split_rows, split_len, -1.0)
    first_inv = (first_fwd[0], -first_fwd[1])
    inner_fwd = phase_pair(split_rows, radix_rows, block_len, -1.0)
    inner_inv = (inner_fwd[0], -inner_fwd[1])
    last_fwd = phase_pair(radix_rows, radix_rows, RADIX, -1.0)
    last_inv = (last_fwd[0], -last_fwd[1])
    pair_rows = 2 * device_index + jnp.arange(2, dtype=jnp.int32)
    column_rows = jnp.arange(block_len, dtype=jnp.int32)
    global_fwd = phase_pair(pair_rows, column_rows, padded_len, -1.0)
    global_inv = (global_fwd[0], -global_fwd[1])
    signals = jnp.stack([inputs, grads, response])
    columns = lax.all_to_all(
        signals.reshape(3, channels, context_size, column_len),
        "context",
        split_axis=2,
        concat_axis=2,
        tiled=True,
    )
    real_part = jnp.einsum("kn,smnj->smkj", outer_fwd[0], columns, precision=HIGHEST)
    imag_part = jnp.einsum("kn,smnj->smkj", outer_fwd[1], columns, precision=HIGHEST)
    columns = jnp.stack([real_part, imag_part], axis=1)
    arrived = lax.all_to_all(columns, "context", split_axis=3, concat_axis=4, tiled=True)
    values = complex_times((arrived[:, 0], arrived[:, 1]), global_fwd)
    shaped = tuple((v.reshape(v.shape[:3] + (split_len, RADIX)) for v in values))
    sectioned = complex_apply("xa,smrab->smrxb", first_fwd, shaped)
    turned = complex_times(sectioned, inner_fwd)
    spec_real, spec_imag = complex_apply("bd,smrxb->smrxd", last_fwd, turned)
    back_input = (
        spec_real[2] * spec_real[1] + spec_imag[2] * spec_imag[1],
        spec_real[2] * spec_imag[1] - spec_imag[2] * spec_real[1],
    )
    back_filter = (
        spec_real[0] * spec_real[1] + spec_imag[0] * spec_imag[1],
        spec_real[0] * spec_imag[1] - spec_imag[0] * spec_real[1],
    )
    inverse_in = ((back_input[0] - back_filter[1])[None], (back_input[1] + back_filter[0])[None])
    sectioned = complex_apply("bd,smrxd->smrxb", last_inv, inverse_in)
    turned = complex_times(sectioned, inner_inv)
    rebuilt = complex_apply("ax,smrxb->smrab", first_inv, turned)
    flat = tuple((v.reshape(v.shape[:3] + (block_len,)) for v in rebuilt))
    untwisted = complex_times(flat, global_inv)
    rows_back = jnp.stack([untwisted[0], untwisted[1]], axis=1)
    arrived = lax.all_to_all(rows_back, "context", split_axis=4, concat_axis=3, tiled=True)
    cos_real = jnp.einsum("nk,smkj->smnj", outer_inv[0], arrived[:, 0], precision=HIGHEST)
    sin_imag = jnp.einsum("nk,smkj->smnj", outer_inv[1], arrived[:, 1], precision=HIGHEST)
    cos_imag = jnp.einsum("nk,smkj->smnj", outer_inv[0], arrived[:, 1], precision=HIGHEST)
    sin_real = jnp.einsum("nk,smkj->smnj", outer_inv[1], arrived[:, 0], precision=HIGHEST)
    folded = jnp.concatenate([cos_real - sin_imag, cos_imag + sin_real], axis=0) / padded_len
    restored = lax.all_to_all(folded, "context", split_axis=2, concat_axis=3, tiled=True).reshape(
        2, channels, block_len
    )
    return (restored[0], restored[1])


def by_shape(inputs, grads, response):
    if inputs.shape[0] == lax.axis_size("context") == 2 * 2 * 2:
        return per_device(inputs, grads, response)
    return by_columns(inputs, grads, response)


def solution(mesh):
    spec = P("tensor", "context")
    return jax.shard_map(by_shape, mesh=mesh, in_specs=(spec,) * 3, out_specs=(spec,) * 2, check_vma=False)
```

```python
import functools
import math

import jax
import jax.numpy as jnp
import numpy as np
from jax import lax
from jax.experimental import pallas as pl
from jax.experimental.pallas import tpu as pltpu
from jax.sharding import PartitionSpec as P

LANES = 128
BF = jnp.bfloat16
PARTS, JOINED, LOADS = 4, 2, 4


def halves(table):
    table = table.astype(np.float32)
    high = table.astype(BF)
    low = (table - high.astype(np.float32)).astype(BF)
    return high, low


def tables(length, parts, joined):
    rows = length // LANES
    k = np.arange(rows)[:, None] + 0.25
    r = np.arange(rows)[None, :]
    outer = 2 * np.pi * k * r / rows
    stacked = np.stack([np.cos(outer), -np.sin(outer)])
    first = stacked.reshape(2, parts, rows // parts, rows).swapaxes(0, 1).reshape(2 * rows, rows)
    last = (stacked / length).reshape(2, joined, rows // joined, rows).transpose(1, 3, 0, 2)
    last = last.reshape(joined, rows, 2 * rows // joined)
    lane = np.arange(LANES)
    turn = 2 * np.pi * k * lane[None, :] / length
    twiddle = np.concatenate([np.cos(turn), np.sin(turn)], axis=1).astype(np.float32)
    inner = 2 * np.pi * (lane[:, None] * lane[None, :] % LANES) / LANES
    cos2, sin2 = np.cos(inner), np.sin(inner)
    into = np.block([[cos2, -sin2], [sin2, cos2]])
    return np.stack(halves(first)), np.stack(halves(last)), np.stack(halves(into)), twiddle


def split(x):
    high = x.astype(BF)
    low = (x - high.astype(jnp.float32)).astype(BF)
    return high, low


def dot(a, b):
    return jnp.dot(a, b, preferred_element_type=jnp.float32)


def dot_right(x, table):
    high, low = split(x)
    return dot(high, table[0]) + (dot(low, table[0]) + dot(high, table[1]))


def dot_left(table_high, table_low, x):
    high, low = x
    return dot(table_high, high) + (dot(table_high, low) + dot(table_low, high))


def lanes_of(x, i, m):
    return x[i * m:(i + 1) * m, :LANES], x[i * m:(i + 1) * m, LANES:]


def place():
    me = lax.axis_index("context")
    chip, core = me // 2, me % 2
    return core, chip, chip ^ 3, chip ^ (1 + core), chip ^ (2 - core)


def pack(pieces, own, far, aside, beside):
    core, chip, opposite, one, two = place()
    step = own.shape[0]
    here, other = core, 1 - core
    for out, at, to_chip, to_core in (
        (own, 0, chip, here), (far, 0, opposite, here), (far, 1, opposite, other),
        (aside, 0, chip, other), (aside, 1, two, other), (aside, 2, one, other),
        (beside, 0, one, here), (beside, 1, two, here),
    ):
        out[at * step:(at + 1) * step, :] = pieces[to_chip * 2 + to_core]


def merge(beside, aside, first, second):
    step = beside.shape[0] // 2
    for i, out in enumerate((first, second)):
        out[:step, :] = beside[i * step:(i + 1) * step, :]
        out[step:, :] = aside[(i + 1) * step:(i + 2) * step, :]


def second_half(x, *rest):
    out = rest[-1]
    out[...] = x[out.shape[0]:, :]


def unpack(got, held):
    core, chip, opposite, one, two = place()
    own, aside, far, far_other, first, second = got
    step = own.shape[0]
    here, other = core, 1 - core
    for ref, at, from_chip, from_core in (
        (own, 0, chip, here), (aside, 0, chip, other), (far, 0, opposite, here), (far_other, 0, opposite, other),
        (first, 0, one, here), (first, 1, one, other), (second, 0, two, here), (second, 1, two, other),
    ):
        held[from_chip * 2 + from_core] = ref[at * step:(at + 1) * step, :]


def fetch(*refs):
    count = (len(refs) - 2) // 2
    copies = [pltpu.make_async_copy(refs[i], refs[count + 1 + i], refs[-1].at[i]) for i in range(count)]
    for copy in copies:
        copy.start()
    for copy in copies:
        copy.wait()


def spread(*refs):
    signals, outs, near, (held, arrived) = refs[:3], refs[3:7], refs[7:10], refs[10:]
    channels, block = signals[0].shape
    chunks = block // LANES
    width = block // LOADS

    def at(load):
        return pl.ds(load * width, width)

    copies = []
    for load in range(LOADS):
        for i in range(3):
            ends = signals[i].at[:, at(load)], near[i].at[:, at(load)]
            copies.append(pltpu.make_async_copy(*ends, arrived.at[load * 3 + i]))
            copies[-1].start()
    for load in range(LOADS):
        for i in range(3):
            copies[load * 3 + i].wait()
            rows = pl.ds(i * chunks + load * chunks // LOADS, chunks // LOADS)
            held[:, rows, :] = near[i][:, at(load)].reshape(channels, chunks // LOADS, LANES)
    pack(held, *outs)


def transform(*refs):
    got, (first, last, into, twiddle), outs, (held, y) = refs[:6], refs[6:10], refs[10:14], refs[14:]
    unpack(got, held)
    n = held.shape[0]
    chunks = held.shape[1] // 3
    rows = n * chunks
    m = rows // PARTS
    whole = [held[:, i * chunks:(i + 1) * chunks, :].reshape(rows, LANES) for i in range(3)]
    signals = split(jnp.concatenate(whole, axis=1))
    turns = [lanes_of(twiddle, q, m) for q in range(PARTS)]
    outer = [dot_left(first[0, 2 * m * q:2 * m * (q + 1)], first[1, 2 * m * q:2 * m * (q + 1)], signals) for q in range(PARTS)]
    spectra = []
    for z, (c, s) in zip(outer, turns):
        turned = []
        for i in range(3):
            re, im = z[:m, i * LANES:(i + 1) * LANES], z[m:, i * LANES:(i + 1) * LANES]
            turned.append(jnp.concatenate([re * c + im * s, im * c - re * s], axis=1))
        spectra.append(dot_right(jnp.concatenate(turned, axis=0), into))
    backs = []
    for z in spectra:
        (xr, xi), (gr, gi), (hr, hi) = (lanes_of(z, i, m) for i in range(3))
        p = [jnp.concatenate([ur * gr + ui * gi, ui * gr - ur * gi], axis=1) for ur, ui in ((hr, hi), (xr, xi))]
        backs.append(dot_right(jnp.concatenate(p, axis=0), into))
    out = 0.0
    for joined in range(JOINED):
        real, imag = [], []
        for q in range(joined * PARTS // JOINED, (joined + 1) * PARTS // JOINED):
            c, s = turns[q]
            pairs = [lanes_of(backs[q], i, m) for i in range(2)]
            real.append(jnp.concatenate([dr * c + di * s for dr, di in pairs], axis=1))
            imag.append(jnp.concatenate([dr * s - di * c for dr, di in pairs], axis=1))
        out += dot_left(last[0, joined], last[1, joined], split(jnp.concatenate(real + imag, axis=0)))
    for d in range(n):
        for i in range(2):
            y[d, i * chunks:(i + 1) * chunks, :] = out[d * chunks:(d + 1) * chunks, i * LANES:(i + 1) * LANES]
    pack(y, *outs)


def gather(*refs):
    got, (a, b, held) = refs[:6], refs[6:]
    unpack(got, held)
    channels, block = a.shape
    chunks = block // LANES
    for i, ref in enumerate((a, b)):
        for j in range(0, chunks, 8):
            ref[:, pl.ds(j * LANES, 8 * LANES)] = held[:, pl.ds(i * chunks + j, 8), :].reshape(channels, 8 * LANES)


def call(body, ins, outs, scratch=(), far_in=0, near_out=True):
    near = pl.BlockSpec(memory_space=pltpu.VMEM)
    kind = pltpu.VMEM if near_out else jax.ShapeDtypeStruct
    return pl.pallas_call(
        body,
        out_shape=[kind(shape, dtype) for shape, dtype in outs],
        in_specs=[pl.BlockSpec(memory_space=pl.ANY)] * far_in + [near] * (len(ins) - far_in),
        out_specs=[near] * len(outs),
        scratch_shapes=scratch,
        name=body.__name__,
    )(*ins[:far_in], *(pltpu.with_memory_space_constraint(x, pltpu.VMEM) for x in ins[far_in:]))


def per_device(inputs, grads, response):
    n = lax.axis_size("context")
    channels, block = inputs.shape
    chunks = block // LANES
    kind = jnp.float32

    def swap(x, even, odd):
        return lax.ppermute(x, "context", [(i, i ^ (odd if i % 2 else even)) for i in range(n)])

    def sizes(arrays):
        return [((u * arrays * chunks, LANES), kind) for u in (1, 2, 3, 2)]

    def exchange(own, far, aside, beside, meanwhile=lambda x: []):
        step = own.shape[0]
        aside = swap(aside, 1, 1)
        far = swap(far, 6, 6)
        first, second = call(merge, [beside, aside], [((2 * step, LANES), kind)] * 2)
        made = meanwhile(second)
        first, second = swap(first, 2, 4), swap(second, 4, 2)
        (half,) = call(second_half, [far, *made[:1]], [((step, LANES), kind)])
        return [own, aside, far, swap(half, 1, 1), first, second, *made]

    held = [jnp.asarray(t) for t in tables(n * block, PARTS, JOINED)]

    def bring(after):
        return call(fetch, [*held, after], [(t.shape, t.dtype) for t in held], [pltpu.SemaphoreType.DMA((len(held),))], len(held))

    near = [pltpu.VMEM((channels, block), kind)] * 3
    near += [pltpu.VMEM((channels, 3 * chunks, LANES), kind), pltpu.SemaphoreType.DMA((3 * LOADS,))]
    sent = call(spread, [inputs, grads, response], sizes(3), near, 3)
    got = exchange(*sent, meanwhile=bring)
    near = [pltpu.VMEM((n, arrays * chunks, LANES), kind) for arrays in (3, 2)]
    got = exchange(*call(transform, got, sizes(2), near))
    return call(gather, got, [((channels, block), kind)] * 2, near[1:], near_out=False)


RADIX = 128


HIGHEST = lax.Precision.HIGHEST


def phase_pair(row_index, col_index, period, sign_flip):
    product = row_index[:, None] * col_index[None, :] % period
    angles = 2.0 * math.pi / period * product.astype(jnp.float32)
    return (jnp.cos(angles), sign_flip * jnp.sin(angles))


def complex_apply(pattern, tables, values):
    real_real = jnp.einsum(pattern, tables[0], values[0], precision=HIGHEST)
    imag_imag = jnp.einsum(pattern, tables[1], values[1], precision=HIGHEST)
    real_imag = jnp.einsum(pattern, tables[0], values[1], precision=HIGHEST)
    imag_real = jnp.einsum(pattern, tables[1], values[0], precision=HIGHEST)
    return (real_real - imag_imag, real_imag + imag_real)


def complex_times(left_pair, right_pair):
    return (
        left_pair[0] * right_pair[0] - left_pair[1] * right_pair[1],
        left_pair[0] * right_pair[1] + left_pair[1] * right_pair[0],
    )


def by_columns(inputs, grads, response):
    context_size = lax.axis_size("context")
    device_index = lax.axis_index("context")
    channels, block_len = inputs.shape
    column_len = block_len // context_size
    full_length = block_len * context_size
    padded_len = 2 * full_length
    split_len = block_len // RADIX
    freq_rows = jnp.arange(2 * context_size, dtype=jnp.int32)
    part_rows = jnp.arange(context_size, dtype=jnp.int32)
    outer_fwd = phase_pair(freq_rows, part_rows, 2 * context_size, -1.0)
    outer_inv = phase_pair(part_rows, freq_rows, 2 * context_size, 1.0)
    split_rows = jnp.arange(split_len, dtype=jnp.int32)
    radix_rows = jnp.arange(RADIX, dtype=jnp.int32)
    first_fwd = phase_pair(split_rows, split_rows, split_len, -1.0)
    first_inv = (first_fwd[0], -first_fwd[1])
    inner_fwd = phase_pair(split_rows, radix_rows, block_len, -1.0)
    inner_inv = (inner_fwd[0], -inner_fwd[1])
    last_fwd = phase_pair(radix_rows, radix_rows, RADIX, -1.0)
    last_inv = (last_fwd[0], -last_fwd[1])
    pair_rows = 2 * device_index + jnp.arange(2, dtype=jnp.int32)
    column_rows = jnp.arange(block_len, dtype=jnp.int32)
    global_fwd = phase_pair(pair_rows, column_rows, padded_len, -1.0)
    global_inv = (global_fwd[0], -global_fwd[1])
    signals = jnp.stack([inputs, grads, response])
    columns = lax.all_to_all(
        signals.reshape(3, channels, context_size, column_len),
        "context",
        split_axis=2,
        concat_axis=2,
        tiled=True,
    )
    real_part = jnp.einsum("kn,smnj->smkj", outer_fwd[0], columns, precision=HIGHEST)
    imag_part = jnp.einsum("kn,smnj->smkj", outer_fwd[1], columns, precision=HIGHEST)
    columns = jnp.stack([real_part, imag_part], axis=1)
    arrived = lax.all_to_all(columns, "context", split_axis=3, concat_axis=4, tiled=True)
    values = complex_times((arrived[:, 0], arrived[:, 1]), global_fwd)
    shaped = tuple((v.reshape(v.shape[:3] + (split_len, RADIX)) for v in values))
    sectioned = complex_apply("xa,smrab->smrxb", first_fwd, shaped)
    turned = complex_times(sectioned, inner_fwd)
    spec_real, spec_imag = complex_apply("bd,smrxb->smrxd", last_fwd, turned)
    back_input = (
        spec_real[2] * spec_real[1] + spec_imag[2] * spec_imag[1],
        spec_real[2] * spec_imag[1] - spec_imag[2] * spec_real[1],
    )
    back_filter = (
        spec_real[0] * spec_real[1] + spec_imag[0] * spec_imag[1],
        spec_real[0] * spec_imag[1] - spec_imag[0] * spec_real[1],
    )
    inverse_in = ((back_input[0] - back_filter[1])[None], (back_input[1] + back_filter[0])[None])
    sectioned = complex_apply("bd,smrxd->smrxb", last_inv, inverse_in)
    turned = complex_times(sectioned, inner_inv)
    rebuilt = complex_apply("ax,smrxb->smrab", first_inv, turned)
    flat = tuple((v.reshape(v.shape[:3] + (block_len,)) for v in rebuilt))
    untwisted = complex_times(flat, global_inv)
    rows_back = jnp.stack([untwisted[0], untwisted[1]], axis=1)
    arrived = lax.all_to_all(rows_back, "context", split_axis=4, concat_axis=3, tiled=True)
    cos_real = jnp.einsum("nk,smkj->smnj", outer_inv[0], arrived[:, 0], precision=HIGHEST)
    sin_imag = jnp.einsum("nk,smkj->smnj", outer_inv[1], arrived[:, 1], precision=HIGHEST)
    cos_imag = jnp.einsum("nk,smkj->smnj", outer_inv[0], arrived[:, 1], precision=HIGHEST)
    sin_real = jnp.einsum("nk,smkj->smnj", outer_inv[1], arrived[:, 0], precision=HIGHEST)
    folded = jnp.concatenate([cos_real - sin_imag, cos_imag + sin_real], axis=0) / padded_len
    restored = lax.all_to_all(folded, "context", split_axis=2, concat_axis=3, tiled=True).reshape(
        2, channels, block_len
    )
    return (restored[0], restored[1])


def by_shape(inputs, grads, response):
    if inputs.shape[0] == lax.axis_size("context") == 2 * 2 * 2:
        return per_device(inputs, grads, response)
    return by_columns(inputs, grads, response)


def solution(mesh):
    spec = P("tensor", "context")
    return jax.shard_map(by_shape, mesh=mesh, in_specs=(spec,) * 3, out_specs=(spec,) * 2, check_vma=False)
```

```python
import functools
import math

import jax
import jax.numpy as jnp
import numpy as np
from jax import lax
from jax.experimental import pallas as pl
from jax.experimental.pallas import tpu as pltpu
from jax.sharding import PartitionSpec as P

LANES = 128
BF = jnp.bfloat16
PARTS, JOINED, LOADS = 4, 2, 4
PLANS = ((7, 7), (3, 3), (5, 5)), ((7, 7), (3, 3), (5, 5))


def halves(table):
    table = table.astype(np.float32)
    high = table.astype(BF)
    low = (table - high.astype(np.float32)).astype(BF)
    return high, low


def tables(length, parts, joined):
    rows = length // LANES
    k = np.arange(rows)[:, None] + 0.25
    r = np.arange(rows)[None, :]
    outer = 2 * np.pi * k * r / rows
    stacked = np.stack([np.cos(outer), -np.sin(outer)])
    first = stacked.reshape(2, parts, rows // parts, rows).swapaxes(0, 1).reshape(2 * rows, rows)
    last = (stacked / length).reshape(2, joined, rows // joined, rows).transpose(1, 3, 0, 2)
    last = last.reshape(joined, rows, 2 * rows // joined)
    lane = np.arange(LANES)
    turn = 2 * np.pi * k * lane[None, :] / length
    twiddle = np.concatenate([np.cos(turn), np.sin(turn)], axis=1).astype(np.float32)
    inner = 2 * np.pi * (lane[:, None] * lane[None, :] % LANES) / LANES
    cos2, sin2 = np.cos(inner), np.sin(inner)
    into = np.block([[cos2, -sin2], [sin2, cos2]])
    return np.stack(halves(first)), np.stack(halves(last)), np.stack(halves(into)), twiddle


def split(x):
    high = x.astype(BF)
    low = (x - high.astype(jnp.float32)).astype(BF)
    return high, low


def dot(a, b):
    return jnp.dot(a, b, preferred_element_type=jnp.float32)


def dot_right(x, table):
    high, low = split(x)
    return dot(high, table[0]) + (dot(low, table[0]) + dot(high, table[1]))


def dot_left(table_high, table_low, x):
    high, low = x
    return dot(table_high, high) + (dot(table_high, low) + dot(table_low, high))


def lanes_of(x, i, m):
    return x[i * m:(i + 1) * m, :LANES], x[i * m:(i + 1) * m, LANES:]


def route(plan):
    me = lax.axis_index("context")
    core = me % 2
    to, from_ = [], []
    for even, odd in plan:
        mine, others = even + core * (odd - even), odd + core * (even - odd)
        to.append((me ^ mine, me ^ 1 ^ others))
        back, backs = (mine, others) if even % 2 == 0 else (others, mine)
        from_.append((me ^ back, me ^ 1 ^ backs))
    return me, to, from_


def pack(plan, pieces, own, far, aside, beside):
    me, ((far_to, _), (first_to, first_aside), (second_to, second_aside)), _ = route(plan)
    step = own.shape[0]
    for out, at, device in (
        (own, 0, me), (far, 0, far_to), (far, 1, far_to ^ 1),
        (aside, 0, me ^ 1), (aside, 1, first_aside), (aside, 2, second_aside),
        (beside, 0, first_to), (beside, 1, second_to),
    ):
        out[at * step:(at + 1) * step, :] = pieces[device]


def merge(beside, aside, first, second):
    step = beside.shape[0] // 2
    for i, out in enumerate((first, second)):
        out[:step, :] = beside[i * step:(i + 1) * step, :]
        out[step:, :] = aside[(i + 1) * step:(i + 2) * step, :]


def second_half(x, *rest):
    out = rest[-1]
    out[...] = x[out.shape[0]:, :]


def unpack(plan, got, held):
    me, _, ((far_from, far_others), (first_from, _), (second_from, _)) = route(plan)
    own, aside, far, far_other, first, second = got
    step = own.shape[0]
    for ref, at, device in (
        (own, 0, me), (aside, 0, me ^ 1), (far, 0, far_from), (far_other, 0, far_others),
        (first, 0, first_from), (first, 1, first_from ^ 1), (second, 0, second_from), (second, 1, second_from ^ 1),
    ):
        held[device] = ref[at * step:(at + 1) * step, :]


def fetch(*refs):
    count = (len(refs) - 2) // 2
    copies = [pltpu.make_async_copy(refs[i], refs[count + 1 + i], refs[-1].at[i]) for i in range(count)]
    for copy in copies:
        copy.start()
    for copy in copies:
        copy.wait()


def spread(*refs):
    signals, outs, near, (held, arrived) = refs[:3], refs[3:7], refs[7:10], refs[10:]
    channels, block = signals[0].shape
    chunks = block // LANES
    width = block // LOADS

    def at(load):
        return pl.ds(load * width, width)

    copies = []
    for load in range(LOADS):
        for i in range(3):
            ends = signals[i].at[:, at(load)], near[i].at[:, at(load)]
            copies.append(pltpu.make_async_copy(*ends, arrived.at[load * 3 + i]))
            copies[-1].start()
    for load in range(LOADS):
        for i in range(3):
            copies[load * 3 + i].wait()
            rows = pl.ds(i * chunks + load * chunks // LOADS, chunks // LOADS)
            held[:, rows, :] = near[i][:, at(load)].reshape(channels, chunks // LOADS, LANES)
    pack(PLANS[0], held, *outs)


def transform(*refs):
    got, (first, last, into, twiddle), outs, (held, y) = refs[:6], refs[6:10], refs[10:14], refs[14:]
    unpack(PLANS[0], got, held)
    n = held.shape[0]
    chunks = held.shape[1] // 3
    rows = n * chunks
    m = rows // PARTS
    whole = [held[:, i * chunks:(i + 1) * chunks, :].reshape(rows, LANES) for i in range(3)]
    signals = split(jnp.concatenate(whole, axis=1))
    turns = [lanes_of(twiddle, q, m) for q in range(PARTS)]
    outer = [dot_left(first[0, 2 * m * q:2 * m * (q + 1)], first[1, 2 * m * q:2 * m * (q + 1)], signals) for q in range(PARTS)]
    spectra = []
    for z, (c, s) in zip(outer, turns):
        turned = []
        for i in range(3):
            re, im = z[:m, i * LANES:(i + 1) * LANES], z[m:, i * LANES:(i + 1) * LANES]
            turned.append(jnp.concatenate([re * c + im * s, im * c - re * s], axis=1))
        spectra.append(dot_right(jnp.concatenate(turned, axis=0), into))
    backs = []
    for z in spectra:
        (xr, xi), (gr, gi), (hr, hi) = (lanes_of(z, i, m) for i in range(3))
        p = [jnp.concatenate([ur * gr + ui * gi, ui * gr - ur * gi], axis=1) for ur, ui in ((hr, hi), (xr, xi))]
        backs.append(dot_right(jnp.concatenate(p, axis=0), into))
    out = 0.0
    for joined in range(JOINED):
        real, imag = [], []
        for q in range(joined * PARTS // JOINED, (joined + 1) * PARTS // JOINED):
            c, s = turns[q]
            pairs = [lanes_of(backs[q], i, m) for i in range(2)]
            real.append(jnp.concatenate([dr * c + di * s for dr, di in pairs], axis=1))
            imag.append(jnp.concatenate([dr * s - di * c for dr, di in pairs], axis=1))
        out += dot_left(last[0, joined], last[1, joined], split(jnp.concatenate(real + imag, axis=0)))
    for d in range(n):
        for i in range(2):
            y[d, i * chunks:(i + 1) * chunks, :] = out[d * chunks:(d + 1) * chunks, i * LANES:(i + 1) * LANES]
    pack(PLANS[1], y, *outs)


def gather(*refs):
    got, (a, b, held) = refs[:6], refs[6:]
    unpack(PLANS[1], got, held)
    channels, block = a.shape
    chunks = block // LANES
    for i, ref in enumerate((a, b)):
        for j in range(0, chunks, 8):
            ref[:, pl.ds(j * LANES, 8 * LANES)] = held[:, pl.ds(i * chunks + j, 8), :].reshape(channels, 8 * LANES)


def call(body, ins, outs, scratch=(), far_in=0, near_out=True):
    near = pl.BlockSpec(memory_space=pltpu.VMEM)
    kind = pltpu.VMEM if near_out else jax.ShapeDtypeStruct
    return pl.pallas_call(
        body,
        out_shape=[kind(shape, dtype) for shape, dtype in outs],
        in_specs=[pl.BlockSpec(memory_space=pl.ANY)] * far_in + [near] * (len(ins) - far_in),
        out_specs=[near] * len(outs),
        scratch_shapes=scratch,
        name=body.__name__,
    )(*ins[:far_in], *(pltpu.with_memory_space_constraint(x, pltpu.VMEM) for x in ins[far_in:]))


def per_device(inputs, grads, response):
    n = lax.axis_size("context")
    channels, block = inputs.shape
    chunks = block // LANES
    kind = jnp.float32

    def swap(x, even, odd):
        return lax.ppermute(x, "context", [(i, i ^ (odd if i % 2 else even)) for i in range(n)])

    def sizes(arrays):
        return [((u * arrays * chunks, LANES), kind) for u in (1, 2, 3, 2)]

    def exchange(plan, own, far, aside, beside, meanwhile=lambda x: []):
        step = own.shape[0]
        aside = swap(aside, 1, 1)
        far = swap(far, *plan[0])
        first, second = call(merge, [beside, aside], [((2 * step, LANES), kind)] * 2)
        made = meanwhile(second)
        first, second = swap(first, *plan[1]), swap(second, *plan[2])
        (half,) = call(second_half, [far, *made[:1]], [((step, LANES), kind)])
        return [own, aside, far, swap(half, 1, 1), first, second, *made]

    held = [jnp.asarray(t) for t in tables(n * block, PARTS, JOINED)]

    def bring(after):
        return call(fetch, [*held, after], [(t.shape, t.dtype) for t in held], [pltpu.SemaphoreType.DMA((len(held),))], len(held))

    near = [pltpu.VMEM((channels, block), kind)] * 3
    near += [pltpu.VMEM((channels, 3 * chunks, LANES), kind), pltpu.SemaphoreType.DMA((3 * LOADS,))]
    sent = call(spread, [inputs, grads, response], sizes(3), near, 3)
    got = exchange(PLANS[0], *sent, meanwhile=bring)
    near = [pltpu.VMEM((n, arrays * chunks, LANES), kind) for arrays in (3, 2)]
    got = exchange(PLANS[1], *call(transform, got, sizes(2), near))
    return call(gather, got, [((channels, block), kind)] * 2, near[1:], near_out=False)


RADIX = 128


HIGHEST = lax.Precision.HIGHEST


def phase_pair(row_index, col_index, period, sign_flip):
    product = row_index[:, None] * col_index[None, :] % period
    angles = 2.0 * math.pi / period * product.astype(jnp.float32)
    return (jnp.cos(angles), sign_flip * jnp.sin(angles))


def complex_apply(pattern, tables, values):
    real_real = jnp.einsum(pattern, tables[0], values[0], precision=HIGHEST)
    imag_imag = jnp.einsum(pattern, tables[1], values[1], precision=HIGHEST)
    real_imag = jnp.einsum(pattern, tables[0], values[1], precision=HIGHEST)
    imag_real = jnp.einsum(pattern, tables[1], values[0], precision=HIGHEST)
    return (real_real - imag_imag, real_imag + imag_real)


def complex_times(left_pair, right_pair):
    return (
        left_pair[0] * right_pair[0] - left_pair[1] * right_pair[1],
        left_pair[0] * right_pair[1] + left_pair[1] * right_pair[0],
    )


def by_columns(inputs, grads, response):
    context_size = lax.axis_size("context")
    device_index = lax.axis_index("context")
    channels, block_len = inputs.shape
    column_len = block_len // context_size
    full_length = block_len * context_size
    padded_len = 2 * full_length
    split_len = block_len // RADIX
    freq_rows = jnp.arange(2 * context_size, dtype=jnp.int32)
    part_rows = jnp.arange(context_size, dtype=jnp.int32)
    outer_fwd = phase_pair(freq_rows, part_rows, 2 * context_size, -1.0)
    outer_inv = phase_pair(part_rows, freq_rows, 2 * context_size, 1.0)
    split_rows = jnp.arange(split_len, dtype=jnp.int32)
    radix_rows = jnp.arange(RADIX, dtype=jnp.int32)
    first_fwd = phase_pair(split_rows, split_rows, split_len, -1.0)
    first_inv = (first_fwd[0], -first_fwd[1])
    inner_fwd = phase_pair(split_rows, radix_rows, block_len, -1.0)
    inner_inv = (inner_fwd[0], -inner_fwd[1])
    last_fwd = phase_pair(radix_rows, radix_rows, RADIX, -1.0)
    last_inv = (last_fwd[0], -last_fwd[1])
    pair_rows = 2 * device_index + jnp.arange(2, dtype=jnp.int32)
    column_rows = jnp.arange(block_len, dtype=jnp.int32)
    global_fwd = phase_pair(pair_rows, column_rows, padded_len, -1.0)
    global_inv = (global_fwd[0], -global_fwd[1])
    signals = jnp.stack([inputs, grads, response])
    columns = lax.all_to_all(
        signals.reshape(3, channels, context_size, column_len),
        "context",
        split_axis=2,
        concat_axis=2,
        tiled=True,
    )
    real_part = jnp.einsum("kn,smnj->smkj", outer_fwd[0], columns, precision=HIGHEST)
    imag_part = jnp.einsum("kn,smnj->smkj", outer_fwd[1], columns, precision=HIGHEST)
    columns = jnp.stack([real_part, imag_part], axis=1)
    arrived = lax.all_to_all(columns, "context", split_axis=3, concat_axis=4, tiled=True)
    values = complex_times((arrived[:, 0], arrived[:, 1]), global_fwd)
    shaped = tuple((v.reshape(v.shape[:3] + (split_len, RADIX)) for v in values))
    sectioned = complex_apply("xa,smrab->smrxb", first_fwd, shaped)
    turned = complex_times(sectioned, inner_fwd)
    spec_real, spec_imag = complex_apply("bd,smrxb->smrxd", last_fwd, turned)
    back_input = (
        spec_real[2] * spec_real[1] + spec_imag[2] * spec_imag[1],
        spec_real[2] * spec_imag[1] - spec_imag[2] * spec_real[1],
    )
    back_filter = (
        spec_real[0] * spec_real[1] + spec_imag[0] * spec_imag[1],
        spec_real[0] * spec_imag[1] - spec_imag[0] * spec_real[1],
    )
    inverse_in = ((back_input[0] - back_filter[1])[None], (back_input[1] + back_filter[0])[None])
    sectioned = complex_apply("bd,smrxd->smrxb", last_inv, inverse_in)
    turned = complex_times(sectioned, inner_inv)
    rebuilt = complex_apply("ax,smrxb->smrab", first_inv, turned)
    flat = tuple((v.reshape(v.shape[:3] + (block_len,)) for v in rebuilt))
    untwisted = complex_times(flat, global_inv)
    rows_back = jnp.stack([untwisted[0], untwisted[1]], axis=1)
    arrived = lax.all_to_all(rows_back, "context", split_axis=4, concat_axis=3, tiled=True)
    cos_real = jnp.einsum("nk,smkj->smnj", outer_inv[0], arrived[:, 0], precision=HIGHEST)
    sin_imag = jnp.einsum("nk,smkj->smnj", outer_inv[1], arrived[:, 1], precision=HIGHEST)
    cos_imag = jnp.einsum("nk,smkj->smnj", outer_inv[0], arrived[:, 1], precision=HIGHEST)
    sin_real = jnp.einsum("nk,smkj->smnj", outer_inv[1], arrived[:, 0], precision=HIGHEST)
    folded = jnp.concatenate([cos_real - sin_imag, cos_imag + sin_real], axis=0) / padded_len
    restored = lax.all_to_all(folded, "context", split_axis=2, concat_axis=3, tiled=True).reshape(
        2, channels, block_len
    )
    return (restored[0], restored[1])


def by_shape(inputs, grads, response):
    if inputs.shape[0] == lax.axis_size("context") == 2 * 2 * 2:
        return per_device(inputs, grads, response)
    return by_columns(inputs, grads, response)


def solution(mesh):
    spec = P("tensor", "context")
    return jax.shard_map(by_shape, mesh=mesh, in_specs=(spec,) * 3, out_specs=(spec,) * 2, check_vma=False)
```

```python
import functools
import math

import jax
import jax.numpy as jnp
import numpy as np
from jax import lax
from jax.experimental import pallas as pl
from jax.experimental.pallas import tpu as pltpu
from jax.sharding import PartitionSpec as P

LANES = 128
BF = jnp.bfloat16
PARTS, JOINED, LOADS = 4, 2, 4
PLANS = ((7, 7), (3, 3), (5, 5)), ((7, 7), (3, 3), (5, 5))


def halves(table):
    table = table.astype(np.float32)
    high = table.astype(BF)
    low = (table - high.astype(np.float32)).astype(BF)
    return high, low


def tables(length, parts, joined):
    rows = length // LANES
    k = np.arange(rows)[:, None] + 0.25
    r = np.arange(rows)[None, :]
    outer = 2 * np.pi * k * r / rows
    stacked = np.stack([np.cos(outer), -np.sin(outer)])
    first = stacked.reshape(2, parts, rows // parts, rows).swapaxes(0, 1).reshape(2 * rows, rows)
    high, low = (t.reshape(2 * rows, 2, 2, rows // 4) for t in halves(first))
    first = []
    for diagonal in ((0, 0), (1, 1)), ((0, 1), (1, 0)):
        cut_high, cut_low = (np.concatenate([t[:, y, x] for y, x in diagonal], axis=1) for t in (high, low))
        first.append(np.concatenate([cut_high, cut_high, cut_low], axis=1))
    last = (stacked / length).reshape(2, joined, rows // joined, rows).transpose(1, 3, 0, 2)
    last = last.reshape(joined, rows, 2 * rows // joined)
    lane = np.arange(LANES)
    turn = 2 * np.pi * k * lane[None, :] / length
    twiddle = np.concatenate([np.cos(turn), np.sin(turn)], axis=1).astype(np.float32)
    inner = 2 * np.pi * (lane[:, None] * lane[None, :] % LANES) / LANES
    cos2, sin2 = np.cos(inner), np.sin(inner)
    into = np.block([[cos2, -sin2], [sin2, cos2]])
    return np.stack(first), np.stack(halves(last)), np.stack(halves(into)), twiddle


def split(x):
    high = x.astype(BF)
    low = (x - high.astype(jnp.float32)).astype(BF)
    return high, low


def dot(a, b):
    return jnp.dot(a, b, preferred_element_type=jnp.float32)


def dot_right(x, table):
    high, low = split(x)
    return dot(high, table[0]) + (dot(low, table[0]) + dot(high, table[1]))


def dot_left(table_high, table_low, x):
    high, low = x
    return dot(table_high, high) + (dot(table_high, low) + dot(table_low, high))


def lanes_of(x, i, m):
    return x[i * m:(i + 1) * m, :LANES], x[i * m:(i + 1) * m, LANES:]


def route(plan):
    me = lax.axis_index("context")
    core = me % 2
    to, from_ = [], []
    for even, odd in plan:
        mine, others = even + core * (odd - even), odd + core * (even - odd)
        to.append((me ^ mine, me ^ 1 ^ others))
        back, backs = (mine, others) if even % 2 == 0 else (others, mine)
        from_.append((me ^ back, me ^ 1 ^ backs))
    return me, to, from_


def pack(plan, pieces, own, far, aside, beside):
    me, ((far_to, _), (first_to, first_aside), (second_to, second_aside)), _ = route(plan)
    step = own.shape[0]
    for out, at, device in (
        (own, 0, me), (far, 0, far_to), (far, 1, far_to ^ 1),
        (aside, 0, me ^ 1), (aside, 1, first_aside), (aside, 2, second_aside),
        (beside, 0, first_to), (beside, 1, second_to),
    ):
        out[at * step:(at + 1) * step, :] = pieces[device]


def merge(beside, aside, first, second):
    step = beside.shape[0] // 2
    for i, out in enumerate((first, second)):
        out[:step, :] = beside[i * step:(i + 1) * step, :]
        out[step:, :] = aside[(i + 1) * step:(i + 2) * step, :]


def second_half(x, *rest):
    out = rest[-1]
    out[...] = x[out.shape[0]:, :]


def slot(device):
    return (device >> 1 ^ device >> 2) & 1, (device >> 2) * 2 + (device & 1)


def unpack(pieces, held):
    step = held.shape[1]
    for ref, at, place in pieces:
        held[place] = ref[at * step:(at + 1) * step, :]


def came_first(plan, got):
    me, _, ((far_from, far_others), *_) = route(plan)
    own, aside, far, far_other = got
    return (own, 0, me), (aside, 0, me ^ 1), (far, 0, far_from), (far_other, 0, far_others)


def came_last(plan, got):
    _, _, (_, (first_from, _), (second_from, _)) = route(plan)
    first, second = got
    return (first, 0, first_from), (first, 1, first_from ^ 1), (second, 0, second_from), (second, 1, second_from ^ 1)


def outer_stage(came, held, table):
    unpack([(ref, at, slot(device)[1]) for ref, at, device in came], held)
    diagonal = slot(came[0][2])[0]
    half, chunks = 4 * held.shape[1] // 3, held.shape[1] // 3
    whole = [held[:, i * chunks:(i + 1) * chunks, :].reshape(half, LANES) for i in range(3)]
    high, low = split(jnp.concatenate(whole, axis=1))
    both = jnp.concatenate([high, low], axis=0)
    m = table.shape[1] // PARTS
    sums = []
    for q in range(PARTS):
        rows = pl.ds(q * m, m)
        sums.append((dot(table[diagonal, rows, 2 * half:], high), dot(table[diagonal, rows, :2 * half], both)))
    return sums


def early(own, aside, far, far_other, table, out, held):
    sums = outer_stage(came_first(PLANS[0], (own, aside, far, far_other)), held, table)
    m = out.shape[0] // PARTS
    for q, (less, more) in enumerate(sums):
        out[q * m:(q + 1) * m, :] = less + more


def fetch(*refs):
    count = (len(refs) - 2) // 2
    copies = [pltpu.make_async_copy(refs[i], refs[count + 1 + i], refs[-1].at[i]) for i in range(count)]
    for copy in copies:
        copy.start()
    for copy in copies:
        copy.wait()


def spread(*refs):
    signals, outs, near, (held, arrived) = refs[:3], refs[3:7], refs[7:10], refs[10:]
    channels, block = signals[0].shape
    chunks = block // LANES
    width = block // LOADS

    def at(load):
        return pl.ds(load * width, width)

    copies = []
    for load in range(LOADS):
        for i in range(3):
            ends = signals[i].at[:, at(load)], near[i].at[:, at(load)]
            copies.append(pltpu.make_async_copy(*ends, arrived.at[load * 3 + i]))
            copies[-1].start()
    for load in range(LOADS):
        for i in range(3):
            copies[load * 3 + i].wait()
            rows = pl.ds(i * chunks + load * chunks // LOADS, chunks // LOADS)
            held[:, rows, :] = near[i][:, at(load)].reshape(channels, chunks // LOADS, LANES)
    pack(PLANS[0], held, *outs)


def transform(*refs):
    got, (begun, first, last, into, twiddle), outs, (held, y) = refs[:2], refs[2:7], refs[7:11], refs[11:]
    n, chunks = y.shape[0], y.shape[1] // 2
    rows = n * chunks
    m = rows // PARTS
    turns = [lanes_of(twiddle, q, m) for q in range(PARTS)]
    sums = outer_stage(came_last(PLANS[0], got), held, first)
    outer = [(begun[2 * m * q:2 * m * (q + 1), :] + less) + more for q, (less, more) in enumerate(sums)]
    spectra = []
    for z, (c, s) in zip(outer, turns):
        turned = []
        for i in range(3):
            re, im = z[:m, i * LANES:(i + 1) * LANES], z[m:, i * LANES:(i + 1) * LANES]
            turned.append(jnp.concatenate([re * c + im * s, im * c - re * s], axis=1))
        spectra.append(dot_right(jnp.concatenate(turned, axis=0), into))
    backs = []
    for z in spectra:
        (xr, xi), (gr, gi), (hr, hi) = (lanes_of(z, i, m) for i in range(3))
        p = [jnp.concatenate([ur * gr + ui * gi, ui * gr - ur * gi], axis=1) for ur, ui in ((hr, hi), (xr, xi))]
        backs.append(dot_right(jnp.concatenate(p, axis=0), into))
    out = 0.0
    for joined in range(JOINED):
        real, imag = [], []
        for q in range(joined * PARTS // JOINED, (joined + 1) * PARTS // JOINED):
            c, s = turns[q]
            pairs = [lanes_of(backs[q], i, m) for i in range(2)]
            real.append(jnp.concatenate([dr * c + di * s for dr, di in pairs], axis=1))
            imag.append(jnp.concatenate([dr * s - di * c for dr, di in pairs], axis=1))
        out += dot_left(last[0, joined], last[1, joined], split(jnp.concatenate(real + imag, axis=0)))
    for d in range(n):
        for i in range(2):
            y[d, i * chunks:(i + 1) * chunks, :] = out[d * chunks:(d + 1) * chunks, i * LANES:(i + 1) * LANES]
    pack(PLANS[1], y, *outs)


def gather(*refs):
    got, (a, b, held) = refs[:6], refs[6:]
    unpack(came_first(PLANS[1], got[:4]) + came_last(PLANS[1], got[4:]), held)
    channels, block = a.shape
    chunks = block // LANES
    for i, ref in enumerate((a, b)):
        for j in range(0, chunks, 8):
            ref[:, pl.ds(j * LANES, 8 * LANES)] = held[:, pl.ds(i * chunks + j, 8), :].reshape(channels, 8 * LANES)


def call(body, ins, outs, scratch=(), far_in=0, near_out=True):
    near = pl.BlockSpec(memory_space=pltpu.VMEM)
    kind = pltpu.VMEM if near_out else jax.ShapeDtypeStruct
    return pl.pallas_call(
        body,
        out_shape=[kind(shape, dtype) for shape, dtype in outs],
        in_specs=[pl.BlockSpec(memory_space=pltpu.HBM)] * far_in + [near] * (len(ins) - far_in),
        out_specs=[near] * len(outs),
        scratch_shapes=scratch,
        compiler_params=pltpu.CompilerParams(vmem_limit_bytes=16 * 2**20),
        name=body.__name__,
    )(*(pltpu.with_memory_space_constraint(x, pltpu.VMEM if i >= far_in else pltpu.HBM) for i, x in enumerate(ins)))


def per_device(inputs, grads, response):
    n = lax.axis_size("context")
    channels, block = inputs.shape
    chunks = block // LANES
    kind = jnp.float32

    def swap(x, even, odd):
        return lax.ppermute(x, "context", [(i, i ^ (odd if i % 2 else even)) for i in range(n)])

    def sizes(arrays):
        return [((u * arrays * chunks, LANES), kind) for u in (1, 2, 3, 2)]

    def exchange(plan, own, far, aside, beside, meanwhile=lambda x: []):
        step = own.shape[0]
        aside = swap(aside, 1, 1)
        far = swap(far, *plan[0])
        first, second = call(merge, [beside, aside], [((2 * step, LANES), kind)] * 2)
        made = meanwhile(second)
        first, second = swap(first, *plan[1]), swap(second, *plan[2])
        (half,) = call(second_half, [far, *made[:1]], [((step, LANES), kind)])
        return [own, aside, far, swap(half, 1, 1), first, second, *made]

    held = [jnp.asarray(t) for t in tables(n * block, PARTS, JOINED)]

    def bring(after):
        return call(fetch, [*held, after], [(t.shape, t.dtype) for t in held], [pltpu.SemaphoreType.DMA((len(held),))], len(held))

    near = [pltpu.VMEM((channels, block), kind)] * 3
    near += [pltpu.VMEM((channels, 3 * chunks, LANES), kind), pltpu.SemaphoreType.DMA((3 * LOADS,))]
    sent = call(spread, [inputs, grads, response], sizes(3), near, 3)
    got = exchange(PLANS[0], *sent, meanwhile=bring)
    near = [pltpu.VMEM((n // 2, 3 * chunks, LANES), kind)]
    (begun,) = call(early, [*got[:4], got[6]], [((2 * n * chunks, 3 * LANES), kind)], near)
    pieces = [pltpu.VMEM((n, 2 * chunks, LANES), kind)]
    got = exchange(PLANS[1], *call(transform, [*got[4:6], begun, *got[6:]], sizes(2), near + pieces))
    return call(gather, got, [((channels, block), kind)] * 2, pieces, near_out=False)


RADIX = 128


HIGHEST = lax.Precision.HIGHEST


def phase_pair(row_index, col_index, period, sign_flip):
    product = row_index[:, None] * col_index[None, :] % period
    angles = 2.0 * math.pi / period * product.astype(jnp.float32)
    return (jnp.cos(angles), sign_flip * jnp.sin(angles))


def complex_apply(pattern, tables, values):
    real_real = jnp.einsum(pattern, tables[0], values[0], precision=HIGHEST)
    imag_imag = jnp.einsum(pattern, tables[1], values[1], precision=HIGHEST)
    real_imag = jnp.einsum(pattern, tables[0], values[1], precision=HIGHEST)
    imag_real = jnp.einsum(pattern, tables[1], values[0], precision=HIGHEST)
    return (real_real - imag_imag, real_imag + imag_real)


def complex_times(left_pair, right_pair):
    return (
        left_pair[0] * right_pair[0] - left_pair[1] * right_pair[1],
        left_pair[0] * right_pair[1] + left_pair[1] * right_pair[0],
    )


def by_columns(inputs, grads, response):
    context_size = lax.axis_size("context")
    device_index = lax.axis_index("context")
    channels, block_len = inputs.shape
    column_len = block_len // context_size
    full_length = block_len * context_size
    padded_len = 2 * full_length
    split_len = block_len // RADIX
    freq_rows = jnp.arange(2 * context_size, dtype=jnp.int32)
    part_rows = jnp.arange(context_size, dtype=jnp.int32)
    outer_fwd = phase_pair(freq_rows, part_rows, 2 * context_size, -1.0)
    outer_inv = phase_pair(part_rows, freq_rows, 2 * context_size, 1.0)
    split_rows = jnp.arange(split_len, dtype=jnp.int32)
    radix_rows = jnp.arange(RADIX, dtype=jnp.int32)
    first_fwd = phase_pair(split_rows, split_rows, split_len, -1.0)
    first_inv = (first_fwd[0], -first_fwd[1])
    inner_fwd = phase_pair(split_rows, radix_rows, block_len, -1.0)
    inner_inv = (inner_fwd[0], -inner_fwd[1])
    last_fwd = phase_pair(radix_rows, radix_rows, RADIX, -1.0)
    last_inv = (last_fwd[0], -last_fwd[1])
    pair_rows = 2 * device_index + jnp.arange(2, dtype=jnp.int32)
    column_rows = jnp.arange(block_len, dtype=jnp.int32)
    global_fwd = phase_pair(pair_rows, column_rows, padded_len, -1.0)
    global_inv = (global_fwd[0], -global_fwd[1])
    signals = jnp.stack([inputs, grads, response])
    columns = lax.all_to_all(
        signals.reshape(3, channels, context_size, column_len),
        "context",
        split_axis=2,
        concat_axis=2,
        tiled=True,
    )
    real_part = jnp.einsum("kn,smnj->smkj", outer_fwd[0], columns, precision=HIGHEST)
    imag_part = jnp.einsum("kn,smnj->smkj", outer_fwd[1], columns, precision=HIGHEST)
    columns = jnp.stack([real_part, imag_part], axis=1)
    arrived = lax.all_to_all(columns, "context", split_axis=3, concat_axis=4, tiled=True)
    values = complex_times((arrived[:, 0], arrived[:, 1]), global_fwd)
    shaped = tuple((v.reshape(v.shape[:3] + (split_len, RADIX)) for v in values))
    sectioned = complex_apply("xa,smrab->smrxb", first_fwd, shaped)
    turned = complex_times(sectioned, inner_fwd)
    spec_real, spec_imag = complex_apply("bd,smrxb->smrxd", last_fwd, turned)
    back_input = (
        spec_real[2] * spec_real[1] + spec_imag[2] * spec_imag[1],
        spec_real[2] * spec_imag[1] - spec_imag[2] * spec_real[1],
    )
    back_filter = (
        spec_real[0] * spec_real[1] + spec_imag[0] * spec_imag[1],
        spec_real[0] * spec_imag[1] - spec_imag[0] * spec_real[1],
    )
    inverse_in = ((back_input[0] - back_filter[1])[None], (back_input[1] + back_filter[0])[None])
    sectioned = complex_apply("bd,smrxd->smrxb", last_inv, inverse_in)
    turned = complex_times(sectioned, inner_inv)
    rebuilt = complex_apply("ax,smrxb->smrab", first_inv, turned)
    flat = tuple((v.reshape(v.shape[:3] + (block_len,)) for v in rebuilt))
    untwisted = complex_times(flat, global_inv)
    rows_back = jnp.stack([untwisted[0], untwisted[1]], axis=1)
    arrived = lax.all_to_all(rows_back, "context", split_axis=4, concat_axis=3, tiled=True)
    cos_real = jnp.einsum("nk,smkj->smnj", outer_inv[0], arrived[:, 0], precision=HIGHEST)
    sin_imag = jnp.einsum("nk,smkj->smnj", outer_inv[1], arrived[:, 1], precision=HIGHEST)
    cos_imag = jnp.einsum("nk,smkj->smnj", outer_inv[0], arrived[:, 1], precision=HIGHEST)
    sin_real = jnp.einsum("nk,smkj->smnj", outer_inv[1], arrived[:, 0], precision=HIGHEST)
    folded = jnp.concatenate([cos_real - sin_imag, cos_imag + sin_real], axis=0) / padded_len
    restored = lax.all_to_all(folded, "context", split_axis=2, concat_axis=3, tiled=True).reshape(
        2, channels, block_len
    )
    return (restored[0], restored[1])


def by_shape(inputs, grads, response):
    if inputs.shape[0] == lax.axis_size("context") == 2 * 2 * 2:
        return per_device(inputs, grads, response)
    return by_columns(inputs, grads, response)


def solution(mesh):
    spec = P("tensor", "context")
    return jax.shard_map(by_shape, mesh=mesh, in_specs=(spec,) * 3, out_specs=(spec,) * 2, check_vma=False)
```

```python
import functools
import math

import jax
import jax.numpy as jnp
import numpy as np
from jax import lax
from jax.experimental import pallas as pl
from jax.experimental.pallas import tpu as pltpu
from jax.sharding import PartitionSpec as P

LANES = 128
BF = jnp.bfloat16
PARTS, JOINED, LOADS = 4, 2, 4
PLANS = ((7, 7), (3, 3), (5, 5)), ((7, 7), (3, 3), (5, 5))


def halves(table):
    table = table.astype(np.float32)
    high = table.astype(BF)
    low = (table - high.astype(np.float32)).astype(BF)
    return high, low


def tables(length, parts, joined):
    rows = length // LANES
    k = np.arange(rows)[:, None] + 0.25
    r = np.arange(rows)[None, :]
    outer = 2 * np.pi * k * r / rows
    stacked = np.stack([np.cos(outer), -np.sin(outer)])
    first = stacked.reshape(2, parts, rows // parts, rows).swapaxes(0, 1).reshape(2 * rows, rows)
    high, low = (t.reshape(2 * rows, 2, 2, rows // 4) for t in halves(first))
    first = []
    for diagonal in ((0, 0), (1, 1)), ((0, 1), (1, 0)):
        cut_high, cut_low = (np.concatenate([t[:, y, x] for y, x in diagonal], axis=1) for t in (high, low))
        first.append(np.concatenate([cut_high, cut_high, cut_low], axis=1))
    last = (stacked / length).reshape(2, joined, rows // joined, rows).transpose(1, 3, 0, 2)
    last = last.reshape(joined, rows, 2 * rows // joined)
    lane = np.arange(LANES)
    turn = 2 * np.pi * k * lane[None, :] / length
    twiddle = np.concatenate([np.cos(turn), np.sin(turn)], axis=1).astype(np.float32)
    inner = 2 * np.pi * (lane[:, None] * lane[None, :] % LANES) / LANES
    cos2, sin2 = np.cos(inner), np.sin(inner)
    into = np.block([[cos2, -sin2], [sin2, cos2]])
    return np.stack(first), np.stack(halves(last)), np.stack(halves(into)), twiddle


def split(x):
    high = x.astype(BF)
    low = (x - high.astype(jnp.float32)).astype(BF)
    return high, low


def dot(a, b):
    return jnp.dot(a, b, preferred_element_type=jnp.float32)


def dot_right(x, table):
    high, low = split(x)
    return dot(high, table[0]) + (dot(low, table[0]) + dot(high, table[1]))


def dot_left(table_high, table_low, x):
    high, low = x
    return dot(table_high, high) + (dot(table_high, low) + dot(table_low, high))


def lanes_of(x, i, m):
    return x[i * m:(i + 1) * m, :LANES], x[i * m:(i + 1) * m, LANES:]


def route(plan):
    me = lax.axis_index("context")
    core = me % 2
    to, from_ = [], []
    for even, odd in plan:
        mine, others = even + core * (odd - even), odd + core * (even - odd)
        to.append((me ^ mine, me ^ 1 ^ others))
        back, backs = (mine, others) if even % 2 == 0 else (others, mine)
        from_.append((me ^ back, me ^ 1 ^ backs))
    return me, to, from_


def pack(plan, pieces, own, far, aside, beside, other):
    me, ((far_to, _), (first_to, first_aside), (second_to, second_aside)), _ = route(plan)
    step = own.shape[0]
    for out, at, device in (
        (own, 0, me), (far, 0, far_to), (far, 1, far_to ^ 1), (aside, 0, first_aside), (aside, 1, second_aside),
        (beside, 0, first_to), (beside, 1, second_to), (other, 0, me ^ 1),
    ):
        out[at * step:(at + 1) * step, :] = pieces[device]


def merge(beside, aside, first, second):
    step = beside.shape[0] // 2
    for i, out in enumerate((first, second)):
        out[:step, :] = beside[i * step:(i + 1) * step, :]
        out[step:, :] = aside[i * step:(i + 1) * step, :]


def second_half(x, *rest):
    out = rest[-1]
    out[...] = x[out.shape[0]:, :]


def slot(device):
    return (device >> 1 ^ device >> 2) & 1, (device >> 2) * 2 + (device & 1)


def unpack(pieces, held):
    step = held.shape[1]
    for ref, at, place in pieces:
        held[place] = ref[at * step:(at + 1) * step, :]


def came_first(plan, got):
    me, _, ((far_from, far_others), *_) = route(plan)
    own, other, far, handed = got
    return (own, 0, me), (other, 0, me ^ 1), (far, 0, far_from), (handed, 0, far_others)


def came_last(plan, got):
    _, _, (_, (first_from, _), (second_from, _)) = route(plan)
    first, second = got
    return (first, 0, first_from), (first, 1, first_from ^ 1), (second, 0, second_from), (second, 1, second_from ^ 1)


def outer_stage(came, held, table):
    unpack([(ref, at, slot(device)[1]) for ref, at, device in came], held)
    diagonal = slot(came[0][2])[0]
    half, chunks = 4 * held.shape[1] // 3, held.shape[1] // 3
    whole = [held[:, i * chunks:(i + 1) * chunks, :].reshape(half, LANES) for i in range(3)]
    high, low = split(jnp.concatenate(whole, axis=1))
    both = jnp.concatenate([high, low], axis=0)
    m = table.shape[1] // PARTS
    sums = []
    for q in range(PARTS):
        rows = pl.ds(q * m, m)
        sums.append((dot(table[diagonal, rows, 2 * half:], high), dot(table[diagonal, rows, :2 * half], both)))
    return sums


def early(own, other, far, handed, table, out, held):
    sums = outer_stage(came_first(PLANS[0], (own, other, far, handed)), held, table)
    m = out.shape[0] // PARTS
    for q, (less, more) in enumerate(sums):
        out[q * m:(q + 1) * m, :] = less + more


def fetch(*refs):
    count = (len(refs) - 2) // 2
    copies = [pltpu.make_async_copy(refs[i], refs[count + 1 + i], refs[-1].at[i]) for i in range(count)]
    for copy in copies:
        copy.start()
    for copy in copies:
        copy.wait()


def spread(*refs):
    signals, outs, near, (held, arrived) = refs[:3], refs[3:8], refs[8:11], refs[11:]
    channels, block = signals[0].shape
    chunks = block // LANES
    width = block // LOADS

    def at(load):
        return pl.ds(load * width, width)

    copies = []
    for load in range(LOADS):
        for i in range(3):
            ends = signals[i].at[:, at(load)], near[i].at[:, at(load)]
            copies.append(pltpu.make_async_copy(*ends, arrived.at[load * 3 + i]))
            copies[-1].start()
    for load in range(LOADS):
        for i in range(3):
            copies[load * 3 + i].wait()
            rows = pl.ds(i * chunks + load * chunks // LOADS, chunks // LOADS)
            held[:, rows, :] = near[i][:, at(load)].reshape(channels, chunks // LOADS, LANES)
    pack(PLANS[0], held, *outs)


def transform(*refs):
    got, (begun, first, last, into, twiddle), outs, (held, y) = refs[:2], refs[2:7], refs[7:12], refs[12:]
    n, chunks = y.shape[0], y.shape[1] // 2
    rows = n * chunks
    m = rows // PARTS
    turns = [lanes_of(twiddle, q, m) for q in range(PARTS)]
    sums = outer_stage(came_last(PLANS[0], got), held, first)
    outer = [(begun[2 * m * q:2 * m * (q + 1), :] + less) + more for q, (less, more) in enumerate(sums)]
    spectra = []
    for z, (c, s) in zip(outer, turns):
        turned = []
        for i in range(3):
            re, im = z[:m, i * LANES:(i + 1) * LANES], z[m:, i * LANES:(i + 1) * LANES]
            turned.append(jnp.concatenate([re * c + im * s, im * c - re * s], axis=1))
        spectra.append(dot_right(jnp.concatenate(turned, axis=0), into))
    backs = []
    for z in spectra:
        (xr, xi), (gr, gi), (hr, hi) = (lanes_of(z, i, m) for i in range(3))
        p = [jnp.concatenate([ur * gr + ui * gi, ui * gr - ur * gi], axis=1) for ur, ui in ((hr, hi), (xr, xi))]
        backs.append(dot_right(jnp.concatenate(p, axis=0), into))
    out = 0.0
    for joined in range(JOINED):
        real, imag = [], []
        for q in range(joined * PARTS // JOINED, (joined + 1) * PARTS // JOINED):
            c, s = turns[q]
            pairs = [lanes_of(backs[q], i, m) for i in range(2)]
            real.append(jnp.concatenate([dr * c + di * s for dr, di in pairs], axis=1))
            imag.append(jnp.concatenate([dr * s - di * c for dr, di in pairs], axis=1))
        out += dot_left(last[0, joined], last[1, joined], split(jnp.concatenate(real + imag, axis=0)))
    for d in range(n):
        for i in range(2):
            y[d, i * chunks:(i + 1) * chunks, :] = out[d * chunks:(d + 1) * chunks, i * LANES:(i + 1) * LANES]
    pack(PLANS[1], y, *outs)


def gather(*refs):
    got, (a, b, held) = refs[:6], refs[6:]
    unpack(came_first(PLANS[1], got[:4]) + came_last(PLANS[1], got[4:]), held)
    channels, block = a.shape
    chunks = block // LANES
    for i, ref in enumerate((a, b)):
        for j in range(0, chunks, 8):
            ref[:, pl.ds(j * LANES, 8 * LANES)] = held[:, pl.ds(i * chunks + j, 8), :].reshape(channels, 8 * LANES)


def call(body, ins, outs, scratch=(), far_in=0, near_out=True):
    near = pl.BlockSpec(memory_space=pltpu.VMEM)
    kind = pltpu.VMEM if near_out else jax.ShapeDtypeStruct
    return pl.pallas_call(
        body,
        out_shape=[kind(shape, dtype) for shape, dtype in outs],
        in_specs=[pl.BlockSpec(memory_space=pltpu.HBM)] * far_in + [near] * (len(ins) - far_in),
        out_specs=[near] * len(outs),
        scratch_shapes=scratch,
        compiler_params=pltpu.CompilerParams(vmem_limit_bytes=16 * 2**20),
        name=body.__name__,
    )(*(pltpu.with_memory_space_constraint(x, pltpu.VMEM if i >= far_in else pltpu.HBM) for i, x in enumerate(ins)))


def per_device(inputs, grads, response):
    n = lax.axis_size("context")
    channels, block = inputs.shape
    chunks = block // LANES
    kind = jnp.float32

    def swap(x, even, odd):
        return lax.ppermute(x, "context", [(i, i ^ (odd if i % 2 else even)) for i in range(n)])

    def sizes(arrays):
        return [((u * arrays * chunks, LANES), kind) for u in (1, 2, 2, 2, 1)]

    def exchange(plan, own, far, aside, beside, other, meanwhile=lambda x: []):
        step = own.shape[0]
        aside = swap(aside, 1, 1)
        far = swap(far, *plan[0])
        first, second = call(merge, [beside, aside], [((2 * step, LANES), kind)] * 2)
        made = meanwhile(second)
        first, second = swap(first, *plan[1]), swap(second, *plan[2])
        (handed,) = call(second_half, [far, *made[:1]], [((step, LANES), kind)])
        return [own, swap(other, 1, 1), far, swap(handed, 1, 1), first, second, *made]

    held = [jnp.asarray(t) for t in tables(n * block, PARTS, JOINED)]

    def bring(after):
        return call(fetch, [*held, after], [(t.shape, t.dtype) for t in held], [pltpu.SemaphoreType.DMA((len(held),))], len(held))

    near = [pltpu.VMEM((channels, block), kind)] * 3
    near += [pltpu.VMEM((channels, 3 * chunks, LANES), kind), pltpu.SemaphoreType.DMA((3 * LOADS,))]
    sent = call(spread, [inputs, grads, response], sizes(3), near, 3)
    got = exchange(PLANS[0], *sent, meanwhile=bring)
    near = [pltpu.VMEM((n // 2, 3 * chunks, LANES), kind)]
    (begun,) = call(early, [*got[:4], got[6]], [((2 * n * chunks, 3 * LANES), kind)], near)
    pieces = [pltpu.VMEM((n, 2 * chunks, LANES), kind)]
    got = exchange(PLANS[1], *call(transform, [*got[4:6], begun, *got[6:]], sizes(2), near + pieces))
    return call(gather, got, [((channels, block), kind)] * 2, pieces, near_out=False)


RADIX = 128


HIGHEST = lax.Precision.HIGHEST


def phase_pair(row_index, col_index, period, sign_flip):
    product = row_index[:, None] * col_index[None, :] % period
    angles = 2.0 * math.pi / period * product.astype(jnp.float32)
    return (jnp.cos(angles), sign_flip * jnp.sin(angles))


def complex_apply(pattern, tables, values):
    real_real = jnp.einsum(pattern, tables[0], values[0], precision=HIGHEST)
    imag_imag = jnp.einsum(pattern, tables[1], values[1], precision=HIGHEST)
    real_imag = jnp.einsum(pattern, tables[0], values[1], precision=HIGHEST)
    imag_real = jnp.einsum(pattern, tables[1], values[0], precision=HIGHEST)
    return (real_real - imag_imag, real_imag + imag_real)


def complex_times(left_pair, right_pair):
    return (
        left_pair[0] * right_pair[0] - left_pair[1] * right_pair[1],
        left_pair[0] * right_pair[1] + left_pair[1] * right_pair[0],
    )


def by_columns(inputs, grads, response):
    context_size = lax.axis_size("context")
    device_index = lax.axis_index("context")
    channels, block_len = inputs.shape
    column_len = block_len // context_size
    full_length = block_len * context_size
    padded_len = 2 * full_length
    split_len = block_len // RADIX
    freq_rows = jnp.arange(2 * context_size, dtype=jnp.int32)
    part_rows = jnp.arange(context_size, dtype=jnp.int32)
    outer_fwd = phase_pair(freq_rows, part_rows, 2 * context_size, -1.0)
    outer_inv = phase_pair(part_rows, freq_rows, 2 * context_size, 1.0)
    split_rows = jnp.arange(split_len, dtype=jnp.int32)
    radix_rows = jnp.arange(RADIX, dtype=jnp.int32)
    first_fwd = phase_pair(split_rows, split_rows, split_len, -1.0)
    first_inv = (first_fwd[0], -first_fwd[1])
    inner_fwd = phase_pair(split_rows, radix_rows, block_len, -1.0)
    inner_inv = (inner_fwd[0], -inner_fwd[1])
    last_fwd = phase_pair(radix_rows, radix_rows, RADIX, -1.0)
    last_inv = (last_fwd[0], -last_fwd[1])
    pair_rows = 2 * device_index + jnp.arange(2, dtype=jnp.int32)
    column_rows = jnp.arange(block_len, dtype=jnp.int32)
    global_fwd = phase_pair(pair_rows, column_rows, padded_len, -1.0)
    global_inv = (global_fwd[0], -global_fwd[1])
    signals = jnp.stack([inputs, grads, response])
    columns = lax.all_to_all(
        signals.reshape(3, channels, context_size, column_len),
        "context",
        split_axis=2,
        concat_axis=2,
        tiled=True,
    )
    real_part = jnp.einsum("kn,smnj->smkj", outer_fwd[0], columns, precision=HIGHEST)
    imag_part = jnp.einsum("kn,smnj->smkj", outer_fwd[1], columns, precision=HIGHEST)
    columns = jnp.stack([real_part, imag_part], axis=1)
    arrived = lax.all_to_all(columns, "context", split_axis=3, concat_axis=4, tiled=True)
    values = complex_times((arrived[:, 0], arrived[:, 1]), global_fwd)
    shaped = tuple((v.reshape(v.shape[:3] + (split_len, RADIX)) for v in values))
    sectioned = complex_apply("xa,smrab->smrxb", first_fwd, shaped)
    turned = complex_times(sectioned, inner_fwd)
    spec_real, spec_imag = complex_apply("bd,smrxb->smrxd", last_fwd, turned)
    back_input = (
        spec_real[2] * spec_real[1] + spec_imag[2] * spec_imag[1],
        spec_real[2] * spec_imag[1] - spec_imag[2] * spec_real[1],
    )
    back_filter = (
        spec_real[0] * spec_real[1] + spec_imag[0] * spec_imag[1],
        spec_real[0] * spec_imag[1] - spec_imag[0] * spec_real[1],
    )
    inverse_in = ((back_input[0] - back_filter[1])[None], (back_input[1] + back_filter[0])[None])
    sectioned = complex_apply("bd,smrxd->smrxb", last_inv, inverse_in)
    turned = complex_times(sectioned, inner_inv)
    rebuilt = complex_apply("ax,smrxb->smrab", first_inv, turned)
    flat = tuple((v.reshape(v.shape[:3] + (block_len,)) for v in rebuilt))
    untwisted = complex_times(flat, global_inv)
    rows_back = jnp.stack([untwisted[0], untwisted[1]], axis=1)
    arrived = lax.all_to_all(rows_back, "context", split_axis=4, concat_axis=3, tiled=True)
    cos_real = jnp.einsum("nk,smkj->smnj", outer_inv[0], arrived[:, 0], precision=HIGHEST)
    sin_imag = jnp.einsum("nk,smkj->smnj", outer_inv[1], arrived[:, 1], precision=HIGHEST)
    cos_imag = jnp.einsum("nk,smkj->smnj", outer_inv[0], arrived[:, 1], precision=HIGHEST)
    sin_real = jnp.einsum("nk,smkj->smnj", outer_inv[1], arrived[:, 0], precision=HIGHEST)
    folded = jnp.concatenate([cos_real - sin_imag, cos_imag + sin_real], axis=0) / padded_len
    restored = lax.all_to_all(folded, "context", split_axis=2, concat_axis=3, tiled=True).reshape(
        2, channels, block_len
    )
    return (restored[0], restored[1])


def by_shape(inputs, grads, response):
    if inputs.shape[0] == lax.axis_size("context") == 2 * 2 * 2:
        return per_device(inputs, grads, response)
    return by_columns(inputs, grads, response)


def solution(mesh):
    spec = P("tensor", "context")
    return jax.shard_map(by_shape, mesh=mesh, in_specs=(spec,) * 3, out_specs=(spec,) * 2, check_vma=False)
```

```python
import functools
import math

import jax
import jax.numpy as jnp
import numpy as np
from jax import lax
from jax.experimental import pallas as pl
from jax.experimental.pallas import tpu as pltpu
from jax.sharding import PartitionSpec as P

LANES = 128
BF = jnp.bfloat16
PARTS, JOINED, LOADS = 4, 2, 4
PLANS = ((7, 7), (3, 3), (5, 5)), ((7, 7), (3, 3), (5, 5))


def halves(table):
    table = table.astype(np.float32)
    high = table.astype(BF)
    low = (table - high.astype(np.float32)).astype(BF)
    return high, low


def tables(length, devices, parts, joined):
    rows = length // LANES
    k = np.arange(rows)[:, None] + 0.25
    r = np.arange(rows)[None, :]
    outer = 2 * np.pi * k * r / rows
    stacked = np.stack([np.cos(outer), -np.sin(outer)])
    first = stacked.reshape(2, parts, rows // parts, rows).swapaxes(0, 1).reshape(2 * rows, rows)
    high, low = (t.reshape(2 * rows, devices, rows // devices) for t in halves(first))
    first = []
    for me in range(devices):
        _, _, ((far, far_others), (one, _), (two, _)) = route(PLANS[0], me)
        for came in (me, me ^ 1, far, far_others), (one, one ^ 1, two, two ^ 1):
            first.append(np.concatenate([t[:, device] for t in (high, high, low) for device in came], axis=1))
    first = np.stack(first).reshape(devices, 2, 2 * rows, -1)
    last = (stacked / length).reshape(2, joined, rows // joined, rows).transpose(1, 3, 0, 2)
    last = last.reshape(joined, rows, 2 * rows // joined)
    lane = np.arange(LANES)
    turn = 2 * np.pi * k * lane[None, :] / length
    twiddle = np.concatenate([np.cos(turn), np.sin(turn)], axis=1).astype(np.float32)
    inner = 2 * np.pi * (lane[:, None] * lane[None, :] % LANES) / LANES
    cos2, sin2 = np.cos(inner), np.sin(inner)
    into = np.block([[cos2, -sin2], [sin2, cos2]])
    return first, np.stack(halves(last)), np.stack(halves(into)), twiddle


def split(x):
    high = x.astype(BF)
    low = (x - high.astype(jnp.float32)).astype(BF)
    return high, low


def dot(a, b):
    return jnp.dot(a, b, preferred_element_type=jnp.float32)


def dot_right(x, table):
    high, low = split(x)
    return dot(high, table[0]) + (dot(low, table[0]) + dot(high, table[1]))


def dot_left(table_high, table_low, x):
    high, low = x
    return dot(table_high, high) + (dot(table_high, low) + dot(table_low, high))


def lanes_of(x, i, m):
    return x[i * m:(i + 1) * m, :LANES], x[i * m:(i + 1) * m, LANES:]


def route(plan, me=None):
    me = lax.axis_index("context") if me is None else me
    core = me % 2
    to, from_ = [], []
    for even, odd in plan:
        mine, others = even + core * (odd - even), odd + core * (even - odd)
        to.append((me ^ mine, me ^ 1 ^ others))
        back, backs = (mine, others) if even % 2 == 0 else (others, mine)
        from_.append((me ^ back, me ^ 1 ^ backs))
    return me, to, from_


def pack(plan, pieces, own, far, aside, beside):
    me, ((far_to, _), (first_to, first_aside), (second_to, second_aside)), _ = route(plan)
    step = own.shape[0]
    for out, at, device in (
        (own, 0, me), (far, 0, far_to), (far, 1, far_to ^ 1),
        (aside, 0, me ^ 1), (aside, 1, first_aside), (aside, 2, second_aside),
        (beside, 0, first_to), (beside, 1, second_to),
    ):
        out[at * step:(at + 1) * step, :] = pieces[device]


def merge(beside, aside, first, second):
    step = beside.shape[0] // 2
    for i, out in enumerate((first, second)):
        out[:step, :] = beside[i * step:(i + 1) * step, :]
        out[step:, :] = aside[(i + 1) * step:(i + 2) * step, :]


def second_half(x, *rest):
    out = rest[-1]
    out[...] = x[out.shape[0]:, :]


def unpack(pieces, held):
    step = held.shape[1]
    for ref, at, place in pieces:
        held[place] = ref[at * step:(at + 1) * step, :]


def came_first(plan, got):
    me, _, ((far_from, far_others), *_) = route(plan)
    own, aside, far, far_other = got
    return (own, 0, me), (aside, 0, me ^ 1), (far, 0, far_from), (far_other, 0, far_others)


def came_last(plan, got):
    _, _, (_, (first_from, _), (second_from, _)) = route(plan)
    first, second = got
    return (first, 0, first_from), (first, 1, first_from ^ 1), (second, 0, second_from), (second, 1, second_from ^ 1)


def outer_stage(came, step, table):
    half, chunks = 4 * step // 3, step // 3
    whole = []
    for i in range(3):
        whole.append(jnp.concatenate([ref[at * step + i * chunks:at * step + (i + 1) * chunks, :] for ref, at, _ in came]))
    high, low = split(jnp.concatenate(whole, axis=1))
    both = jnp.concatenate([high, low], axis=0)
    m = table.shape[0] // PARTS
    sums = []
    for q in range(PARTS):
        rows = slice(q * m, (q + 1) * m)
        sums.append((dot(table[rows, 2 * half:], high), dot(table[rows, :2 * half], both)))
    return sums


def early(own, aside, far, far_other, table, out):
    sums = outer_stage(came_first(PLANS[0], (own, aside, far, far_other)), own.shape[0], table.at[0])
    m = out.shape[0] // PARTS
    for q, (less, more) in enumerate(sums):
        out[q * m:(q + 1) * m, :] = less + more


def fetch(*refs):
    count = (len(refs) - 2) // 2
    sources = [refs[0].at[lax.axis_index("context")], *refs[1:count]]
    copies = [pltpu.make_async_copy(sources[i], refs[count + 1 + i], refs[-1].at[i]) for i in range(count)]
    for copy in copies:
        copy.start()
    for copy in copies:
        copy.wait()


def spread(*refs):
    signals, outs, near, (held, arrived) = refs[:3], refs[3:7], refs[7:10], refs[10:]
    channels, block = signals[0].shape
    chunks = block // LANES
    width = block // LOADS

    def at(load):
        return pl.ds(load * width, width)

    copies = []
    for load in range(LOADS):
        for i in range(3):
            ends = signals[i].at[:, at(load)], near[i].at[:, at(load)]
            copies.append(pltpu.make_async_copy(*ends, arrived.at[load * 3 + i]))
            copies[-1].start()
    for load in range(LOADS):
        for i in range(3):
            copies[load * 3 + i].wait()
            rows = pl.ds(i * chunks + load * chunks // LOADS, chunks // LOADS)
            held[:, rows, :] = near[i][:, at(load)].reshape(channels, chunks // LOADS, LANES)
    pack(PLANS[0], held, *outs)


def transform(*refs):
    got, (begun, first, last, into, twiddle), outs, (y,) = refs[:2], refs[2:7], refs[7:11], refs[11:]
    n, chunks = y.shape[0], y.shape[1] // 2
    rows = n * chunks
    m = rows // PARTS
    turns = [lanes_of(twiddle, q, m) for q in range(PARTS)]
    sums = outer_stage(came_last(PLANS[0], got), got[0].shape[0] // 2, first.at[1])
    outer = [(begun[2 * m * q:2 * m * (q + 1), :] + less) + more for q, (less, more) in enumerate(sums)]
    spectra = []
    for z, (c, s) in zip(outer, turns):
        turned = []
        for i in range(3):
            re, im = z[:m, i * LANES:(i + 1) * LANES], z[m:, i * LANES:(i + 1) * LANES]
            turned.append(jnp.concatenate([re * c + im * s, im * c - re * s], axis=1))
        spectra.append(dot_right(jnp.concatenate(turned, axis=0), into))
    backs = []
    for z in spectra:
        (xr, xi), (gr, gi), (hr, hi) = (lanes_of(z, i, m) for i in range(3))
        p = [jnp.concatenate([ur * gr + ui * gi, ui * gr - ur * gi], axis=1) for ur, ui in ((hr, hi), (xr, xi))]
        backs.append(dot_right(jnp.concatenate(p, axis=0), into))
    out = 0.0
    for joined in range(JOINED):
        real, imag = [], []
        for q in range(joined * PARTS // JOINED, (joined + 1) * PARTS // JOINED):
            c, s = turns[q]
            pairs = [lanes_of(backs[q], i, m) for i in range(2)]
            real.append(jnp.concatenate([dr * c + di * s for dr, di in pairs], axis=1))
            imag.append(jnp.concatenate([dr * s - di * c for dr, di in pairs], axis=1))
        out += dot_left(last[0, joined], last[1, joined], split(jnp.concatenate(real + imag, axis=0)))
    for d in range(n):
        for i in range(2):
            y[d, i * chunks:(i + 1) * chunks, :] = out[d * chunks:(d + 1) * chunks, i * LANES:(i + 1) * LANES]
    pack(PLANS[1], y, *outs)


def gather(*refs):
    got, (a, b, held) = refs[:6], refs[6:]
    unpack(came_first(PLANS[1], got[:4]) + came_last(PLANS[1], got[4:]), held)
    channels, block = a.shape
    chunks = block // LANES
    for i, ref in enumerate((a, b)):
        for j in range(0, chunks, 8):
            ref[:, pl.ds(j * LANES, 8 * LANES)] = held[:, pl.ds(i * chunks + j, 8), :].reshape(channels, 8 * LANES)


def call(body, ins, outs, scratch=(), far_in=0, near_out=True):
    near = pl.BlockSpec(memory_space=pltpu.VMEM)
    kind = pltpu.VMEM if near_out else jax.ShapeDtypeStruct
    return pl.pallas_call(
        body,
        out_shape=[kind(shape, dtype) for shape, dtype in outs],
        in_specs=[pl.BlockSpec(memory_space=pltpu.HBM)] * far_in + [near] * (len(ins) - far_in),
        out_specs=[near] * len(outs),
        scratch_shapes=scratch,
        compiler_params=pltpu.CompilerParams(vmem_limit_bytes=16 * 2**20),
        name=body.__name__,
    )(*(pltpu.with_memory_space_constraint(x, pltpu.VMEM if i >= far_in else pltpu.HBM) for i, x in enumerate(ins)))


def per_device(inputs, grads, response):
    n = lax.axis_size("context")
    channels, block = inputs.shape
    chunks = block // LANES
    kind = jnp.float32

    def swap(x, even, odd):
        return lax.ppermute(x, "context", [(i, i ^ (odd if i % 2 else even)) for i in range(n)])

    def sizes(arrays):
        return [((u * arrays * chunks, LANES), kind) for u in (1, 2, 3, 2)]

    def exchange(plan, own, far, aside, beside, meanwhile=lambda x: []):
        step = own.shape[0]
        aside = swap(aside, 1, 1)
        far = swap(far, *plan[0])
        first, second = call(merge, [beside, aside], [((2 * step, LANES), kind)] * 2)
        made = meanwhile(second)
        first, second = swap(first, *plan[1]), swap(second, *plan[2])
        (half,) = call(second_half, [far, *made[:1]], [((step, LANES), kind)])
        return [own, aside, far, swap(half, 1, 1), first, second, *made]

    held = [jnp.asarray(t) for t in tables(n * block, n, PARTS, JOINED)]

    def bring(after):
        return call(fetch, [*held, after], [(t.shape[1:] if t is held[0] else t.shape, t.dtype) for t in held], [pltpu.SemaphoreType.DMA((len(held),))], len(held))

    near = [pltpu.VMEM((channels, block), kind)] * 3
    near += [pltpu.VMEM((channels, 3 * chunks, LANES), kind), pltpu.SemaphoreType.DMA((3 * LOADS,))]
    sent = call(spread, [inputs, grads, response], sizes(3), near, 3)
    got = exchange(PLANS[0], *sent, meanwhile=bring)
    (begun,) = call(early, [*got[:4], got[6]], [((2 * n * chunks, 3 * LANES), kind)])
    pieces = [pltpu.VMEM((n, 2 * chunks, LANES), kind)]
    got = exchange(PLANS[1], *call(transform, [*got[4:6], begun, *got[6:]], sizes(2), pieces))
    return call(gather, got, [((channels, block), kind)] * 2, pieces, near_out=False)


RADIX = 128


HIGHEST = lax.Precision.HIGHEST


def phase_pair(row_index, col_index, period, sign_flip):
    product = row_index[:, None] * col_index[None, :] % period
    angles = 2.0 * math.pi / period * product.astype(jnp.float32)
    return (jnp.cos(angles), sign_flip * jnp.sin(angles))


def complex_apply(pattern, tables, values):
    real_real = jnp.einsum(pattern, tables[0], values[0], precision=HIGHEST)
    imag_imag = jnp.einsum(pattern, tables[1], values[1], precision=HIGHEST)
    real_imag = jnp.einsum(pattern, tables[0], values[1], precision=HIGHEST)
    imag_real = jnp.einsum(pattern, tables[1], values[0], precision=HIGHEST)
    return (real_real - imag_imag, real_imag + imag_real)


def complex_times(left_pair, right_pair):
    return (
        left_pair[0] * right_pair[0] - left_pair[1] * right_pair[1],
        left_pair[0] * right_pair[1] + left_pair[1] * right_pair[0],
    )


def by_columns(inputs, grads, response):
    context_size = lax.axis_size("context")
    device_index = lax.axis_index("context")
    channels, block_len = inputs.shape
    column_len = block_len // context_size
    full_length = block_len * context_size
    padded_len = 2 * full_length
    split_len = block_len // RADIX
    freq_rows = jnp.arange(2 * context_size, dtype=jnp.int32)
    part_rows = jnp.arange(context_size, dtype=jnp.int32)
    outer_fwd = phase_pair(freq_rows, part_rows, 2 * context_size, -1.0)
    outer_inv = phase_pair(part_rows, freq_rows, 2 * context_size, 1.0)
    split_rows = jnp.arange(split_len, dtype=jnp.int32)
    radix_rows = jnp.arange(RADIX, dtype=jnp.int32)
    first_fwd = phase_pair(split_rows, split_rows, split_len, -1.0)
    first_inv = (first_fwd[0], -first_fwd[1])
    inner_fwd = phase_pair(split_rows, radix_rows, block_len, -1.0)
    inner_inv = (inner_fwd[0], -inner_fwd[1])
    last_fwd = phase_pair(radix_rows, radix_rows, RADIX, -1.0)
    last_inv = (last_fwd[0], -last_fwd[1])
    pair_rows = 2 * device_index + jnp.arange(2, dtype=jnp.int32)
    column_rows = jnp.arange(block_len, dtype=jnp.int32)
    global_fwd = phase_pair(pair_rows, column_rows, padded_len, -1.0)
    global_inv = (global_fwd[0], -global_fwd[1])
    signals = jnp.stack([inputs, grads, response])
    columns = lax.all_to_all(
        signals.reshape(3, channels, context_size, column_len),
        "context",
        split_axis=2,
        concat_axis=2,
        tiled=True,
    )
    real_part = jnp.einsum("kn,smnj->smkj", outer_fwd[0], columns, precision=HIGHEST)
    imag_part = jnp.einsum("kn,smnj->smkj", outer_fwd[1], columns, precision=HIGHEST)
    columns = jnp.stack([real_part, imag_part], axis=1)
    arrived = lax.all_to_all(columns, "context", split_axis=3, concat_axis=4, tiled=True)
    values = complex_times((arrived[:, 0], arrived[:, 1]), global_fwd)
    shaped = tuple((v.reshape(v.shape[:3] + (split_len, RADIX)) for v in values))
    sectioned = complex_apply("xa,smrab->smrxb", first_fwd, shaped)
    turned = complex_times(sectioned, inner_fwd)
    spec_real, spec_imag = complex_apply("bd,smrxb->smrxd", last_fwd, turned)
    back_input = (
        spec_real[2] * spec_real[1] + spec_imag[2] * spec_imag[1],
        spec_real[2] * spec_imag[1] - spec_imag[2] * spec_real[1],
    )
    back_filter = (
        spec_real[0] * spec_real[1] + spec_imag[0] * spec_imag[1],
        spec_real[0] * spec_imag[1] - spec_imag[0] * spec_real[1],
    )
    inverse_in = ((back_input[0] - back_filter[1])[None], (back_input[1] + back_filter[0])[None])
    sectioned = complex_apply("bd,smrxd->smrxb", last_inv, inverse_in)
    turned = complex_times(sectioned, inner_inv)
    rebuilt = complex_apply("ax,smrxb->smrab", first_inv, turned)
    flat = tuple((v.reshape(v.shape[:3] + (block_len,)) for v in rebuilt))
    untwisted = complex_times(flat, global_inv)
    rows_back = jnp.stack([untwisted[0], untwisted[1]], axis=1)
    arrived = lax.all_to_all(rows_back, "context", split_axis=4, concat_axis=3, tiled=True)
    cos_real = jnp.einsum("nk,smkj->smnj", outer_inv[0], arrived[:, 0], precision=HIGHEST)
    sin_imag = jnp.einsum("nk,smkj->smnj", outer_inv[1], arrived[:, 1], precision=HIGHEST)
    cos_imag = jnp.einsum("nk,smkj->smnj", outer_inv[0], arrived[:, 1], precision=HIGHEST)
    sin_real = jnp.einsum("nk,smkj->smnj", outer_inv[1], arrived[:, 0], precision=HIGHEST)
    folded = jnp.concatenate([cos_real - sin_imag, cos_imag + sin_real], axis=0) / padded_len
    restored = lax.all_to_all(folded, "context", split_axis=2, concat_axis=3, tiled=True).reshape(
        2, channels, block_len
    )
    return (restored[0], restored[1])


def by_shape(inputs, grads, response):
    if inputs.shape[0] == lax.axis_size("context") == 2 * 2 * 2:
        return per_device(inputs, grads, response)
    return by_columns(inputs, grads, response)


def solution(mesh):
    spec = P("tensor", "context")
    return jax.shard_map(by_shape, mesh=mesh, in_specs=(spec,) * 3, out_specs=(spec,) * 2, check_vma=False)
```

```python
import functools
import math

import jax
import jax.numpy as jnp
import numpy as np
from jax import lax
from jax.experimental import pallas as pl
from jax.experimental.pallas import tpu as pltpu
from jax.sharding import PartitionSpec as P

LANES = 128
BF = jnp.bfloat16
PARTS, JOINED, LOADS = 4, 2, 4
PLANS = ((7, 7), (3, 3), (5, 5)), ((7, 7), (3, 3), (5, 5))


def halves(table):
    table = table.astype(np.float32)
    high = table.astype(BF)
    low = (table - high.astype(np.float32)).astype(BF)
    return high, low


def tables(length, devices, parts, joined):
    rows = length // LANES
    k = np.arange(rows)[:, None] + 0.25
    r = np.arange(rows)[None, :]
    outer = 2 * np.pi * k * r / rows
    stacked = np.stack([np.cos(outer), -np.sin(outer)])
    first = stacked.reshape(2, parts, rows // parts, rows).swapaxes(0, 1).reshape(2 * rows, rows)
    high, low = (t.reshape(2 * rows, devices, rows // devices) for t in halves(first))
    first = []
    for me in range(devices):
        _, _, ((far, far_others), (one, _), (two, _)) = route(PLANS[0], me)
        for came in (me, me ^ 1, far, far_others), (one, one ^ 1, two, two ^ 1):
            first.append(np.concatenate([t[:, device] for t in (high, high, low) for device in came], axis=1))
    first = np.stack(first).reshape(devices, 2, 2 * rows, -1)
    last = (stacked / length).reshape(2, joined, rows // joined, rows).transpose(1, 3, 0, 2)
    last = last.reshape(joined, rows, 2 * rows // joined)
    lane = np.arange(LANES)
    turn = 2 * np.pi * k * lane[None, :] / length
    twiddle = np.concatenate([np.cos(turn), np.sin(turn)], axis=1).astype(np.float32)
    inner = 2 * np.pi * (lane[:, None] * lane[None, :] % LANES) / LANES
    cos2, sin2 = np.cos(inner), np.sin(inner)
    into = np.block([[cos2, -sin2], [sin2, cos2]])
    return first, np.stack(halves(last)), np.stack(halves(into)), twiddle


def split(x):
    high = x.astype(BF)
    low = (x - high.astype(jnp.float32)).astype(BF)
    return high, low


def dot(a, b):
    return jnp.dot(a, b, preferred_element_type=jnp.float32)


def dot_right(x, table):
    high, low = split(x)
    return dot(high, table[0]) + (dot(low, table[0]) + dot(high, table[1]))


def dot_left(table_high, table_low, x):
    high, low = x
    return dot(table_high, high) + (dot(table_high, low) + dot(table_low, high))


def lanes_of(x, i, m):
    return x[i * m:(i + 1) * m, :LANES], x[i * m:(i + 1) * m, LANES:]


def route(plan, me=None):
    me = lax.axis_index("context") if me is None else me
    core = me % 2
    to, from_ = [], []
    for even, odd in plan:
        mine, others = even + core * (odd - even), odd + core * (even - odd)
        to.append((me ^ mine, me ^ 1 ^ others))
        back, backs = (mine, others) if even % 2 == 0 else (others, mine)
        from_.append((me ^ back, me ^ 1 ^ backs))
    return me, to, from_


def pack(plan, pieces, own, far, aside, beside, other):
    me, ((far_to, _), (first_to, first_aside), (second_to, second_aside)), _ = route(plan)
    step = own.shape[0]
    for out, at, device in (
        (own, 0, me), (far, 0, far_to), (far, 1, far_to ^ 1), (aside, 0, first_aside), (aside, 1, second_aside),
        (beside, 0, first_to), (beside, 1, second_to), (other, 0, me ^ 1),
    ):
        out[at * step:(at + 1) * step, :] = pieces[device]


def merge(beside, aside, first, second):
    step = beside.shape[0] // 2
    for i, out in enumerate((first, second)):
        out[:step, :] = beside[i * step:(i + 1) * step, :]
        out[step:, :] = aside[i * step:(i + 1) * step, :]


def second_half(x, *rest):
    out = rest[-1]
    out[...] = x[out.shape[0]:, :]


def unpack(pieces, held):
    step = held.shape[1]
    for ref, at, place in pieces:
        held[place] = ref[at * step:(at + 1) * step, :]


def came_first(plan, got):
    me, _, ((far_from, far_others), *_) = route(plan)
    own, other, far, handed = got
    return (own, 0, me), (other, 0, me ^ 1), (far, 0, far_from), (handed, 0, far_others)


def came_last(plan, got):
    _, _, (_, (first_from, _), (second_from, _)) = route(plan)
    first, second = got
    return (first, 0, first_from), (first, 1, first_from ^ 1), (second, 0, second_from), (second, 1, second_from ^ 1)


def outer_stage(came, step, table):
    half, chunks = 4 * step // 3, step // 3
    whole = []
    for i in range(3):
        whole.append(jnp.concatenate([ref[at * step + i * chunks:at * step + (i + 1) * chunks, :] for ref, at, _ in came]))
    high, low = split(jnp.concatenate(whole, axis=1))
    both = jnp.concatenate([high, low], axis=0)
    m = table.shape[0] // PARTS
    sums = []
    for q in range(PARTS):
        rows = slice(q * m, (q + 1) * m)
        sums.append((dot(table[rows, 2 * half:], high), dot(table[rows, :2 * half], both)))
    return sums


def early(own, other, far, handed, table, out):
    sums = outer_stage(came_first(PLANS[0], (own, other, far, handed)), own.shape[0], table.at[0])
    m = out.shape[0] // PARTS
    for q, (less, more) in enumerate(sums):
        out[q * m:(q + 1) * m, :] = less + more


def fetch(*refs):
    count = (len(refs) - 2) // 2
    sources = [refs[0].at[lax.axis_index("context")], *refs[1:count]]
    copies = [pltpu.make_async_copy(sources[i], refs[count + 1 + i], refs[-1].at[i]) for i in range(count)]
    for copy in copies:
        copy.start()
    for copy in copies:
        copy.wait()


def spread(*refs):
    signals, outs, near, (held, arrived) = refs[:3], refs[3:8], refs[8:11], refs[11:]
    channels, block = signals[0].shape
    chunks = block // LANES
    width = block // LOADS

    def at(load):
        return pl.ds(load * width, width)

    copies = []
    for load in range(LOADS):
        for i in range(3):
            ends = signals[i].at[:, at(load)], near[i].at[:, at(load)]
            copies.append(pltpu.make_async_copy(*ends, arrived.at[load * 3 + i]))
            copies[-1].start()
    for load in range(LOADS):
        for i in range(3):
            copies[load * 3 + i].wait()
            rows = pl.ds(i * chunks + load * chunks // LOADS, chunks // LOADS)
            held[:, rows, :] = near[i][:, at(load)].reshape(channels, chunks // LOADS, LANES)
    pack(PLANS[0], held, *outs)


def transform(*refs):
    got, (begun, first, last, into, twiddle), outs, (y,) = refs[:2], refs[2:7], refs[7:12], refs[12:]
    n, chunks = y.shape[0], y.shape[1] // 2
    rows = n * chunks
    m = rows // PARTS
    turns = [lanes_of(twiddle, q, m) for q in range(PARTS)]
    sums = outer_stage(came_last(PLANS[0], got), got[0].shape[0] // 2, first.at[1])
    outer = [(begun[2 * m * q:2 * m * (q + 1), :] + less) + more for q, (less, more) in enumerate(sums)]
    spectra = []
    for z, (c, s) in zip(outer, turns):
        turned = []
        for i in range(3):
            re, im = z[:m, i * LANES:(i + 1) * LANES], z[m:, i * LANES:(i + 1) * LANES]
            turned.append(jnp.concatenate([re * c + im * s, im * c - re * s], axis=1))
        spectra.append(dot_right(jnp.concatenate(turned, axis=0), into))
    backs = []
    for z in spectra:
        (xr, xi), (gr, gi), (hr, hi) = (lanes_of(z, i, m) for i in range(3))
        p = [jnp.concatenate([ur * gr + ui * gi, ui * gr - ur * gi], axis=1) for ur, ui in ((hr, hi), (xr, xi))]
        backs.append(dot_right(jnp.concatenate(p, axis=0), into))
    out = 0.0
    for joined in range(JOINED):
        real, imag = [], []
        for q in range(joined * PARTS // JOINED, (joined + 1) * PARTS // JOINED):
            c, s = turns[q]
            pairs = [lanes_of(backs[q], i, m) for i in range(2)]
            real.append(jnp.concatenate([dr * c + di * s for dr, di in pairs], axis=1))
            imag.append(jnp.concatenate([dr * s - di * c for dr, di in pairs], axis=1))
        out += dot_left(last[0, joined], last[1, joined], split(jnp.concatenate(real + imag, axis=0)))
    for d in range(n):
        for i in range(2):
            y[d, i * chunks:(i + 1) * chunks, :] = out[d * chunks:(d + 1) * chunks, i * LANES:(i + 1) * LANES]
    pack(PLANS[1], y, *outs)


def gather(*refs):
    got, (a, b, held) = refs[:6], refs[6:]
    unpack(came_first(PLANS[1], got[:4]) + came_last(PLANS[1], got[4:]), held)
    channels, block = a.shape
    chunks = block // LANES
    for i, ref in enumerate((a, b)):
        for j in range(0, chunks, 8):
            ref[:, pl.ds(j * LANES, 8 * LANES)] = held[:, pl.ds(i * chunks + j, 8), :].reshape(channels, 8 * LANES)


def call(body, ins, outs, scratch=(), far_in=0, near_out=True):
    near = pl.BlockSpec(memory_space=pltpu.VMEM)
    kind = pltpu.VMEM if near_out else jax.ShapeDtypeStruct
    return pl.pallas_call(
        body,
        out_shape=[kind(shape, dtype) for shape, dtype in outs],
        in_specs=[pl.BlockSpec(memory_space=pltpu.HBM)] * far_in + [near] * (len(ins) - far_in),
        out_specs=[near] * len(outs),
        scratch_shapes=scratch,
        compiler_params=pltpu.CompilerParams(vmem_limit_bytes=16 * 2**20),
        name=body.__name__,
    )(*(pltpu.with_memory_space_constraint(x, pltpu.VMEM if i >= far_in else pltpu.HBM) for i, x in enumerate(ins)))


def per_device(inputs, grads, response):
    n = lax.axis_size("context")
    channels, block = inputs.shape
    chunks = block // LANES
    kind = jnp.float32

    def swap(x, even, odd):
        return lax.ppermute(x, "context", [(i, i ^ (odd if i % 2 else even)) for i in range(n)])

    def sizes(arrays):
        return [((u * arrays * chunks, LANES), kind) for u in (1, 2, 2, 2, 1)]

    def exchange(plan, own, far, aside, beside, other, meanwhile=lambda x: []):
        step = own.shape[0]
        aside = swap(aside, 1, 1)
        far = swap(far, *plan[0])
        first, second = call(merge, [beside, aside], [((2 * step, LANES), kind)] * 2)
        made = meanwhile(second)
        first, second = swap(first, *plan[1]), swap(second, *plan[2])
        (handed,) = call(second_half, [far, *made[:1]], [((step, LANES), kind)])
        return [own, swap(other, 1, 1), far, swap(handed, 1, 1), first, second, *made]

    held = [jnp.asarray(t) for t in tables(n * block, n, PARTS, JOINED)]

    def bring(after):
        return call(fetch, [*held, after], [(t.shape[1:] if t is held[0] else t.shape, t.dtype) for t in held], [pltpu.SemaphoreType.DMA((len(held),))], len(held))

    near = [pltpu.VMEM((channels, block), kind)] * 3
    near += [pltpu.VMEM((channels, 3 * chunks, LANES), kind), pltpu.SemaphoreType.DMA((3 * LOADS,))]
    sent = call(spread, [inputs, grads, response], sizes(3), near, 3)
    got = exchange(PLANS[0], *sent, meanwhile=bring)
    (begun,) = call(early, [*got[:4], got[6]], [((2 * n * chunks, 3 * LANES), kind)])
    pieces = [pltpu.VMEM((n, 2 * chunks, LANES), kind)]
    got = exchange(PLANS[1], *call(transform, [*got[4:6], begun, *got[6:]], sizes(2), pieces))
    return call(gather, got, [((channels, block), kind)] * 2, pieces, near_out=False)


RADIX = 128


HIGHEST = lax.Precision.HIGHEST


def phase_pair(row_index, col_index, period, sign_flip):
    product = row_index[:, None] * col_index[None, :] % period
    angles = 2.0 * math.pi / period * product.astype(jnp.float32)
    return (jnp.cos(angles), sign_flip * jnp.sin(angles))


def complex_apply(pattern, tables, values):
    real_real = jnp.einsum(pattern, tables[0], values[0], precision=HIGHEST)
    imag_imag = jnp.einsum(pattern, tables[1], values[1], precision=HIGHEST)
    real_imag = jnp.einsum(pattern, tables[0], values[1], precision=HIGHEST)
    imag_real = jnp.einsum(pattern, tables[1], values[0], precision=HIGHEST)
    return (real_real - imag_imag, real_imag + imag_real)


def complex_times(left_pair, right_pair):
    return (
        left_pair[0] * right_pair[0] - left_pair[1] * right_pair[1],
        left_pair[0] * right_pair[1] + left_pair[1] * right_pair[0],
    )


def by_columns(inputs, grads, response):
    context_size = lax.axis_size("context")
    device_index = lax.axis_index("context")
    channels, block_len = inputs.shape
    column_len = block_len // context_size
    full_length = block_len * context_size
    padded_len = 2 * full_length
    split_len = block_len // RADIX
    freq_rows = jnp.arange(2 * context_size, dtype=jnp.int32)
    part_rows = jnp.arange(context_size, dtype=jnp.int32)
    outer_fwd = phase_pair(freq_rows, part_rows, 2 * context_size, -1.0)
    outer_inv = phase_pair(part_rows, freq_rows, 2 * context_size, 1.0)
    split_rows = jnp.arange(split_len, dtype=jnp.int32)
    radix_rows = jnp.arange(RADIX, dtype=jnp.int32)
    first_fwd = phase_pair(split_rows, split_rows, split_len, -1.0)
    first_inv = (first_fwd[0], -first_fwd[1])
    inner_fwd = phase_pair(split_rows, radix_rows, block_len, -1.0)
    inner_inv = (inner_fwd[0], -inner_fwd[1])
    last_fwd = phase_pair(radix_rows, radix_rows, RADIX, -1.0)
    last_inv = (last_fwd[0], -last_fwd[1])
    pair_rows = 2 * device_index + jnp.arange(2, dtype=jnp.int32)
    column_rows = jnp.arange(block_len, dtype=jnp.int32)
    global_fwd = phase_pair(pair_rows, column_rows, padded_len, -1.0)
    global_inv = (global_fwd[0], -global_fwd[1])
    signals = jnp.stack([inputs, grads, response])
    columns = lax.all_to_all(
        signals.reshape(3, channels, context_size, column_len),
        "context",
        split_axis=2,
        concat_axis=2,
        tiled=True,
    )
    real_part = jnp.einsum("kn,smnj->smkj", outer_fwd[0], columns, precision=HIGHEST)
    imag_part = jnp.einsum("kn,smnj->smkj", outer_fwd[1], columns, precision=HIGHEST)
    columns = jnp.stack([real_part, imag_part], axis=1)
    arrived = lax.all_to_all(columns, "context", split_axis=3, concat_axis=4, tiled=True)
    values = complex_times((arrived[:, 0], arrived[:, 1]), global_fwd)
    shaped = tuple((v.reshape(v.shape[:3] + (split_len, RADIX)) for v in values))
    sectioned = complex_apply("xa,smrab->smrxb", first_fwd, shaped)
    turned = complex_times(sectioned, inner_fwd)
    spec_real, spec_imag = complex_apply("bd,smrxb->smrxd", last_fwd, turned)
    back_input = (
        spec_real[2] * spec_real[1] + spec_imag[2] * spec_imag[1],
        spec_real[2] * spec_imag[1] - spec_imag[2] * spec_real[1],
    )
    back_filter = (
        spec_real[0] * spec_real[1] + spec_imag[0] * spec_imag[1],
        spec_real[0] * spec_imag[1] - spec_imag[0] * spec_real[1],
    )
    inverse_in = ((back_input[0] - back_filter[1])[None], (back_input[1] + back_filter[0])[None])
    sectioned = complex_apply("bd,smrxd->smrxb", last_inv, inverse_in)
    turned = complex_times(sectioned, inner_inv)
    rebuilt = complex_apply("ax,smrxb->smrab", first_inv, turned)
    flat = tuple((v.reshape(v.shape[:3] + (block_len,)) for v in rebuilt))
    untwisted = complex_times(flat, global_inv)
    rows_back = jnp.stack([untwisted[0], untwisted[1]], axis=1)
    arrived = lax.all_to_all(rows_back, "context", split_axis=4, concat_axis=3, tiled=True)
    cos_real = jnp.einsum("nk,smkj->smnj", outer_inv[0], arrived[:, 0], precision=HIGHEST)
    sin_imag = jnp.einsum("nk,smkj->smnj", outer_inv[1], arrived[:, 1], precision=HIGHEST)
    cos_imag = jnp.einsum("nk,smkj->smnj", outer_inv[0], arrived[:, 1], precision=HIGHEST)
    sin_real = jnp.einsum("nk,smkj->smnj", outer_inv[1], arrived[:, 0], precision=HIGHEST)
    folded = jnp.concatenate([cos_real - sin_imag, cos_imag + sin_real], axis=0) / padded_len
    restored = lax.all_to_all(folded, "context", split_axis=2, concat_axis=3, tiled=True).reshape(
        2, channels, block_len
    )
    return (restored[0], restored[1])


def by_shape(inputs, grads, response):
    if inputs.shape[0] == lax.axis_size("context") == 2 * 2 * 2:
        return per_device(inputs, grads, response)
    return by_columns(inputs, grads, response)


def solution(mesh):
    spec = P("tensor", "context")
    return jax.shard_map(by_shape, mesh=mesh, in_specs=(spec,) * 3, out_specs=(spec,) * 2, check_vma=False)
```

```python
import functools
import math

import jax
import jax.numpy as jnp
import numpy as np
from jax import lax
from jax.experimental import pallas as pl
from jax.experimental.pallas import tpu as pltpu
from jax.sharding import PartitionSpec as P

LANES = 128
BF = jnp.bfloat16
PARTS, JOINED, LOADS = 4, 2, 1
PLANS = ((7, 7), (3, 3), (5, 5)), ((7, 7), (3, 3), (5, 5))


def halves(table):
    table = table.astype(np.float32)
    high = table.astype(BF)
    low = (table - high.astype(np.float32)).astype(BF)
    return high, low


def tables(length, parts, joined):
    rows = length // LANES
    k = np.arange(rows)[:, None] + 0.25
    r = np.arange(rows)[None, :]
    outer = 2 * np.pi * k * r / rows
    stacked = np.stack([np.cos(outer), -np.sin(outer)])
    first = stacked.reshape(2, parts, rows // parts, rows).swapaxes(0, 1).reshape(2 * rows, rows)
    high, low = (t.reshape(2 * rows, 2, 2, rows // 4) for t in halves(first))
    first = []
    for diagonal in ((0, 0), (1, 1)), ((0, 1), (1, 0)):
        cut_high, cut_low = (np.concatenate([t[:, y, x] for y, x in diagonal], axis=1) for t in (high, low))
        first.append(np.concatenate([cut_high, cut_high, cut_low], axis=1))
    last = (stacked / length).reshape(2, joined, rows // joined, rows).transpose(1, 3, 0, 2)
    last = last.reshape(joined, rows, 2 * rows // joined)
    lane = np.arange(LANES)
    turn = 2 * np.pi * k * lane[None, :] / length
    twiddle = np.concatenate([np.cos(turn), np.sin(turn)], axis=1).astype(np.float32)
    inner = 2 * np.pi * (lane[:, None] * lane[None, :] % LANES) / LANES
    cos2, sin2 = np.cos(inner), np.sin(inner)
    into = np.block([[cos2, -sin2], [sin2, cos2]])
    return np.stack(first), np.stack(halves(last)), np.stack(halves(into)), twiddle


def split(x):
    high = x.astype(BF)
    low = (x - high.astype(jnp.float32)).astype(BF)
    return high, low


def dot(a, b):
    return jnp.dot(a, b, preferred_element_type=jnp.float32)


def dot_right(x, table):
    high, low = split(x)
    return dot(high, table[0]) + (dot(low, table[0]) + dot(high, table[1]))


def dot_left(table_high, table_low, x):
    high, low = x
    return dot(table_high, high) + (dot(table_high, low) + dot(table_low, high))


def lanes_of(x, i, m):
    return x[i * m:(i + 1) * m, :LANES], x[i * m:(i + 1) * m, LANES:]


def route(plan):
    me = lax.axis_index("context")
    core = me % 2
    to, from_ = [], []
    for even, odd in plan:
        mine, others = even + core * (odd - even), odd + core * (even - odd)
        to.append((me ^ mine, me ^ 1 ^ others))
        back, backs = (mine, others) if even % 2 == 0 else (others, mine)
        from_.append((me ^ back, me ^ 1 ^ backs))
    return me, to, from_


def pack(plan, pieces, own, far, aside, beside):
    me, ((far_to, _), (first_to, first_aside), (second_to, second_aside)), _ = route(plan)
    step = own.shape[0]
    for out, at, device in (
        (own, 0, me), (far, 0, far_to), (far, 1, far_to ^ 1),
        (aside, 0, me ^ 1), (aside, 1, first_aside), (aside, 2, second_aside),
        (beside, 0, first_to), (beside, 1, second_to),
    ):
        out[at * step:(at + 1) * step, :] = pieces[device]


def merge(beside, aside, first, second):
    step = beside.shape[0] // 2
    for i, out in enumerate((first, second)):
        out[:step, :] = beside[i * step:(i + 1) * step, :]
        out[step:, :] = aside[(i + 1) * step:(i + 2) * step, :]


def second_half(x, *rest):
    out = rest[-1]
    out[...] = x[out.shape[0]:, :]


def slot(device):
    return (device >> 1 ^ device >> 2) & 1, (device >> 2) * 2 + (device & 1)


def unpack(pieces, held):
    step = held.shape[1]
    for ref, at, place in pieces:
        held[place] = ref[at * step:(at + 1) * step, :]


def came_first(plan, got):
    me, _, ((far_from, far_others), *_) = route(plan)
    own, aside, far, far_other = got
    return (own, 0, me), (aside, 0, me ^ 1), (far, 0, far_from), (far_other, 0, far_others)


def came_last(plan, got):
    _, _, (_, (first_from, _), (second_from, _)) = route(plan)
    first, second = got
    return (first, 0, first_from), (first, 1, first_from ^ 1), (second, 0, second_from), (second, 1, second_from ^ 1)


def outer_stage(came, held, table):
    unpack([(ref, at, slot(device)[1]) for ref, at, device in came], held)
    diagonal = slot(came[0][2])[0]
    half, chunks = 4 * held.shape[1] // 3, held.shape[1] // 3
    whole = [held[:, i * chunks:(i + 1) * chunks, :].reshape(half, LANES) for i in range(3)]
    high, low = split(jnp.concatenate(whole, axis=1))
    both = jnp.concatenate([high, low], axis=0)
    m = table.shape[1] // PARTS
    sums = []
    for q in range(PARTS):
        rows = pl.ds(q * m, m)
        sums.append((dot(table[diagonal, rows, 2 * half:], high), dot(table[diagonal, rows, :2 * half], both)))
    return sums


def early(own, aside, far, far_other, table, out, held):
    sums = outer_stage(came_first(PLANS[0], (own, aside, far, far_other)), held, table)
    m = out.shape[0] // PARTS
    for q, (less, more) in enumerate(sums):
        out[q * m:(q + 1) * m, :] = less + more


def fetch(*refs):
    count = (len(refs) - 2) // 2
    copies = [pltpu.make_async_copy(refs[i], refs[count + 1 + i], refs[-1].at[i]) for i in range(count)]
    for copy in copies:
        copy.start()
    for copy in copies:
        copy.wait()


def spread(*refs):
    signals, outs, near, (held, arrived) = refs[:3], refs[3:7], refs[7:10], refs[10:]
    channels, block = signals[0].shape
    chunks = block // LANES
    width = block // LOADS

    def at(load):
        return pl.ds(load * width, width)

    copies = []
    for load in range(LOADS):
        for i in range(3):
            ends = signals[i].at[:, at(load)], near[i].at[:, at(load)]
            copies.append(pltpu.make_async_copy(*ends, arrived.at[load * 3 + i]))
            copies[-1].start()
    for load in range(LOADS):
        for i in range(3):
            copies[load * 3 + i].wait()
            rows = pl.ds(i * chunks + load * chunks // LOADS, chunks // LOADS)
            held[:, rows, :] = near[i][:, at(load)].reshape(channels, chunks // LOADS, LANES)
    pack(PLANS[0], held, *outs)


def transform(*refs):
    got, (begun, first, last, into, twiddle), outs, (held, y) = refs[:2], refs[2:7], refs[7:11], refs[11:]
    n, chunks = y.shape[0], y.shape[1] // 2
    rows = n * chunks
    m = rows // PARTS
    turns = [lanes_of(twiddle, q, m) for q in range(PARTS)]
    sums = outer_stage(came_last(PLANS[0], got), held, first)
    outer = [(begun[2 * m * q:2 * m * (q + 1), :] + less) + more for q, (less, more) in enumerate(sums)]
    spectra = []
    for z, (c, s) in zip(outer, turns):
        turned = []
        for i in range(3):
            re, im = z[:m, i * LANES:(i + 1) * LANES], z[m:, i * LANES:(i + 1) * LANES]
            turned.append(jnp.concatenate([re * c + im * s, im * c - re * s], axis=1))
        spectra.append(dot_right(jnp.concatenate(turned, axis=0), into))
    backs = []
    for z in spectra:
        (xr, xi), (gr, gi), (hr, hi) = (lanes_of(z, i, m) for i in range(3))
        p = [jnp.concatenate([ur * gr + ui * gi, ui * gr - ur * gi], axis=1) for ur, ui in ((hr, hi), (xr, xi))]
        backs.append(dot_right(jnp.concatenate(p, axis=0), into))
    out = 0.0
    for joined in range(JOINED):
        real, imag = [], []
        for q in range(joined * PARTS // JOINED, (joined + 1) * PARTS // JOINED):
            c, s = turns[q]
            pairs = [lanes_of(backs[q], i, m) for i in range(2)]
            real.append(jnp.concatenate([dr * c + di * s for dr, di in pairs], axis=1))
            imag.append(jnp.concatenate([dr * s - di * c for dr, di in pairs], axis=1))
        out += dot_left(last[0, joined], last[1, joined], split(jnp.concatenate(real + imag, axis=0)))
    for d in range(n):
        for i in range(2):
            y[d, i * chunks:(i + 1) * chunks, :] = out[d * chunks:(d + 1) * chunks, i * LANES:(i + 1) * LANES]
    pack(PLANS[1], y, *outs)


def gather(*refs):
    got, (a, b, held) = refs[:6], refs[6:]
    unpack(came_first(PLANS[1], got[:4]) + came_last(PLANS[1], got[4:]), held)
    channels, block = a.shape
    chunks = block // LANES
    for i, ref in enumerate((a, b)):
        for j in range(0, chunks, 8):
            ref[:, pl.ds(j * LANES, 8 * LANES)] = held[:, pl.ds(i * chunks + j, 8), :].reshape(channels, 8 * LANES)


def call(body, ins, outs, scratch=(), far_in=0, near_out=True):
    near = pl.BlockSpec(memory_space=pltpu.VMEM)
    kind = pltpu.VMEM if near_out else jax.ShapeDtypeStruct
    return pl.pallas_call(
        body,
        out_shape=[kind(shape, dtype) for shape, dtype in outs],
        in_specs=[pl.BlockSpec(memory_space=pltpu.HBM)] * far_in + [near] * (len(ins) - far_in),
        out_specs=[near] * len(outs),
        scratch_shapes=scratch,
        compiler_params=pltpu.CompilerParams(vmem_limit_bytes=16 * 2**20),
        name=body.__name__,
    )(*(pltpu.with_memory_space_constraint(x, pltpu.VMEM if i >= far_in else pltpu.HBM) for i, x in enumerate(ins)))


def per_device(inputs, grads, response):
    n = lax.axis_size("context")
    channels, block = inputs.shape
    chunks = block // LANES
    kind = jnp.float32

    def swap(x, even, odd):
        return lax.ppermute(x, "context", [(i, i ^ (odd if i % 2 else even)) for i in range(n)])

    def sizes(arrays):
        return [((u * arrays * chunks, LANES), kind) for u in (1, 2, 3, 2)]

    def exchange(plan, own, far, aside, beside, meanwhile=lambda x: []):
        step = own.shape[0]
        aside = swap(aside, 1, 1)
        far = swap(far, *plan[0])
        first, second = call(merge, [beside, aside], [((2 * step, LANES), kind)] * 2)
        made = meanwhile(second)
        first, second = swap(first, *plan[1]), swap(second, *plan[2])
        (half,) = call(second_half, [far, *made[:1]], [((step, LANES), kind)])
        return [own, aside, far, swap(half, 1, 1), first, second, *made]

    held = [jnp.asarray(t) for t in tables(n * block, PARTS, JOINED)]

    def bring(after):
        return call(fetch, [*held, after], [(t.shape, t.dtype) for t in held], [pltpu.SemaphoreType.DMA((len(held),))], len(held))

    near = [pltpu.VMEM((channels, block), kind)] * 3
    near += [pltpu.VMEM((channels, 3 * chunks, LANES), kind), pltpu.SemaphoreType.DMA((3 * LOADS,))]
    sent = call(spread, [inputs, grads, response], sizes(3), near, 3)
    got = exchange(PLANS[0], *sent, meanwhile=bring)
    near = [pltpu.VMEM((n // 2, 3 * chunks, LANES), kind)]
    (begun,) = call(early, [*got[:4], got[6]], [((2 * n * chunks, 3 * LANES), kind)], near)
    pieces = [pltpu.VMEM((n, 2 * chunks, LANES), kind)]
    got = exchange(PLANS[1], *call(transform, [*got[4:6], begun, *got[6:]], sizes(2), near + pieces))
    return call(gather, got, [((channels, block), kind)] * 2, pieces, near_out=False)


RADIX = 128


HIGHEST = lax.Precision.HIGHEST


def phase_pair(row_index, col_index, period, sign_flip):
    product = row_index[:, None] * col_index[None, :] % period
    angles = 2.0 * math.pi / period * product.astype(jnp.float32)
    return (jnp.cos(angles), sign_flip * jnp.sin(angles))


def complex_apply(pattern, tables, values):
    real_real = jnp.einsum(pattern, tables[0], values[0], precision=HIGHEST)
    imag_imag = jnp.einsum(pattern, tables[1], values[1], precision=HIGHEST)
    real_imag = jnp.einsum(pattern, tables[0], values[1], precision=HIGHEST)
    imag_real = jnp.einsum(pattern, tables[1], values[0], precision=HIGHEST)
    return (real_real - imag_imag, real_imag + imag_real)


def complex_times(left_pair, right_pair):
    return (
        left_pair[0] * right_pair[0] - left_pair[1] * right_pair[1],
        left_pair[0] * right_pair[1] + left_pair[1] * right_pair[0],
    )


def by_columns(inputs, grads, response):
    context_size = lax.axis_size("context")
    device_index = lax.axis_index("context")
    channels, block_len = inputs.shape
    column_len = block_len // context_size
    full_length = block_len * context_size
    padded_len = 2 * full_length
    split_len = block_len // RADIX
    freq_rows = jnp.arange(2 * context_size, dtype=jnp.int32)
    part_rows = jnp.arange(context_size, dtype=jnp.int32)
    outer_fwd = phase_pair(freq_rows, part_rows, 2 * context_size, -1.0)
    outer_inv = phase_pair(part_rows, freq_rows, 2 * context_size, 1.0)
    split_rows = jnp.arange(split_len, dtype=jnp.int32)
    radix_rows = jnp.arange(RADIX, dtype=jnp.int32)
    first_fwd = phase_pair(split_rows, split_rows, split_len, -1.0)
    first_inv = (first_fwd[0], -first_fwd[1])
    inner_fwd = phase_pair(split_rows, radix_rows, block_len, -1.0)
    inner_inv = (inner_fwd[0], -inner_fwd[1])
    last_fwd = phase_pair(radix_rows, radix_rows, RADIX, -1.0)
    last_inv = (last_fwd[0], -last_fwd[1])
    pair_rows = 2 * device_index + jnp.arange(2, dtype=jnp.int32)
    column_rows = jnp.arange(block_len, dtype=jnp.int32)
    global_fwd = phase_pair(pair_rows, column_rows, padded_len, -1.0)
    global_inv = (global_fwd[0], -global_fwd[1])
    signals = jnp.stack([inputs, grads, response])
    columns = lax.all_to_all(
        signals.reshape(3, channels, context_size, column_len),
        "context",
        split_axis=2,
        concat_axis=2,
        tiled=True,
    )
    real_part = jnp.einsum("kn,smnj->smkj", outer_fwd[0], columns, precision=HIGHEST)
    imag_part = jnp.einsum("kn,smnj->smkj", outer_fwd[1], columns, precision=HIGHEST)
    columns = jnp.stack([real_part, imag_part], axis=1)
    arrived = lax.all_to_all(columns, "context", split_axis=3, concat_axis=4, tiled=True)
    values = complex_times((arrived[:, 0], arrived[:, 1]), global_fwd)
    shaped = tuple((v.reshape(v.shape[:3] + (split_len, RADIX)) for v in values))
    sectioned = complex_apply("xa,smrab->smrxb", first_fwd, shaped)
    turned = complex_times(sectioned, inner_fwd)
    spec_real, spec_imag = complex_apply("bd,smrxb->smrxd", last_fwd, turned)
    back_input = (
        spec_real[2] * spec_real[1] + spec_imag[2] * spec_imag[1],
        spec_real[2] * spec_imag[1] - spec_imag[2] * spec_real[1],
    )
    back_filter = (
        spec_real[0] * spec_real[1] + spec_imag[0] * spec_imag[1],
        spec_real[0] * spec_imag[1] - spec_imag[0] * spec_real[1],
    )
    inverse_in = ((back_input[0] - back_filter[1])[None], (back_input[1] + back_filter[0])[None])
    sectioned = complex_apply("bd,smrxd->smrxb", last_inv, inverse_in)
    turned = complex_times(sectioned, inner_inv)
    rebuilt = complex_apply("ax,smrxb->smrab", first_inv, turned)
    flat = tuple((v.reshape(v.shape[:3] + (block_len,)) for v in rebuilt))
    untwisted = complex_times(flat, global_inv)
    rows_back = jnp.stack([untwisted[0], untwisted[1]], axis=1)
    arrived = lax.all_to_all(rows_back, "context", split_axis=4, concat_axis=3, tiled=True)
    cos_real = jnp.einsum("nk,smkj->smnj", outer_inv[0], arrived[:, 0], precision=HIGHEST)
    sin_imag = jnp.einsum("nk,smkj->smnj", outer_inv[1], arrived[:, 1], precision=HIGHEST)
    cos_imag = jnp.einsum("nk,smkj->smnj", outer_inv[0], arrived[:, 1], precision=HIGHEST)
    sin_real = jnp.einsum("nk,smkj->smnj", outer_inv[1], arrived[:, 0], precision=HIGHEST)
    folded = jnp.concatenate([cos_real - sin_imag, cos_imag + sin_real], axis=0) / padded_len
    restored = lax.all_to_all(folded, "context", split_axis=2, concat_axis=3, tiled=True).reshape(
        2, channels, block_len
    )
    return (restored[0], restored[1])


def by_shape(inputs, grads, response):
    if inputs.shape[0] == lax.axis_size("context") == 2 * 2 * 2:
        return per_device(inputs, grads, response)
    return by_columns(inputs, grads, response)


def solution(mesh):
    spec = P("tensor", "context")
    return jax.shard_map(by_shape, mesh=mesh, in_specs=(spec,) * 3, out_specs=(spec,) * 2, check_vma=False)
```

```python
import functools
import math

import jax
import jax.numpy as jnp
import numpy as np
from jax import lax
from jax.experimental import pallas as pl
from jax.experimental.pallas import tpu as pltpu
from jax.sharding import PartitionSpec as P

LANES = 128
BF = jnp.bfloat16
PARTS, JOINED, LOADS = 4, 2, 1
PLANS = ((7, 7), (3, 3), (5, 5)), ((7, 7), (3, 3), (5, 5))


def halves(table):
    table = table.astype(np.float32)
    high = table.astype(BF)
    low = (table - high.astype(np.float32)).astype(BF)
    return high, low


def tables(length, parts, joined):
    rows = length // LANES
    k = np.arange(rows)[:, None] + 0.25
    r = np.arange(rows)[None, :]
    outer = 2 * np.pi * k * r / rows
    stacked = np.stack([np.cos(outer), -np.sin(outer)])
    first = stacked.reshape(2, parts, rows // parts, rows).swapaxes(0, 1).reshape(2 * rows, rows)
    high, low = (t.reshape(2 * rows, 2, 2, rows // 4) for t in halves(first))
    first = []
    for diagonal in ((0, 0), (1, 1)), ((0, 1), (1, 0)):
        cut_high, cut_low = (np.concatenate([t[:, y, x] for y, x in diagonal], axis=1) for t in (high, low))
        first.append(np.concatenate([cut_high, cut_high, cut_low], axis=1))
    last = (stacked / length).reshape(2, joined, rows // joined, rows).transpose(1, 3, 0, 2)
    last = last.reshape(joined, rows, 2 * rows // joined)
    lane = np.arange(LANES)
    turn = 2 * np.pi * k * lane[None, :] / length
    twiddle = np.concatenate([np.cos(turn), np.sin(turn)], axis=1).astype(np.float32)
    inner = 2 * np.pi * (lane[:, None] * lane[None, :] % LANES) / LANES
    cos2, sin2 = np.cos(inner), np.sin(inner)
    into = np.block([[cos2, -sin2], [sin2, cos2]])
    return np.stack(first), np.stack(halves(last)), np.stack(halves(into)), twiddle


def split(x):
    high = x.astype(BF)
    low = (x - high.astype(jnp.float32)).astype(BF)
    return high, low


def dot(a, b):
    return jnp.dot(a, b, preferred_element_type=jnp.float32)


def dot_right(x, table):
    high, low = split(x)
    return dot(high, table[0]) + (dot(low, table[0]) + dot(high, table[1]))


def dot_left(table_high, table_low, x):
    high, low = x
    return dot(table_high, high) + (dot(table_high, low) + dot(table_low, high))


def lanes_of(x, i, m):
    return x[i * m:(i + 1) * m, :LANES], x[i * m:(i + 1) * m, LANES:]


def route(plan):
    me = lax.axis_index("context")
    core = me % 2
    to, from_ = [], []
    for even, odd in plan:
        mine, others = even + core * (odd - even), odd + core * (even - odd)
        to.append((me ^ mine, me ^ 1 ^ others))
        back, backs = (mine, others) if even % 2 == 0 else (others, mine)
        from_.append((me ^ back, me ^ 1 ^ backs))
    return me, to, from_


def pack(plan, pieces, own, far, aside, beside, other):
    me, ((far_to, _), (first_to, first_aside), (second_to, second_aside)), _ = route(plan)
    step = own.shape[0]
    for out, at, device in (
        (own, 0, me), (far, 0, far_to), (far, 1, far_to ^ 1), (aside, 0, first_aside), (aside, 1, second_aside),
        (beside, 0, first_to), (beside, 1, second_to), (other, 0, me ^ 1),
    ):
        out[at * step:(at + 1) * step, :] = pieces[device]


def merge(beside, aside, first, second):
    step = beside.shape[0] // 2
    for i, out in enumerate((first, second)):
        out[:step, :] = beside[i * step:(i + 1) * step, :]
        out[step:, :] = aside[i * step:(i + 1) * step, :]


def second_half(x, *rest):
    out = rest[-1]
    out[...] = x[out.shape[0]:, :]


def slot(device):
    return (device >> 1 ^ device >> 2) & 1, (device >> 2) * 2 + (device & 1)


def unpack(pieces, held):
    step = held.shape[1]
    for ref, at, place in pieces:
        held[place] = ref[at * step:(at + 1) * step, :]


def came_first(plan, got):
    me, _, ((far_from, far_others), *_) = route(plan)
    own, other, far, handed = got
    return (own, 0, me), (other, 0, me ^ 1), (far, 0, far_from), (handed, 0, far_others)


def came_last(plan, got):
    _, _, (_, (first_from, _), (second_from, _)) = route(plan)
    first, second = got
    return (first, 0, first_from), (first, 1, first_from ^ 1), (second, 0, second_from), (second, 1, second_from ^ 1)


def outer_stage(came, held, table):
    unpack([(ref, at, slot(device)[1]) for ref, at, device in came], held)
    diagonal = slot(came[0][2])[0]
    half, chunks = 4 * held.shape[1] // 3, held.shape[1] // 3
    whole = [held[:, i * chunks:(i + 1) * chunks, :].reshape(half, LANES) for i in range(3)]
    high, low = split(jnp.concatenate(whole, axis=1))
    both = jnp.concatenate([high, low], axis=0)
    m = table.shape[1] // PARTS
    sums = []
    for q in range(PARTS):
        rows = pl.ds(q * m, m)
        sums.append((dot(table[diagonal, rows, 2 * half:], high), dot(table[diagonal, rows, :2 * half], both)))
    return sums


def early(own, other, far, handed, table, out, held):
    sums = outer_stage(came_first(PLANS[0], (own, other, far, handed)), held, table)
    m = out.shape[0] // PARTS
    for q, (less, more) in enumerate(sums):
        out[q * m:(q + 1) * m, :] = less + more


def fetch(*refs):
    count = (len(refs) - 2) // 2
    copies = [pltpu.make_async_copy(refs[i], refs[count + 1 + i], refs[-1].at[i]) for i in range(count)]
    for copy in copies:
        copy.start()
    for copy in copies:
        copy.wait()


def spread(*refs):
    signals, outs, near, (held, arrived) = refs[:3], refs[3:8], refs[8:11], refs[11:]
    channels, block = signals[0].shape
    chunks = block // LANES
    width = block // LOADS

    def at(load):
        return pl.ds(load * width, width)

    copies = []
    for load in range(LOADS):
        for i in range(3):
            ends = signals[i].at[:, at(load)], near[i].at[:, at(load)]
            copies.append(pltpu.make_async_copy(*ends, arrived.at[load * 3 + i]))
            copies[-1].start()
    for load in range(LOADS):
        for i in range(3):
            copies[load * 3 + i].wait()
            rows = pl.ds(i * chunks + load * chunks // LOADS, chunks // LOADS)
            held[:, rows, :] = near[i][:, at(load)].reshape(channels, chunks // LOADS, LANES)
    pack(PLANS[0], held, *outs)


def transform(*refs):
    got, (begun, first, last, into, twiddle), outs, (held, y) = refs[:2], refs[2:7], refs[7:12], refs[12:]
    n, chunks = y.shape[0], y.shape[1] // 2
    rows = n * chunks
    m = rows // PARTS
    turns = [lanes_of(twiddle, q, m) for q in range(PARTS)]
    sums = outer_stage(came_last(PLANS[0], got), held, first)
    outer = [(begun[2 * m * q:2 * m * (q + 1), :] + less) + more for q, (less, more) in enumerate(sums)]
    spectra = []
    for z, (c, s) in zip(outer, turns):
        turned = []
        for i in range(3):
            re, im = z[:m, i * LANES:(i + 1) * LANES], z[m:, i * LANES:(i + 1) * LANES]
            turned.append(jnp.concatenate([re * c + im * s, im * c - re * s], axis=1))
        spectra.append(dot_right(jnp.concatenate(turned, axis=0), into))
    backs = []
    for z in spectra:
        (xr, xi), (gr, gi), (hr, hi) = (lanes_of(z, i, m) for i in range(3))
        p = [jnp.concatenate([ur * gr + ui * gi, ui * gr - ur * gi], axis=1) for ur, ui in ((hr, hi), (xr, xi))]
        backs.append(dot_right(jnp.concatenate(p, axis=0), into))
    out = 0.0
    for joined in range(JOINED):
        real, imag = [], []
        for q in range(joined * PARTS // JOINED, (joined + 1) * PARTS // JOINED):
            c, s = turns[q]
            pairs = [lanes_of(backs[q], i, m) for i in range(2)]
            real.append(jnp.concatenate([dr * c + di * s for dr, di in pairs], axis=1))
            imag.append(jnp.concatenate([dr * s - di * c for dr, di in pairs], axis=1))
        out += dot_left(last[0, joined], last[1, joined], split(jnp.concatenate(real + imag, axis=0)))
    for d in range(n):
        for i in range(2):
            y[d, i * chunks:(i + 1) * chunks, :] = out[d * chunks:(d + 1) * chunks, i * LANES:(i + 1) * LANES]
    pack(PLANS[1], y, *outs)


def gather(*refs):
    got, (a, b, held) = refs[:6], refs[6:]
    unpack(came_first(PLANS[1], got[:4]) + came_last(PLANS[1], got[4:]), held)
    channels, block = a.shape
    chunks = block // LANES
    for i, ref in enumerate((a, b)):
        for j in range(0, chunks, 8):
            ref[:, pl.ds(j * LANES, 8 * LANES)] = held[:, pl.ds(i * chunks + j, 8), :].reshape(channels, 8 * LANES)


def call(body, ins, outs, scratch=(), far_in=0, near_out=True):
    near = pl.BlockSpec(memory_space=pltpu.VMEM)
    kind = pltpu.VMEM if near_out else jax.ShapeDtypeStruct
    return pl.pallas_call(
        body,
        out_shape=[kind(shape, dtype) for shape, dtype in outs],
        in_specs=[pl.BlockSpec(memory_space=pltpu.HBM)] * far_in + [near] * (len(ins) - far_in),
        out_specs=[near] * len(outs),
        scratch_shapes=scratch,
        compiler_params=pltpu.CompilerParams(vmem_limit_bytes=16 * 2**20),
        name=body.__name__,
    )(*(pltpu.with_memory_space_constraint(x, pltpu.VMEM if i >= far_in else pltpu.HBM) for i, x in enumerate(ins)))


def per_device(inputs, grads, response):
    n = lax.axis_size("context")
    channels, block = inputs.shape
    chunks = block // LANES
    kind = jnp.float32

    def swap(x, even, odd):
        return lax.ppermute(x, "context", [(i, i ^ (odd if i % 2 else even)) for i in range(n)])

    def sizes(arrays):
        return [((u * arrays * chunks, LANES), kind) for u in (1, 2, 2, 2, 1)]

    def exchange(plan, own, far, aside, beside, other, meanwhile=lambda x: []):
        step = own.shape[0]
        aside = swap(aside, 1, 1)
        far = swap(far, *plan[0])
        first, second = call(merge, [beside, aside], [((2 * step, LANES), kind)] * 2)
        made = meanwhile(second)
        first, second = swap(first, *plan[1]), swap(second, *plan[2])
        (handed,) = call(second_half, [far, *made[:1]], [((step, LANES), kind)])
        return [own, swap(other, 1, 1), far, swap(handed, 1, 1), first, second, *made]

    held = [jnp.asarray(t) for t in tables(n * block, PARTS, JOINED)]

    def bring(after):
        return call(fetch, [*held, after], [(t.shape, t.dtype) for t in held], [pltpu.SemaphoreType.DMA((len(held),))], len(held))

    near = [pltpu.VMEM((channels, block), kind)] * 3
    near += [pltpu.VMEM((channels, 3 * chunks, LANES), kind), pltpu.SemaphoreType.DMA((3 * LOADS,))]
    sent = call(spread, [inputs, grads, response], sizes(3), near, 3)
    got = exchange(PLANS[0], *sent, meanwhile=bring)
    near = [pltpu.VMEM((n // 2, 3 * chunks, LANES), kind)]
    (begun,) = call(early, [*got[:4], got[6]], [((2 * n * chunks, 3 * LANES), kind)], near)
    pieces = [pltpu.VMEM((n, 2 * chunks, LANES), kind)]
    got = exchange(PLANS[1], *call(transform, [*got[4:6], begun, *got[6:]], sizes(2), near + pieces))
    return call(gather, got, [((channels, block), kind)] * 2, pieces, near_out=False)


RADIX = 128


HIGHEST = lax.Precision.HIGHEST


def phase_pair(row_index, col_index, period, sign_flip):
    product = row_index[:, None] * col_index[None, :] % period
    angles = 2.0 * math.pi / period * product.astype(jnp.float32)
    return (jnp.cos(angles), sign_flip * jnp.sin(angles))


def complex_apply(pattern, tables, values):
    real_real = jnp.einsum(pattern, tables[0], values[0], precision=HIGHEST)
    imag_imag = jnp.einsum(pattern, tables[1], values[1], precision=HIGHEST)
    real_imag = jnp.einsum(pattern, tables[0], values[1], precision=HIGHEST)
    imag_real = jnp.einsum(pattern, tables[1], values[0], precision=HIGHEST)
    return (real_real - imag_imag, real_imag + imag_real)


def complex_times(left_pair, right_pair):
    return (
        left_pair[0] * right_pair[0] - left_pair[1] * right_pair[1],
        left_pair[0] * right_pair[1] + left_pair[1] * right_pair[0],
    )


def by_columns(inputs, grads, response):
    context_size = lax.axis_size("context")
    device_index = lax.axis_index("context")
    channels, block_len = inputs.shape
    column_len = block_len // context_size
    full_length = block_len * context_size
    padded_len = 2 * full_length
    split_len = block_len // RADIX
    freq_rows = jnp.arange(2 * context_size, dtype=jnp.int32)
    part_rows = jnp.arange(context_size, dtype=jnp.int32)
    outer_fwd = phase_pair(freq_rows, part_rows, 2 * context_size, -1.0)
    outer_inv = phase_pair(part_rows, freq_rows, 2 * context_size, 1.0)
    split_rows = jnp.arange(split_len, dtype=jnp.int32)
    radix_rows = jnp.arange(RADIX, dtype=jnp.int32)
    first_fwd = phase_pair(split_rows, split_rows, split_len, -1.0)
    first_inv = (first_fwd[0], -first_fwd[1])
    inner_fwd = phase_pair(split_rows, radix_rows, block_len, -1.0)
    inner_inv = (inner_fwd[0], -inner_fwd[1])
    last_fwd = phase_pair(radix_rows, radix_rows, RADIX, -1.0)
    last_inv = (last_fwd[0], -last_fwd[1])
    pair_rows = 2 * device_index + jnp.arange(2, dtype=jnp.int32)
    column_rows = jnp.arange(block_len, dtype=jnp.int32)
    global_fwd = phase_pair(pair_rows, column_rows, padded_len, -1.0)
    global_inv = (global_fwd[0], -global_fwd[1])
    signals = jnp.stack([inputs, grads, response])
    columns = lax.all_to_all(
        signals.reshape(3, channels, context_size, column_len),
        "context",
        split_axis=2,
        concat_axis=2,
        tiled=True,
    )
    real_part = jnp.einsum("kn,smnj->smkj", outer_fwd[0], columns, precision=HIGHEST)
    imag_part = jnp.einsum("kn,smnj->smkj", outer_fwd[1], columns, precision=HIGHEST)
    columns = jnp.stack([real_part, imag_part], axis=1)
    arrived = lax.all_to_all(columns, "context", split_axis=3, concat_axis=4, tiled=True)
    values = complex_times((arrived[:, 0], arrived[:, 1]), global_fwd)
    shaped = tuple((v.reshape(v.shape[:3] + (split_len, RADIX)) for v in values))
    sectioned = complex_apply("xa,smrab->smrxb", first_fwd, shaped)
    turned = complex_times(sectioned, inner_fwd)
    spec_real, spec_imag = complex_apply("bd,smrxb->smrxd", last_fwd, turned)
    back_input = (
        spec_real[2] * spec_real[1] + spec_imag[2] * spec_imag[1],
        spec_real[2] * spec_imag[1] - spec_imag[2] * spec_real[1],
    )
    back_filter = (
        spec_real[0] * spec_real[1] + spec_imag[0] * spec_imag[1],
        spec_real[0] * spec_imag[1] - spec_imag[0] * spec_real[1],
    )
    inverse_in = ((back_input[0] - back_filter[1])[None], (back_input[1] + back_filter[0])[None])
    sectioned = complex_apply("bd,smrxd->smrxb", last_inv, inverse_in)
    turned = complex_times(sectioned, inner_inv)
    rebuilt = complex_apply("ax,smrxb->smrab", first_inv, turned)
    flat = tuple((v.reshape(v.shape[:3] + (block_len,)) for v in rebuilt))
    untwisted = complex_times(flat, global_inv)
    rows_back = jnp.stack([untwisted[0], untwisted[1]], axis=1)
    arrived = lax.all_to_all(rows_back, "context", split_axis=4, concat_axis=3, tiled=True)
    cos_real = jnp.einsum("nk,smkj->smnj", outer_inv[0], arrived[:, 0], precision=HIGHEST)
    sin_imag = jnp.einsum("nk,smkj->smnj", outer_inv[1], arrived[:, 1], precision=HIGHEST)
    cos_imag = jnp.einsum("nk,smkj->smnj", outer_inv[0], arrived[:, 1], precision=HIGHEST)
    sin_real = jnp.einsum("nk,smkj->smnj", outer_inv[1], arrived[:, 0], precision=HIGHEST)
    folded = jnp.concatenate([cos_real - sin_imag, cos_imag + sin_real], axis=0) / padded_len
    restored = lax.all_to_all(folded, "context", split_axis=2, concat_axis=3, tiled=True).reshape(
        2, channels, block_len
    )
    return (restored[0], restored[1])


def by_shape(inputs, grads, response):
    if inputs.shape[0] == lax.axis_size("context") == 2 * 2 * 2:
        return per_device(inputs, grads, response)
    return by_columns(inputs, grads, response)


def solution(mesh):
    spec = P("tensor", "context")
    return jax.shard_map(by_shape, mesh=mesh, in_specs=(spec,) * 3, out_specs=(spec,) * 2, check_vma=False)
```

```python
import functools
import math

import jax
import jax.numpy as jnp
import numpy as np
from jax import lax
from jax.experimental import pallas as pl
from jax.experimental.pallas import tpu as pltpu
from jax.sharding import PartitionSpec as P

LANES = 128
BF = jnp.bfloat16
PARTS, JOINED, LOADS = 4, 2, 1
PLANS = ((7, 7), (3, 3), (5, 5)), ((7, 7), (3, 3), (5, 5))


def halves(table):
    table = table.astype(np.float32)
    high = table.astype(BF)
    low = (table - high.astype(np.float32)).astype(BF)
    return high, low


def tables(length, devices, parts, joined):
    rows = length // LANES
    k = np.arange(rows)[:, None] + 0.25
    r = np.arange(rows)[None, :]
    outer = 2 * np.pi * k * r / rows
    stacked = np.stack([np.cos(outer), -np.sin(outer)])
    first = stacked.reshape(2, parts, rows // parts, rows).swapaxes(0, 1).reshape(2 * rows, rows)
    high, low = (t.reshape(2 * rows, devices, rows // devices) for t in halves(first))
    first = []
    for me in range(devices):
        _, _, ((far, far_others), (one, _), (two, _)) = route(PLANS[0], me)
        for came in (me, me ^ 1, far, far_others), (one, one ^ 1, two, two ^ 1):
            first.append(np.concatenate([t[:, device] for t in (high, high, low) for device in came], axis=1))
    first = np.stack(first).reshape(devices, 2, 2 * rows, -1)
    last = (stacked / length).reshape(2, joined, rows // joined, rows).transpose(1, 3, 0, 2)
    last = last.reshape(joined, rows, 2 * rows // joined)
    lane = np.arange(LANES)
    turn = 2 * np.pi * k * lane[None, :] / length
    twiddle = np.concatenate([np.cos(turn), np.sin(turn)], axis=1).astype(np.float32)
    inner = 2 * np.pi * (lane[:, None] * lane[None, :] % LANES) / LANES
    cos2, sin2 = np.cos(inner), np.sin(inner)
    into = np.block([[cos2, -sin2], [sin2, cos2]])
    return first, np.stack(halves(last)), np.stack(halves(into)), twiddle


def split(x):
    high = x.astype(BF)
    low = (x - high.astype(jnp.float32)).astype(BF)
    return high, low


def dot(a, b):
    return jnp.dot(a, b, preferred_element_type=jnp.float32)


def dot_right(x, table):
    high, low = split(x)
    return dot(high, table[0]) + (dot(low, table[0]) + dot(high, table[1]))


def dot_left(table_high, table_low, x):
    high, low = x
    return dot(table_high, high) + (dot(table_high, low) + dot(table_low, high))


def lanes_of(x, i, m):
    return x[i * m:(i + 1) * m, :LANES], x[i * m:(i + 1) * m, LANES:]


def route(plan, me=None):
    me = lax.axis_index("context") if me is None else me
    core = me % 2
    to, from_ = [], []
    for even, odd in plan:
        mine, others = even + core * (odd - even), odd + core * (even - odd)
        to.append((me ^ mine, me ^ 1 ^ others))
        back, backs = (mine, others) if even % 2 == 0 else (others, mine)
        from_.append((me ^ back, me ^ 1 ^ backs))
    return me, to, from_


def pack(plan, pieces, own, far, aside, beside, other):
    me, ((far_to, _), (first_to, first_aside), (second_to, second_aside)), _ = route(plan)
    step = own.shape[0]
    for out, at, device in (
        (own, 0, me), (far, 0, far_to), (far, 1, far_to ^ 1), (aside, 0, first_aside), (aside, 1, second_aside),
        (beside, 0, first_to), (beside, 1, second_to), (other, 0, me ^ 1),
    ):
        out[at * step:(at + 1) * step, :] = pieces[device]


def merge(beside, aside, first, second):
    step = beside.shape[0] // 2
    for i, out in enumerate((first, second)):
        out[:step, :] = beside[i * step:(i + 1) * step, :]
        out[step:, :] = aside[i * step:(i + 1) * step, :]


def second_half(x, *rest):
    out = rest[-1]
    out[...] = x[out.shape[0]:, :]


def unpack(pieces, held):
    step = held.shape[1]
    for ref, at, place in pieces:
        held[place] = ref[at * step:(at + 1) * step, :]


def came_first(plan, got):
    me, _, ((far_from, far_others), *_) = route(plan)
    own, other, far, handed = got
    return (own, 0, me), (other, 0, me ^ 1), (far, 0, far_from), (handed, 0, far_others)


def came_last(plan, got):
    _, _, (_, (first_from, _), (second_from, _)) = route(plan)
    first, second = got
    return (first, 0, first_from), (first, 1, first_from ^ 1), (second, 0, second_from), (second, 1, second_from ^ 1)


def outer_stage(came, step, table):
    half, chunks = 4 * step // 3, step // 3
    whole = []
    for i in range(3):
        whole.append(jnp.concatenate([ref[at * step + i * chunks:at * step + (i + 1) * chunks, :] for ref, at, _ in came]))
    high, low = split(jnp.concatenate(whole, axis=1))
    both = jnp.concatenate([high, low], axis=0)
    m = table.shape[0] // PARTS
    sums = []
    for q in range(PARTS):
        rows = slice(q * m, (q + 1) * m)
        sums.append((dot(table[rows, 2 * half:], high), dot(table[rows, :2 * half], both)))
    return sums


def early(own, other, far, handed, table, out):
    sums = outer_stage(came_first(PLANS[0], (own, other, far, handed)), own.shape[0], table.at[0])
    m = out.shape[0] // PARTS
    for q, (less, more) in enumerate(sums):
        out[q * m:(q + 1) * m, :] = less + more


def fetch(*refs):
    count = (len(refs) - 2) // 2
    sources = [refs[0].at[lax.axis_index("context")], *refs[1:count]]
    copies = [pltpu.make_async_copy(sources[i], refs[count + 1 + i], refs[-1].at[i]) for i in range(count)]
    for copy in copies:
        copy.start()
    for copy in copies:
        copy.wait()


def spread(*refs):
    signals, outs, near, (held, arrived) = refs[:3], refs[3:8], refs[8:11], refs[11:]
    channels, block = signals[0].shape
    chunks = block // LANES
    width = block // LOADS

    def at(load):
        return pl.ds(load * width, width)

    copies = []
    for load in range(LOADS):
        for i in range(3):
            ends = signals[i].at[:, at(load)], near[i].at[:, at(load)]
            copies.append(pltpu.make_async_copy(*ends, arrived.at[load * 3 + i]))
            copies[-1].start()
    for load in range(LOADS):
        for i in range(3):
            copies[load * 3 + i].wait()
            rows = pl.ds(i * chunks + load * chunks // LOADS, chunks // LOADS)
            held[:, rows, :] = near[i][:, at(load)].reshape(channels, chunks // LOADS, LANES)
    pack(PLANS[0], held, *outs)


def transform(*refs):
    got, (begun, first, last, into, twiddle), outs, (y,) = refs[:2], refs[2:7], refs[7:12], refs[12:]
    n, chunks = y.shape[0], y.shape[1] // 2
    rows = n * chunks
    m = rows // PARTS
    turns = [lanes_of(twiddle, q, m) for q in range(PARTS)]
    sums = outer_stage(came_last(PLANS[0], got), got[0].shape[0] // 2, first.at[1])
    outer = [(begun[2 * m * q:2 * m * (q + 1), :] + less) + more for q, (less, more) in enumerate(sums)]
    spectra = []
    for z, (c, s) in zip(outer, turns):
        turned = []
        for i in range(3):
            re, im = z[:m, i * LANES:(i + 1) * LANES], z[m:, i * LANES:(i + 1) * LANES]
            turned.append(jnp.concatenate([re * c + im * s, im * c - re * s], axis=1))
        spectra.append(dot_right(jnp.concatenate(turned, axis=0), into))
    backs = []
    for z in spectra:
        (xr, xi), (gr, gi), (hr, hi) = (lanes_of(z, i, m) for i in range(3))
        p = [jnp.concatenate([ur * gr + ui * gi, ui * gr - ur * gi], axis=1) for ur, ui in ((hr, hi), (xr, xi))]
        backs.append(dot_right(jnp.concatenate(p, axis=0), into))
    out = 0.0
    for joined in range(JOINED):
        real, imag = [], []
        for q in range(joined * PARTS // JOINED, (joined + 1) * PARTS // JOINED):
            c, s = turns[q]
            pairs = [lanes_of(backs[q], i, m) for i in range(2)]
            real.append(jnp.concatenate([dr * c + di * s for dr, di in pairs], axis=1))
            imag.append(jnp.concatenate([dr * s - di * c for dr, di in pairs], axis=1))
        out += dot_left(last[0, joined], last[1, joined], split(jnp.concatenate(real + imag, axis=0)))
    for d in range(n):
        for i in range(2):
            y[d, i * chunks:(i + 1) * chunks, :] = out[d * chunks:(d + 1) * chunks, i * LANES:(i + 1) * LANES]
    pack(PLANS[1], y, *outs)


def gather(*refs):
    got, (a, b, held) = refs[:6], refs[6:]
    unpack(came_first(PLANS[1], got[:4]) + came_last(PLANS[1], got[4:]), held)
    channels, block = a.shape
    chunks = block // LANES
    for i, ref in enumerate((a, b)):
        for j in range(0, chunks, 8):
            ref[:, pl.ds(j * LANES, 8 * LANES)] = held[:, pl.ds(i * chunks + j, 8), :].reshape(channels, 8 * LANES)


def call(body, ins, outs, scratch=(), far_in=0, near_out=True):
    near = pl.BlockSpec(memory_space=pltpu.VMEM)
    kind = pltpu.VMEM if near_out else jax.ShapeDtypeStruct
    return pl.pallas_call(
        body,
        out_shape=[kind(shape, dtype) for shape, dtype in outs],
        in_specs=[pl.BlockSpec(memory_space=pltpu.HBM)] * far_in + [near] * (len(ins) - far_in),
        out_specs=[near] * len(outs),
        scratch_shapes=scratch,
        compiler_params=pltpu.CompilerParams(vmem_limit_bytes=16 * 2**20),
        name=body.__name__,
    )(*(pltpu.with_memory_space_constraint(x, pltpu.VMEM if i >= far_in else pltpu.HBM) for i, x in enumerate(ins)))


def per_device(inputs, grads, response):
    n = lax.axis_size("context")
    channels, block = inputs.shape
    chunks = block // LANES
    kind = jnp.float32

    def swap(x, even, odd):
        return lax.ppermute(x, "context", [(i, i ^ (odd if i % 2 else even)) for i in range(n)])

    def sizes(arrays):
        return [((u * arrays * chunks, LANES), kind) for u in (1, 2, 2, 2, 1)]

    def exchange(plan, own, far, aside, beside, other, meanwhile=lambda x: []):
        step = own.shape[0]
        aside = swap(aside, 1, 1)
        far = swap(far, *plan[0])
        first, second = call(merge, [beside, aside], [((2 * step, LANES), kind)] * 2)
        made = meanwhile(second)
        first, second = swap(first, *plan[1]), swap(second, *plan[2])
        (handed,) = call(second_half, [far, *made[:1]], [((step, LANES), kind)])
        return [own, swap(other, 1, 1), far, swap(handed, 1, 1), first, second, *made]

    held = [jnp.asarray(t) for t in tables(n * block, n, PARTS, JOINED)]

    def bring(after):
        return call(fetch, [*held, after], [(t.shape[1:] if t is held[0] else t.shape, t.dtype) for t in held], [pltpu.SemaphoreType.DMA((len(held),))], len(held))

    near = [pltpu.VMEM((channels, block), kind)] * 3
    near += [pltpu.VMEM((channels, 3 * chunks, LANES), kind), pltpu.SemaphoreType.DMA((3 * LOADS,))]
    sent = call(spread, [inputs, grads, response], sizes(3), near, 3)
    got = exchange(PLANS[0], *sent, meanwhile=bring)
    (begun,) = call(early, [*got[:4], got[6]], [((2 * n * chunks, 3 * LANES), kind)])
    pieces = [pltpu.VMEM((n, 2 * chunks, LANES), kind)]
    got = exchange(PLANS[1], *call(transform, [*got[4:6], begun, *got[6:]], sizes(2), pieces))
    return call(gather, got, [((channels, block), kind)] * 2, pieces, near_out=False)


RADIX = 128


HIGHEST = lax.Precision.HIGHEST


def phase_pair(row_index, col_index, period, sign_flip):
    product = row_index[:, None] * col_index[None, :] % period
    angles = 2.0 * math.pi / period * product.astype(jnp.float32)
    return (jnp.cos(angles), sign_flip * jnp.sin(angles))


def complex_apply(pattern, tables, values):
    real_real = jnp.einsum(pattern, tables[0], values[0], precision=HIGHEST)
    imag_imag = jnp.einsum(pattern, tables[1], values[1], precision=HIGHEST)
    real_imag = jnp.einsum(pattern, tables[0], values[1], precision=HIGHEST)
    imag_real = jnp.einsum(pattern, tables[1], values[0], precision=HIGHEST)
    return (real_real - imag_imag, real_imag + imag_real)


def complex_times(left_pair, right_pair):
    return (
        left_pair[0] * right_pair[0] - left_pair[1] * right_pair[1],
        left_pair[0] * right_pair[1] + left_pair[1] * right_pair[0],
    )


def by_columns(inputs, grads, response):
    context_size = lax.axis_size("context")
    device_index = lax.axis_index("context")
    channels, block_len = inputs.shape
    column_len = block_len // context_size
    full_length = block_len * context_size
    padded_len = 2 * full_length
    split_len = block_len // RADIX
    freq_rows = jnp.arange(2 * context_size, dtype=jnp.int32)
    part_rows = jnp.arange(context_size, dtype=jnp.int32)
    outer_fwd = phase_pair(freq_rows, part_rows, 2 * context_size, -1.0)
    outer_inv = phase_pair(part_rows, freq_rows, 2 * context_size, 1.0)
    split_rows = jnp.arange(split_len, dtype=jnp.int32)
    radix_rows = jnp.arange(RADIX, dtype=jnp.int32)
    first_fwd = phase_pair(split_rows, split_rows, split_len, -1.0)
    first_inv = (first_fwd[0], -first_fwd[1])
    inner_fwd = phase_pair(split_rows, radix_rows, block_len, -1.0)
    inner_inv = (inner_fwd[0], -inner_fwd[1])
    last_fwd = phase_pair(radix_rows, radix_rows, RADIX, -1.0)
    last_inv = (last_fwd[0], -last_fwd[1])
    pair_rows = 2 * device_index + jnp.arange(2, dtype=jnp.int32)
    column_rows = jnp.arange(block_len, dtype=jnp.int32)
    global_fwd = phase_pair(pair_rows, column_rows, padded_len, -1.0)
    global_inv = (global_fwd[0], -global_fwd[1])
    signals = jnp.stack([inputs, grads, response])
    columns = lax.all_to_all(
        signals.reshape(3, channels, context_size, column_len),
        "context",
        split_axis=2,
        concat_axis=2,
        tiled=True,
    )
    real_part = jnp.einsum("kn,smnj->smkj", outer_fwd[0], columns, precision=HIGHEST)
    imag_part = jnp.einsum("kn,smnj->smkj", outer_fwd[1], columns, precision=HIGHEST)
    columns = jnp.stack([real_part, imag_part], axis=1)
    arrived = lax.all_to_all(columns, "context", split_axis=3, concat_axis=4, tiled=True)
    values = complex_times((arrived[:, 0], arrived[:, 1]), global_fwd)
    shaped = tuple((v.reshape(v.shape[:3] + (split_len, RADIX)) for v in values))
    sectioned = complex_apply("xa,smrab->smrxb", first_fwd, shaped)
    turned = complex_times(sectioned, inner_fwd)
    spec_real, spec_imag = complex_apply("bd,smrxb->smrxd", last_fwd, turned)
    back_input = (
        spec_real[2] * spec_real[1] + spec_imag[2] * spec_imag[1],
        spec_real[2] * spec_imag[1] - spec_imag[2] * spec_real[1],
    )
    back_filter = (
        spec_real[0] * spec_real[1] + spec_imag[0] * spec_imag[1],
        spec_real[0] * spec_imag[1] - spec_imag[0] * spec_real[1],
    )
    inverse_in = ((back_input[0] - back_filter[1])[None], (back_input[1] + back_filter[0])[None])
    sectioned = complex_apply("bd,smrxd->smrxb", last_inv, inverse_in)
    turned = complex_times(sectioned, inner_inv)
    rebuilt = complex_apply("ax,smrxb->smrab", first_inv, turned)
    flat = tuple((v.reshape(v.shape[:3] + (block_len,)) for v in rebuilt))
    untwisted = complex_times(flat, global_inv)
    rows_back = jnp.stack([untwisted[0], untwisted[1]], axis=1)
    arrived = lax.all_to_all(rows_back, "context", split_axis=4, concat_axis=3, tiled=True)
    cos_real = jnp.einsum("nk,smkj->smnj", outer_inv[0], arrived[:, 0], precision=HIGHEST)
    sin_imag = jnp.einsum("nk,smkj->smnj", outer_inv[1], arrived[:, 1], precision=HIGHEST)
    cos_imag = jnp.einsum("nk,smkj->smnj", outer_inv[0], arrived[:, 1], precision=HIGHEST)
    sin_real = jnp.einsum("nk,smkj->smnj", outer_inv[1], arrived[:, 0], precision=HIGHEST)
    folded = jnp.concatenate([cos_real - sin_imag, cos_imag + sin_real], axis=0) / padded_len
    restored = lax.all_to_all(folded, "context", split_axis=2, concat_axis=3, tiled=True).reshape(
        2, channels, block_len
    )
    return (restored[0], restored[1])


def by_shape(inputs, grads, response):
    if inputs.shape[0] == lax.axis_size("context") == 2 * 2 * 2:
        return per_device(inputs, grads, response)
    return by_columns(inputs, grads, response)


def solution(mesh):
    spec = P("tensor", "context")
    return jax.shard_map(by_shape, mesh=mesh, in_specs=(spec,) * 3, out_specs=(spec,) * 2, check_vma=False)
```

```python
import functools
import math

import jax
import jax.numpy as jnp
import numpy as np
from jax import lax
from jax.experimental import pallas as pl
from jax.experimental.pallas import tpu as pltpu
from jax.sharding import PartitionSpec as P

LANES = 128
BF = jnp.bfloat16
PARTS, JOINED, LOADS = 4, 2, 1
PLANS = ((7, 7), (3, 3), (5, 5)), ((7, 7), (3, 3), (5, 5))


def halves(table):
    table = table.astype(np.float32)
    high = table.astype(BF)
    low = (table - high.astype(np.float32)).astype(BF)
    return high, low


def tables(length, devices, parts, joined):
    rows = length // LANES
    k = np.arange(rows)[:, None] + 0.25
    r = np.arange(rows)[None, :]
    outer = 2 * np.pi * k * r / rows
    stacked = np.stack([np.cos(outer), -np.sin(outer)])
    first = stacked.reshape(2, parts, rows // parts, rows).swapaxes(0, 1).reshape(2 * rows, rows)
    high, low = (t.reshape(2 * rows, devices, rows // devices) for t in halves(first))
    first = []
    for me in range(devices):
        _, _, ((far, far_others), (one, _), (two, _)) = route(PLANS[0], me)
        for came in (me, me ^ 1, far, far_others), (one, one ^ 1, two, two ^ 1):
            first.append(np.concatenate([t[:, device] for t in (high, high, low) for device in came], axis=1))
    first = np.stack(first).reshape(devices, 2, 2 * rows, -1)
    last = (stacked / length).reshape(2, joined, rows // joined, rows).transpose(1, 3, 0, 2)
    last = last.reshape(joined, rows, 2 * rows // joined)
    lane = np.arange(LANES)
    turn = 2 * np.pi * k * lane[None, :] / length
    twiddle = np.concatenate([np.cos(turn), np.sin(turn)], axis=1).astype(np.float32)
    inner = 2 * np.pi * (lane[:, None] * lane[None, :] % LANES) / LANES
    cos2, sin2 = np.cos(inner), np.sin(inner)
    into = np.block([[cos2, -sin2], [sin2, cos2]])
    return first, np.stack(halves(last)), np.stack(halves(into)), twiddle


def split(x):
    high = x.astype(BF)
    low = (x - high.astype(jnp.float32)).astype(BF)
    return high, low


def dot(a, b):
    return jnp.dot(a, b, preferred_element_type=jnp.float32)


def dot_right(x, table):
    high, low = split(x)
    return dot(high, table[0]) + (dot(low, table[0]) + dot(high, table[1]))


def dot_left(table_high, table_low, x):
    high, low = x
    return dot(table_high, high) + (dot(table_high, low) + dot(table_low, high))


def lanes_of(x, i, m):
    return x[i * m:(i + 1) * m, :LANES], x[i * m:(i + 1) * m, LANES:]


def route(plan, me=None):
    me = lax.axis_index("context") if me is None else me
    core = me % 2
    to, from_ = [], []
    for even, odd in plan:
        mine, others = even + core * (odd - even), odd + core * (even - odd)
        to.append((me ^ mine, me ^ 1 ^ others))
        back, backs = (mine, others) if even % 2 == 0 else (others, mine)
        from_.append((me ^ back, me ^ 1 ^ backs))
    return me, to, from_


def pack(plan, pieces, own, far, aside, beside, other):
    me, ((far_to, _), (first_to, first_aside), (second_to, second_aside)), _ = route(plan)
    step = own.shape[0]
    for out, at, device in (
        (own, 0, me), (far, 0, far_to), (far, 1, far_to ^ 1), (aside, 0, first_aside), (aside, 1, second_aside),
        (beside, 0, first_to), (beside, 1, second_to), (other, 0, me ^ 1),
    ):
        out[at * step:(at + 1) * step, :] = pieces[device]


def merge(beside, aside, first, second):
    step = beside.shape[0] // 2
    for i, out in enumerate((first, second)):
        out[:step, :] = beside[i * step:(i + 1) * step, :]
        out[step:, :] = aside[i * step:(i + 1) * step, :]


def second_half(x, *rest):
    out = rest[-1]
    out[...] = x[out.shape[0]:, :]


def unpack(pieces, held):
    step = held.shape[1]
    for ref, at, place in pieces:
        held[place] = ref[at * step:(at + 1) * step, :]


def came_first(plan, got):
    me, _, ((far_from, far_others), *_) = route(plan)
    own, other, far, handed = got
    return (own, 0, me), (other, 0, me ^ 1), (far, 0, far_from), (handed, 0, far_others)


def came_last(plan, got):
    _, _, (_, (first_from, _), (second_from, _)) = route(plan)
    first, second = got
    return (first, 0, first_from), (first, 1, first_from ^ 1), (second, 0, second_from), (second, 1, second_from ^ 1)


def outer_stage(came, step, table):
    half, chunks = 4 * step // 3, step // 3
    whole = []
    for i in range(3):
        whole.append(jnp.concatenate([ref[at * step + i * chunks:at * step + (i + 1) * chunks, :] for ref, at, _ in came]))
    high, low = split(jnp.concatenate(whole, axis=1))
    both = jnp.concatenate([high, low], axis=0)
    m = table.shape[0] // PARTS
    sums = []
    for q in range(PARTS):
        rows = slice(q * m, (q + 1) * m)
        sums.append((dot(table[rows, 2 * half:], high), dot(table[rows, :2 * half], both)))
    return sums


def early(own, other, far, handed, table, out):
    sums = outer_stage(came_first(PLANS[0], (own, other, far, handed)), own.shape[0], table.at[0])
    m = out.shape[0] // PARTS
    for q, (less, more) in enumerate(sums):
        out[q * m:(q + 1) * m, :] = less + more


def fetch(*refs):
    count = (len(refs) - 2) // 2
    sources = [refs[0].at[lax.axis_index("context")], *refs[1:count]]
    copies = [pltpu.make_async_copy(sources[i], refs[count + 1 + i], refs[-1].at[i]) for i in range(count)]
    for copy in copies:
        copy.start()
    for copy in copies:
        copy.wait()


def spread(*refs):
    signals, outs, near, (held, arrived) = refs[:3], refs[3:8], refs[8:11], refs[11:]
    channels, block = signals[0].shape
    chunks = block // LANES
    width = block // LOADS

    def at(load):
        return pl.ds(load * width, width)

    copies = []
    for load in range(LOADS):
        for i in range(3):
            ends = signals[i].at[:, at(load)], near[i].at[:, at(load)]
            copies.append(pltpu.make_async_copy(*ends, arrived.at[load * 3 + i]))
            copies[-1].start()
    for load in range(LOADS):
        for i in range(3):
            copies[load * 3 + i].wait()
            rows = pl.ds(i * chunks + load * chunks // LOADS, chunks // LOADS)
            held[:, rows, :] = near[i][:, at(load)].reshape(channels, chunks // LOADS, LANES)
    pack(PLANS[0], held, *outs)


def transform(*refs):
    got, (begun, first, last, into, twiddle), outs, (y,) = refs[:2], refs[2:7], refs[7:12], refs[12:]
    n, chunks = y.shape[0], y.shape[1] // 2
    rows = n * chunks
    m = rows // PARTS
    turns = [lanes_of(twiddle, q, m) for q in range(PARTS)]
    sums = outer_stage(came_last(PLANS[0], got), got[0].shape[0] // 2, first.at[1])
    outer = [(begun[2 * m * q:2 * m * (q + 1), :] + less) + more for q, (less, more) in enumerate(sums)]
    spectra = []
    for z, (c, s) in zip(outer, turns):
        turned = []
        for i in range(3):
            re, im = z[:m, i * LANES:(i + 1) * LANES], z[m:, i * LANES:(i + 1) * LANES]
            turned.append(jnp.concatenate([re * c + im * s, im * c - re * s], axis=1))
        spectra.append(dot_right(jnp.concatenate(turned, axis=0), into))
    backs = []
    for z in spectra:
        (xr, xi), (gr, gi), (hr, hi) = (lanes_of(z, i, m) for i in range(3))
        p = [jnp.concatenate([ur * gr + ui * gi, ui * gr - ur * gi], axis=1) for ur, ui in ((hr, hi), (xr, xi))]
        backs.append(dot_right(jnp.concatenate(p, axis=0), into))
    out = 0.0
    for joined in range(JOINED):
        real, imag = [], []
        for q in range(joined * PARTS // JOINED, (joined + 1) * PARTS // JOINED):
            c, s = turns[q]
            pairs = [lanes_of(backs[q], i, m) for i in range(2)]
            real.append(jnp.concatenate([dr * c + di * s for dr, di in pairs], axis=1))
            imag.append(jnp.concatenate([dr * s - di * c for dr, di in pairs], axis=1))
        out += dot_left(last[0, joined], last[1, joined], split(jnp.concatenate(real + imag, axis=0)))
    for d in range(n):
        for i in range(2):
            y[d, i * chunks:(i + 1) * chunks, :] = out[d * chunks:(d + 1) * chunks, i * LANES:(i + 1) * LANES]
    pack(PLANS[1], y, *outs)


def gather(*refs):
    got, (a, b, held) = refs[:6], refs[6:]
    unpack(came_first(PLANS[1], got[:4]) + came_last(PLANS[1], got[4:]), held)
    channels, block = a.shape
    chunks = block // LANES
    for i, ref in enumerate((a, b)):
        for j in range(0, chunks, 16):
            ref[:, pl.ds(j * LANES, 16 * LANES)] = held[:, pl.ds(i * chunks + j, 16), :].reshape(channels, 16 * LANES)


def call(body, ins, outs, scratch=(), far_in=0, near_out=True):
    near = pl.BlockSpec(memory_space=pltpu.VMEM)
    kind = pltpu.VMEM if near_out else jax.ShapeDtypeStruct
    return pl.pallas_call(
        body,
        out_shape=[kind(shape, dtype) for shape, dtype in outs],
        in_specs=[pl.BlockSpec(memory_space=pltpu.HBM)] * far_in + [near] * (len(ins) - far_in),
        out_specs=[near] * len(outs),
        scratch_shapes=scratch,
        compiler_params=pltpu.CompilerParams(vmem_limit_bytes=16 * 2**20),
        name=body.__name__,
    )(*(pltpu.with_memory_space_constraint(x, pltpu.VMEM if i >= far_in else pltpu.HBM) for i, x in enumerate(ins)))


def per_device(inputs, grads, response):
    n = lax.axis_size("context")
    channels, block = inputs.shape
    chunks = block // LANES
    kind = jnp.float32

    def swap(x, even, odd):
        return lax.ppermute(x, "context", [(i, i ^ (odd if i % 2 else even)) for i in range(n)])

    def sizes(arrays):
        return [((u * arrays * chunks, LANES), kind) for u in (1, 2, 2, 2, 1)]

    def exchange(plan, own, far, aside, beside, other, meanwhile=lambda x: []):
        step = own.shape[0]
        aside = swap(aside, 1, 1)
        far = swap(far, *plan[0])
        first, second = call(merge, [beside, aside], [((2 * step, LANES), kind)] * 2)
        made = meanwhile(second)
        first, second = swap(first, *plan[1]), swap(second, *plan[2])
        (handed,) = call(second_half, [far, *made[:1]], [((step, LANES), kind)])
        return [own, swap(other, 1, 1), far, swap(handed, 1, 1), first, second, *made]

    held = [jnp.asarray(t) for t in tables(n * block, n, PARTS, JOINED)]

    def bring(after):
        return call(fetch, [*held, after], [(t.shape[1:] if t is held[0] else t.shape, t.dtype) for t in held], [pltpu.SemaphoreType.DMA((len(held),))], len(held))

    near = [pltpu.VMEM((channels, block), kind)] * 3
    near += [pltpu.VMEM((channels, 3 * chunks, LANES), kind), pltpu.SemaphoreType.DMA((3 * LOADS,))]
    sent = call(spread, [inputs, grads, response], sizes(3), near, 3)
    got = exchange(PLANS[0], *sent, meanwhile=bring)
    (begun,) = call(early, [*got[:4], got[6]], [((2 * n * chunks, 3 * LANES), kind)])
    pieces = [pltpu.VMEM((n, 2 * chunks, LANES), kind)]
    got = exchange(PLANS[1], *call(transform, [*got[4:6], begun, *got[6:]], sizes(2), pieces))
    return call(gather, got, [((channels, block), kind)] * 2, pieces, near_out=False)


RADIX = 128


HIGHEST = lax.Precision.HIGHEST


def phase_pair(row_index, col_index, period, sign_flip):
    product = row_index[:, None] * col_index[None, :] % period
    angles = 2.0 * math.pi / period * product.astype(jnp.float32)
    return (jnp.cos(angles), sign_flip * jnp.sin(angles))


def complex_apply(pattern, tables, values):
    real_real = jnp.einsum(pattern, tables[0], values[0], precision=HIGHEST)
    imag_imag = jnp.einsum(pattern, tables[1], values[1], precision=HIGHEST)
    real_imag = jnp.einsum(pattern, tables[0], values[1], precision=HIGHEST)
    imag_real = jnp.einsum(pattern, tables[1], values[0], precision=HIGHEST)
    return (real_real - imag_imag, real_imag + imag_real)


def complex_times(left_pair, right_pair):
    return (
        left_pair[0] * right_pair[0] - left_pair[1] * right_pair[1],
        left_pair[0] * right_pair[1] + left_pair[1] * right_pair[0],
    )


def by_columns(inputs, grads, response):
    context_size = lax.axis_size("context")
    device_index = lax.axis_index("context")
    channels, block_len = inputs.shape
    column_len = block_len // context_size
    full_length = block_len * context_size
    padded_len = 2 * full_length
    split_len = block_len // RADIX
    freq_rows = jnp.arange(2 * context_size, dtype=jnp.int32)
    part_rows = jnp.arange(context_size, dtype=jnp.int32)
    outer_fwd = phase_pair(freq_rows, part_rows, 2 * context_size, -1.0)
    outer_inv = phase_pair(part_rows, freq_rows, 2 * context_size, 1.0)
    split_rows = jnp.arange(split_len, dtype=jnp.int32)
    radix_rows = jnp.arange(RADIX, dtype=jnp.int32)
    first_fwd = phase_pair(split_rows, split_rows, split_len, -1.0)
    first_inv = (first_fwd[0], -first_fwd[1])
    inner_fwd = phase_pair(split_rows, radix_rows, block_len, -1.0)
    inner_inv = (inner_fwd[0], -inner_fwd[1])
    last_fwd = phase_pair(radix_rows, radix_rows, RADIX, -1.0)
    last_inv = (last_fwd[0], -last_fwd[1])
    pair_rows = 2 * device_index + jnp.arange(2, dtype=jnp.int32)
    column_rows = jnp.arange(block_len, dtype=jnp.int32)
    global_fwd = phase_pair(pair_rows, column_rows, padded_len, -1.0)
    global_inv = (global_fwd[0], -global_fwd[1])
    signals = jnp.stack([inputs, grads, response])
    columns = lax.all_to_all(
        signals.reshape(3, channels, context_size, column_len),
        "context",
        split_axis=2,
        concat_axis=2,
        tiled=True,
    )
    real_part = jnp.einsum("kn,smnj->smkj", outer_fwd[0], columns, precision=HIGHEST)
    imag_part = jnp.einsum("kn,smnj->smkj", outer_fwd[1], columns, precision=HIGHEST)
    columns = jnp.stack([real_part, imag_part], axis=1)
    arrived = lax.all_to_all(columns, "context", split_axis=3, concat_axis=4, tiled=True)
    values = complex_times((arrived[:, 0], arrived[:, 1]), global_fwd)
    shaped = tuple((v.reshape(v.shape[:3] + (split_len, RADIX)) for v in values))
    sectioned = complex_apply("xa,smrab->smrxb", first_fwd, shaped)
    turned = complex_times(sectioned, inner_fwd)
    spec_real, spec_imag = complex_apply("bd,smrxb->smrxd", last_fwd, turned)
    back_input = (
        spec_real[2] * spec_real[1] + spec_imag[2] * spec_imag[1],
        spec_real[2] * spec_imag[1] - spec_imag[2] * spec_real[1],
    )
    back_filter = (
        spec_real[0] * spec_real[1] + spec_imag[0] * spec_imag[1],
        spec_real[0] * spec_imag[1] - spec_imag[0] * spec_real[1],
    )
    inverse_in = ((back_input[0] - back_filter[1])[None], (back_input[1] + back_filter[0])[None])
    sectioned = complex_apply("bd,smrxd->smrxb", last_inv, inverse_in)
    turned = complex_times(sectioned, inner_inv)
    rebuilt = complex_apply("ax,smrxb->smrab", first_inv, turned)
    flat = tuple((v.reshape(v.shape[:3] + (block_len,)) for v in rebuilt))
    untwisted = complex_times(flat, global_inv)
    rows_back = jnp.stack([untwisted[0], untwisted[1]], axis=1)
    arrived = lax.all_to_all(rows_back, "context", split_axis=4, concat_axis=3, tiled=True)
    cos_real = jnp.einsum("nk,smkj->smnj", outer_inv[0], arrived[:, 0], precision=HIGHEST)
    sin_imag = jnp.einsum("nk,smkj->smnj", outer_inv[1], arrived[:, 1], precision=HIGHEST)
    cos_imag = jnp.einsum("nk,smkj->smnj", outer_inv[0], arrived[:, 1], precision=HIGHEST)
    sin_real = jnp.einsum("nk,smkj->smnj", outer_inv[1], arrived[:, 0], precision=HIGHEST)
    folded = jnp.concatenate([cos_real - sin_imag, cos_imag + sin_real], axis=0) / padded_len
    restored = lax.all_to_all(folded, "context", split_axis=2, concat_axis=3, tiled=True).reshape(
        2, channels, block_len
    )
    return (restored[0], restored[1])


def by_shape(inputs, grads, response):
    if inputs.shape[0] == lax.axis_size("context") == 2 * 2 * 2:
        return per_device(inputs, grads, response)
    return by_columns(inputs, grads, response)


def solution(mesh):
    spec = P("tensor", "context")
    return jax.shard_map(by_shape, mesh=mesh, in_specs=(spec,) * 3, out_specs=(spec,) * 2, check_vma=False)
```
